512 devices in a mesh: dp: 8 (over z_lo, x), space: 64 (over z_hi, y, core).
Axes of the slice: x: 4, y: 8, z: 8 (z_hi: 4, z_lo: 2; z = z_hi * 2 + z_lo), core: 2. Of those that a mesh axis runs over, the one named last changes fastest.
Arguments:
- volume_in: float32 [8, 64, 4, 64, 216], P('dp', 'space'), may hold values from -6 to 6
- filter_one: float32 [27, 16, 4], replicated, may hold values from -0.625 to 0.625
- filter_two: float32 [27, 32, 16], replicated, may hold values from -0.3125 to 0.3125
- out_grad: float32 [8, 64, 32, 216], P('dp', 'space'), may hold values from -6 to 6
Outputs:
- level_two: float32 [8, 64, 32, 216], P('dp', 'space')
- hidden_grad: float32 [8, 64, 16, 8, 216], P('dp', 'space')
- grad_one: float32 [27, 16, 4], replicated
- grad_two: float32 [27, 32, 16], replicated
The draws below stay inside these ranges and needn't reach their ends.
All inputs are finite; a program needn't handle non-finite values.
Results may differ from the reference program's by a relative error of at most 0.0014.
Values sent between devices are 32-bit elements; how exact they have to be, the bound alone decides.
A program may use at most 64 MiB of HBM per device.

```python
import jax
import jax.numpy as jnp
from jax import lax

CIN = 4
C1 = 16
C2 = 32
EDGE = 24
BRICKS = 64
VOLS = 8
N_SPACE = 64


def steps_of(own_key, extent, cuts, least, largest):
    loudness = 1.0
    for axis_at, shards_of in cuts:
        steps = jax.random.uniform(jax.random.fold_in(jax.random.fold_in(own_key, 6), axis_at), (shards_of,), jnp.float32, least / len(cuts), largest / len(cuts))
        loudness = loudness * jnp.repeat(jnp.exp(steps), extent[axis_at] // shards_of).reshape((-1,) + (1,) * (len(extent) - 1 - axis_at))
    return loudness


def bell_draw(rng, extent, deviation, reach, pieces=(), held_as=jnp.bfloat16):
    array = deviation * jax.random.normal(rng, extent, jnp.float32)
    if pieces:
        array = array * steps_of(rng, extent, pieces, -0.22, 0.18)
    return jnp.clip(array, -reach, reach).astype(held_as)


def setup_inputs(seed: int = 0) -> dict:
    splits = jax.random.split(jax.random.key(seed), 5)
    volume_in = bell_draw(splits[0], (VOLS, BRICKS, CIN, 64, (EDGE // 4) ** 3), 1.0, 6.0, ((0, 8), (1, 64)), jnp.float32)
    filter_one = bell_draw(splits[1], (27, C1, CIN), (27 * CIN) ** -0.5, 0.625, (), jnp.float32)
    filter_two = bell_draw(splits[2], (27, C2, C1), (27 * C1) ** -0.5, 0.3125, (), jnp.float32)
    out_grad = bell_draw(splits[3], (VOLS, BRICKS, C2, (EDGE // 4) ** 3), 1.0, 6.0, ((0, 8), (1, 64)), jnp.float32)
    return {"volume_in": volume_in, "filter_one": filter_one, "filter_two": filter_two, "out_grad": out_grad}


SLOPE = 0.3

def lrelu(v):
    return jnp.where(v > 0, v, SLOPE * v)

def dslope(v):
    return jnp.where(v > 0, 1.0, SLOPE).astype(v.dtype)

def conv_down(padded, weight):
    sizes = [(padded.shape[d] - 1) // 2 for d in (2, 3, 4)]
    total = None
    for k in range(27):
        kx, ky, kz = (k // 9, k // 3 % 3, k % 3)
        piece = padded[:, :, kx:kx + 2 * sizes[0]:2, ky:ky + 2 * sizes[1]:2, kz:kz + 2 * sizes[2]:2]
        term = jnp.einsum('oi,vixyz->voxyz', weight[k], piece, precision=lax.Precision.HIGHEST)
        total = term if total is None else total + term
    return total

def filter_grad(delta, padded):
    sizes = delta.shape[2:]
    grads = []
    for k in range(27):
        kx, ky, kz = (k // 9, k // 3 % 3, k % 3)
        piece = padded[:, :, kx:kx + 2 * sizes[0]:2, ky:ky + 2 * sizes[1]:2, kz:kz + 2 * sizes[2]:2]
        grads.append(jnp.einsum('voxyz,vixyz->oi', delta, piece, precision=lax.Precision.HIGHEST))
    return jnp.stack(grads)

def conv_back(extended, weight):
    total = None
    for k in range(27):
        kx, ky, kz = (k // 9, k // 3 % 3, k % 3)
        term = jnp.einsum('oi,voxyz->vixyz', weight[k], extended, precision=lax.Precision.HIGHEST)
        spread = lax.pad(term, jnp.float32(0.0), [(0, 0, 0), (0, 0, 0), (kx, 2 - kx, 1), (ky, 2 - ky, 1), (kz, 2 - kz, 1)])
        total = spread if total is None else total + spread
    nx, ny, nz = [2 * (extended.shape[d] - 1) for d in (2, 3, 4)]
    return total[:, :, 1:nx + 1, 1:ny + 1, 1:nz + 1]

def to_volume(bricks, edge):
    grid_z = N_SPACE // 16
    chans = bricks.shape[1]
    cube = bricks.reshape(4, 4, grid_z, chans, edge, edge, edge)
    cube = jnp.transpose(cube, (3, 0, 4, 1, 5, 2, 6))
    return cube.reshape(chans, 4 * edge, 4 * edge, grid_z * edge)

def from_volume(field, edge):
    grid_z = N_SPACE // 16
    chans = field.shape[0]
    cube = field.reshape(chans, 4, edge, 4, edge, grid_z, edge)
    cube = jnp.transpose(cube, (1, 3, 5, 0, 2, 4, 6))
    return cube.reshape(4 * 4 * grid_z, chans, edge * edge * edge)

def unpack_input(bricks):
    side = EDGE // 4
    count, chans = (bricks.shape[0], bricks.shape[1])
    cube = bricks.reshape(count, chans, 2, 2, 2, 2, 2, 2, side, side, side)
    cube = jnp.transpose(cube, (0, 1, 8, 5, 2, 9, 6, 3, 10, 7, 4))
    return cube.reshape(count, chans, EDGE * EDGE * EDGE)

def pack_hidden(bricks):
    side = EDGE // 4
    count, chans = (bricks.shape[0], bricks.shape[1])
    cube = bricks.reshape(count, chans, side, 2, side, 2, side, 2)
    cube = jnp.transpose(cube, (0, 1, 3, 5, 7, 2, 4, 6))
    return cube.reshape(count, chans, 8, side * side * side)

def reference(volume_in, filter_one, filter_two, out_grad):

    def run(items):
        bricks_in, bricks_grad = items
        low = ((0, 0), (0, 0), (1, 0), (1, 0), (1, 0))
        high = ((0, 0), (0, 0), (0, 1), (0, 1), (0, 1))
        padded_in = jnp.pad(to_volume(unpack_input(bricks_in), EDGE)[None], low)
        pre_one = conv_down(padded_in, filter_one)
        hidden = lrelu(pre_one)
        padded_hidden = jnp.pad(hidden, low)
        pre_two = conv_down(padded_hidden, filter_two)
        act_two = lrelu(pre_two)
        delta_two = to_volume(bricks_grad, EDGE // 4)[None] * dslope(pre_two)
        grad_two = filter_grad(delta_two, padded_hidden)
        back = conv_back(jnp.pad(delta_two, high), filter_two)
        delta_one = back * dslope(pre_one)
        grad_one = filter_grad(delta_one, padded_in)
        return (from_volume(act_two[0], EDGE // 4), pack_hidden(from_volume(back[0], EDGE // 2)), grad_one, grad_two)
    act, back, grad_one, grad_two = lax.map(run, (volume_in, out_grad))
    return (act, back, lax.optimization_barrier(jnp.sum(grad_one, axis=0)), lax.optimization_barrier(jnp.sum(grad_two, axis=0)))
```

```python
import itertools

import jax
import jax.numpy as jnp
import numpy as np
from jax import lax
from jax.experimental import pallas as pl
from jax.experimental.pallas import tpu as pltpu
from jax.sharding import PartitionSpec as P

SLOPE = 0.3
SIDE = 6
CELLS = SIDE**3
BF16 = jnp.bfloat16
F32 = jnp.float32
MESH = pl.DeviceIdType.MESH
HIGHEST = lax.Precision.HIGHEST

SUBSETS = [(0,), (1,), (2,), (0, 1), (0, 2), (1, 2), (0, 1, 2)]
SIZES = [SIDE ** (3 - len(s)) for s in SUBSETS]
STARTS = [sum(SIZES[:i]) for i in range(7)]


def rows_for(tiles):
    rows = [8 * -(-tiles // (128 // size)) for size in SIZES]
    return rows, [sum(rows[:i]) for i in range(7)]


IN_ROWS, IN_AT = rows_for(32)
D_ROWS, D_AT = rows_for(4)


def lane_of(coords, outside):
    dims = tuple(d for d in range(3) if coords[d] == outside)
    rest = [coords[d] for d in range(3) if d not in dims]
    place = 0
    for c in rest:
        place = place * SIDE + c
    return place if not dims else 256 + STARTS[SUBSETS.index(dims)] + place


def shift_matrices(step):
    outside = -1 if step < 0 else SIDE
    span = range(-1, SIDE) if step < 0 else range(SIDE + 1)
    m = np.zeros((3, 384, 384), np.float32)
    for coords in itertools.product(span, repeat=3):
        for d in range(3):
            source = list(coords)
            source[d] += step
            if coords[d] != outside:
                m[d, lane_of(source, outside), lane_of(coords, outside)] = 1
    return m


def pick_matrix(edge):
    m = np.zeros((256, 128), np.float32)
    for dims, start in zip(SUBSETS, STARTS):
        rest = [d for d in range(3) if d not in dims]
        for place, digits in enumerate(itertools.product(range(SIDE), repeat=len(rest))):
            coords = [edge] * 3
            for d, digit in zip(rest, digits):
                coords[d] = digit
            m[lane_of(coords, None), start + place] = 1
    return m


def spread_matrix():
    m = np.zeros((27, 432), np.float32)
    for k in range(27):
        m[k, 16 * k : 16 * k + 12] = 1
    return m


def iota(shape, dim):
    return lax.broadcasted_iota(jnp.int32, shape, dim)


def split(x, pieces):
    out = []
    for _ in range(pieces):
        piece = x.astype(BF16)
        out.append(piece)
        x = x - piece.astype(F32)
    return out


def dot(a, b, precision=None):
    return jnp.dot(a, b, preferred_element_type=F32, precision=precision)


def dot_t(a, b, precision=None):
    return lax.dot_general(a, b, (((1,), (1,)), ((), ())), preferred_element_type=F32, precision=precision)


def pack(tiles, buf, starts):
    lane = iota((8, 128), 1)
    for s in range(7):
        size = SIZES[s]
        per = 128 // size
        for block in range(-(-len(tiles) // per)):
            total = jnp.zeros((8, 128), F32)
            for i, tile in enumerate(tiles[block * per : (block + 1) * per]):
                moved = pltpu.roll(tile, (i * size - STARTS[s]) % 128, 1)
                total = jnp.where((lane >= i * size) & (lane < (i + 1) * size), moved, total)
            buf[starts[s] + 8 * block : starts[s] + 8 * block + 8, :] = total


def unpack(t, buf, starts, valid):
    lane = iota((8, 128), 1)
    total = jnp.zeros((8, 128), F32)
    for s in range(7):
        size = SIZES[s]
        per = 128 // size
        row = starts[s] + 8 * (t // per)
        moved = pltpu.roll(buf[row : row + 8, :], (STARTS[s] - (t % per) * size) % 128, 1)
        here = (lane >= STARTS[s]) & (lane < STARTS[s] + size) & (valid[s] > 0)
        total = jnp.where(here, moved, total)
    return total


def cell(i, j, l):
    return 16 * (25 * i + 5 * j + l)


def offsets(k):
    return (k // 9, k // 3 % 3, k % 3)


def bits(q):
    return (q >> 2 & 1, q >> 1 & 1, q & 1)


def level_kernel(
    x_ref, w1_ref, w2_ref, g_ref, low_ref, high_ref, pick_ref, pickl_ref, spread_ref,
    lev_ref, hid_ref, part_ref,
    xs, xc, hk, pre, back, send, recv, dsend, drecv, send_sem, recv_sem, dsend_sem, drecv_sem,
):
    where = lax.axis_index("space")
    coords = (where // 16, where // 4 % 4, where % 4)

    def neighbour(dims, step):
        moved = [(coords[d] + (step if d in dims else 0) + 4) % 4 for d in range(3)]
        return {"space": moved[0] * 16 + moved[1] * 4 + moved[2]}

    def flags(edge):
        inside = [jnp.where(coords[d] == edge, 0, 1) for d in range(3)]
        out = []
        for dims in SUBSETS:
            flag = 1
            for d in dims:
                flag = flag * inside[d]
            out.append(flag)
        return out

    barrier = pltpu.get_barrier_semaphore()
    for dims in SUBSETS:
        for step in (-1, 1):
            pl.semaphore_signal(barrier, inc=1, device_id=neighbour(dims, step), device_id_type=MESH)

    x = jnp.concatenate([x_ref[...], jnp.zeros((256, 40), F32)], axis=1)
    pieces = split(x, 3)
    picked = dot(pieces[0], pick_ref[...]) + dot(pieces[1], pick_ref[...])
    picked = picked + dot(pieces[2], pick_ref[...])
    pack([picked[8 * t : 8 * t + 8] for t in range(32)], send, IN_AT)
    pl.semaphore_wait(barrier, 14)
    copies = []
    for s, dims in enumerate(SUBSETS):
        rows = pl.ds(IN_AT[s], IN_ROWS[s])
        copies.append(
            pltpu.make_async_remote_copy(
                src_ref=send.at[rows],
                dst_ref=recv.at[rows],
                send_sem=send_sem.at[s],
                recv_sem=recv_sem.at[s],
                device_id=neighbour(dims, 1),
                device_id_type=MESH,
            )
        )
        copies[-1].start()

    w1 = dot(w1_ref[...], spread_ref[...], HIGHEST)
    w1 = jnp.where(iota((64, 432), 0) % 4 == iota((64, 432), 1) % 4, w1, 0.0)
    w1 = dot((iota((16, 64), 1) // 4 == iota((16, 64), 0)).astype(F32), w1, HIGHEST)
    slot = iota((16, 432), 1) // 4 % 4
    zero = jnp.zeros((16, 432), BF16)
    w1a, w1b, w1c = split(w1, 3)
    one_lhs = jnp.concatenate([w1a, jnp.where(slot < 2, w1b, zero), jnp.where(slot < 1, w1c, zero)], axis=0)
    eye = (iota((32, 32), 0) == iota((32, 32), 1)).astype(F32)
    two_lhs = jnp.concatenate(split(dot_t(eye, w2_ref[...], HIGHEST), 3), axis=0)
    back_rows = []
    for q in range(8):
        line = []
        for s in range(8):
            if s & ~q:
                line.append(jnp.zeros((16, 32), F32))
            else:
                k = 0
                for qb, sb in zip(bits(q), bits(s)):
                    k = 3 * k + (1 if qb == 0 else 0 if sb else 2)
                line.append(w2_ref[16 * k : 16 * k + 16, :])
        back_rows.append(jnp.concatenate(line, axis=1))
    back_lhs = jnp.concatenate(split(jnp.concatenate(back_rows, axis=0), 2), axis=0)

    for t in range(2):
        part = x[:, 128 * t : 128 * t + 128]
        xs[t, 0:256] = part
        xs[t, 256:512] = part
    upper = iota((8, 128), 0) < 4

    def gather(t):
        for g in range(64):
            index = [1 + 2 * (g >> (2 - d) & 1) + (g >> (5 - d) & 1) for d in range(3)]
            at = cell(*index)
            value = xs[t, pl.ds(g, 8, stride=64), :]
            hi, mid, lo = split(value, 3)
            first = jnp.where(upper, hi.astype(F32), mid.astype(F32))
            second = jnp.where(upper, lo.astype(F32), 0.0)
            xc[at : at + 16, 128 * t : 128 * t + 128] = jnp.concatenate([first, second], axis=0).astype(BF16)

    gather(0)
    gather(1)
    for copy in copies:
        copy.wait_recv()
    lower = flags(0)
    for t in range(32):
        tile = unpack(t, recv, IN_AT, lower)
        xs[2, 8 * t : 8 * t + 8] = tile
        xs[2, 256 + 8 * t : 264 + 8 * t] = tile
    gather(2)

    four, five = range(1, 5), range(5)
    for d, (ri, rj, rl) in enumerate([((4,), four, four), (five, (4,), four), (five, five, (4,))]):
        source = [cell(i, j, l) for i in ri for j in rj for l in rl]
        target = [at - cell(*[4 if e == d else 0 for e in range(3)]) for at in source]
        moved = dot(jnp.concatenate([xc[at : at + 16, :] for at in source], axis=0), low_ref[d]).astype(BF16)
        for n, at in enumerate(target):
            xc[at : at + 16, :] = moved[16 * n : 16 * n + 16]

    def stacked(q, lanes):
        b = bits(q)
        tiles = []
        for k in range(27):
            at = cell(*[2 * b[d] + offsets(k)[d] for d in range(3)])
            tiles.append(xc[at : at + 16, 0:lanes])
        return jnp.concatenate(tiles, axis=0)

    def three(k):
        return 16 * (9 * k[0] + 3 * k[1] + k[2])

    for q in range(8):
        r = dot(one_lhs, stacked(q, 384))
        value = (r[32:48] + r[16:32]) + r[0:16]
        pre[q] = value[:, 0:256]
        hidden = jnp.where(value > 0, value, SLOPE * value)
        at = three([1 + b for b in bits(q)])
        for n, piece in enumerate(split(hidden, 3)):
            hk[n, at : at + 16, :] = piece

    two = range(1, 3)
    for d, (ri, rj, rl) in enumerate([((2,), two, two), (range(3), (2,), two), (range(3), range(3), (2,))]):
        source = [three((i, j, l)) for i in ri for j in rj for l in rl]
        rows = jnp.concatenate([hk[n, at : at + 16, :] for n in range(3) for at in source], axis=0)
        lanes = 384 if d < 2 else 256
        moved = dot(rows, low_ref[d, :, 0:lanes]).astype(BF16)
        step = three([2 if e == d else 0 for e in range(3)])
        for n in range(3):
            for m, at in enumerate(source):
                row = 16 * (n * len(source) + m)
                hk[n, at - step : at - step + 16, 0:lanes] = moved[row : row + 16]

    r = dot(two_lhs, hk[0, :, 0:256])
    r2 = dot(two_lhs[0:64], hk[1, :, 0:256])
    r3 = dot(two_lhs[0:32], hk[2, :, 0:256])
    pre_two = ((r[64:96] + r2[32:64]) + r3 + (r[32:64] + r2[0:32])) + r[0:32]
    lev_ref[...] = jnp.where(pre_two > 0, pre_two, SLOPE * pre_two)[:, 0:CELLS]
    grad = jnp.concatenate([g_ref[...], jnp.zeros((32, 40), F32)], axis=1)
    delta = grad * jnp.where(pre_two > 0, 1.0, SLOPE)

    pieces = split(delta, 3)
    r = dot(jnp.concatenate(pieces, axis=0), pickl_ref[...])
    picked = (r[0:32] + r[32:64]) + r[64:96]
    pack([picked[8 * t : 8 * t + 8] for t in range(4)], dsend, D_AT)
    dcopies = []
    for s, dims in enumerate(SUBSETS):
        rows = pl.ds(D_AT[s], D_ROWS[s])
        dcopies.append(
            pltpu.make_async_remote_copy(
                src_ref=dsend.at[rows],
                dst_ref=drecv.at[rows],
                send_sem=dsend_sem.at[s],
                recv_sem=drecv_sem.at[s],
                device_id=neighbour(dims, -1),
                device_id_type=MESH,
            )
        )
        dcopies[-1].start()

    d1, d2 = pieces[0], pieces[1]
    r = dot_t(hk[0, :, 0:256], d1) + dot_t(hk[0, :, 0:256], d2) + dot_t(hk[1, :, 0:256], d1)
    r = jnp.concatenate([r, jnp.zeros((16, 32), F32)], axis=0)
    part_ref[0:112, :] = jnp.concatenate([r[112 * n : 112 * n + 112] for n in range(4)], axis=1)

    for copy in dcopies:
        copy.wait_recv()
    higher = flags(3)
    halo = jnp.concatenate([unpack(t, drecv, D_AT, higher) for t in range(4)], axis=0)
    both = jnp.concatenate(split(jnp.concatenate([delta, halo], axis=1), 2), axis=0)
    by_shift = {0: both}
    for d in range(3):
        bit = 4 >> d
        keys = sorted(by_shift)
        moved = dot(jnp.concatenate([by_shift[s] for s in keys], axis=0), high_ref[d]).astype(BF16)
        for n, s in enumerate(keys):
            by_shift[s | bit] = moved[64 * n : 64 * n + 64]
    da = jnp.concatenate([by_shift[s][0:32, 0:256] for s in range(8)], axis=0)
    db = jnp.concatenate([by_shift[s][32:64, 0:256] for s in range(8)], axis=0)
    r = dot(back_lhs, da)
    r = (r[128:256] + dot(back_lhs[0:128], db)) + r[0:128]
    total = None
    for q in range(8):
        value = r[16 * q : 16 * q + 16]
        for t in range(2):
            back[t, pl.ds(q, 16, stride=8), :] = value[:, 128 * t : 128 * t + 128]
        d_one = value * jnp.where(pre[q] > 0, 1.0, SLOPE)
        term = dot_t(stacked(q, 256), jnp.concatenate(split(d_one, 2), axis=0))
        total = term if total is None else total + term
    hid_ref[...] = jnp.concatenate([back[0], back[1]], axis=1)[:, 0:CELLS]

    lane, row = iota((8, 128), 1), iota((8, 128), 0)
    packed = [jnp.zeros((8, 128), F32), jnp.zeros((8, 128), F32)]
    for k in range(27):
        tile = jnp.concatenate([total[16 * k : 16 * k + 8], jnp.zeros((8, 96), F32)], axis=1)
        tile = tile + pltpu.roll(tile, 112, 1)
        tile = tile + pltpu.roll(tile, 4, 0)
        tile = pltpu.roll(tile, 16 * (k % 8), 1)
        here = (lane // 16 == k % 8) & (row // 4 == k // 8 % 2)
        packed[k // 16] = jnp.where(here, tile, packed[k // 16])
    part_ref[112:128, :] = jnp.concatenate(packed, axis=0)
    for copy in copies + dcopies:
        copy.wait_send()


def sum_kernel(part_ref, out_ref, ra, rb, mine, final, sem_a, sem_b, sem_c, out_a, out_b, out_c):
    dp, where = lax.axis_index("dp"), lax.axis_index("space")
    b, core = where // 2, where % 2
    a = dp * 2 + core

    def near(j):
        p = (a + j) % 16
        return p, {"dp": p // 2, "space": b * 2 + p % 2}

    def far(j):
        p = (b + j) % 32
        return p, {"space": p * 2 + core}

    barrier = pltpu.get_barrier_semaphore()
    for j in range(1, 16):
        pl.semaphore_signal(barrier, inc=1, device_id=near(j)[1], device_id_type=MESH)
    for j in range(1, 32):
        pl.semaphore_signal(barrier, inc=1, device_id=far(j)[1], device_id_type=MESH)
    pl.semaphore_wait(barrier, 46)

    def copy(src, dst, out_sem, in_sem, device):
        return pltpu.make_async_remote_copy(
            src_ref=src, dst_ref=dst, send_sem=out_sem, recv_sem=in_sem, device_id=device, device_id_type=MESH
        )

    first = []
    for j in range(1, 16):
        p, device = near(j)
        first.append(copy(part_ref.at[p], ra.at[a], out_a.at[j], sem_a.at[a], device))
        first[-1].start()
    ra[a] = part_ref[a]
    for j in range(1, 16):
        p, device = near(j)
        copy(part_ref.at[p], ra.at[p], out_a.at[j], sem_a.at[p], device).wait_recv()
    value = jnp.sum(ra[...], axis=0)
    mine[...] = value
    rb[b] = value
    second = []
    for j in range(1, 32):
        p, device = far(j)
        second.append(copy(mine, rb.at[b], out_b.at[j], sem_b.at[b], device))
        second[-1].start()
    for j in range(1, 32):
        p, device = far(j)
        copy(mine, rb.at[p], out_b.at[j], sem_b.at[p], device).wait_recv()
    value = jnp.sum(rb[...], axis=0)
    final[...] = value
    out_ref[a] = value
    third = []
    for j in range(1, 16):
        p, device = near(j)
        third.append(copy(final, out_ref.at[a], out_c.at[j], sem_c.at[a], device))
        third[-1].start()
    for j in range(1, 16):
        p, device = near(j)
        copy(final, out_ref.at[p], out_c.at[j], sem_c.at[p], device).wait_recv()
    for c in first + second + third:
        c.wait_send()


def body(volume_in, filter_one, filter_two, out_grad):
    vmem = pl.BlockSpec(memory_space=pltpu.VMEM)
    dma = pltpu.SemaphoreType.DMA
    constants = [
        jnp.asarray(shift_matrices(-1), BF16),
        jnp.asarray(shift_matrices(1), BF16),
        jnp.asarray(pick_matrix(SIDE - 1), BF16),
        jnp.asarray(pick_matrix(0), BF16),
        jnp.asarray(spread_matrix(), F32),
    ]
    level, hidden, part = pl.pallas_call(
        level_kernel,
        out_shape=[
            jax.ShapeDtypeStruct((32, CELLS), F32),
            jax.ShapeDtypeStruct((128, CELLS), F32),
            jax.ShapeDtypeStruct((128, 128), F32),
        ],
        in_specs=[vmem] * 9,
        out_specs=[vmem] * 3,
        scratch_shapes=[
            pltpu.VMEM((3, 512, 128), F32),
            pltpu.VMEM((2000, 384), BF16),
            pltpu.VMEM((3, 432, 384), BF16),
            pltpu.VMEM((8, 16, 256), F32),
            pltpu.VMEM((2, 128, 128), F32),
            pltpu.VMEM((sum(IN_ROWS), 128), F32),
            pltpu.VMEM((sum(IN_ROWS), 128), F32),
            pltpu.VMEM((sum(D_ROWS), 128), F32),
            pltpu.VMEM((sum(D_ROWS), 128), F32),
            dma((7,)),
            dma((7,)),
            dma((7,)),
            dma((7,)),
        ],
        compiler_params=pltpu.CompilerParams(
            collective_id=0, has_side_effects=True, vmem_limit_bytes=48 * 2**20
        ),
    )(
        volume_in.reshape(256, CELLS),
        jnp.transpose(filter_one, (1, 2, 0)).reshape(64, 27),
        jnp.transpose(filter_two, (0, 2, 1)).reshape(432, 32),
        out_grad.reshape(32, CELLS),
        *constants,
    )
    total = pl.pallas_call(
        sum_kernel,
        out_shape=jax.ShapeDtypeStruct((16, 8, 128), F32),
        in_specs=[vmem],
        out_specs=vmem,
        scratch_shapes=[
            pltpu.VMEM((16, 8, 128), F32),
            pltpu.VMEM((32, 8, 128), F32),
            pltpu.VMEM((8, 128), F32),
            pltpu.VMEM((8, 128), F32),
            dma((16,)),
            dma((32,)),
            dma((16,)),
            dma((16,)),
            dma((32,)),
            dma((16,)),
        ],
        compiler_params=pltpu.CompilerParams(
            collective_id=1, has_side_effects=True, vmem_limit_bytes=16 * 2**20
        ),
    )(part.reshape(16, 8, 128))
    total = total.reshape(128, 128)
    grad_two = total[0:112].reshape(7, 16, 4, 32)
    grad_two = jnp.transpose(grad_two, (2, 0, 1, 3)).reshape(28, 16, 32)[0:27]
    grad_one = total[112:128].reshape(4, 4, 8, 16)
    grad_one = jnp.transpose(grad_one, (0, 2, 1, 3)).reshape(32, 4, 16)[0:27]
    return (
        level.reshape(1, 1, 32, CELLS),
        hidden.reshape(1, 1, 16, 8, CELLS),
        jnp.transpose(grad_one, (0, 2, 1)),
        jnp.transpose(grad_two, (0, 2, 1)),
    )


def solution(mesh):
    placed = (P("dp", "space", None, None, None), P(), P(), P("dp", "space", None, None))
    return jax.shard_map(
        body,
        mesh=mesh,
        in_specs=placed,
        out_specs=(P("dp", "space", None, None), P("dp", "space", None, None, None), P(), P()),
        check_vma=False,
    )
```

```python
import itertools

import jax
import jax.numpy as jnp
import numpy as np
from jax import lax
from jax.experimental import pallas as pl
from jax.experimental.pallas import tpu as pltpu
from jax.sharding import PartitionSpec as P

SLOPE = 0.3
SIDE = 6
CELLS = SIDE**3
BF16 = jnp.bfloat16
F32 = jnp.float32
MESH = pl.DeviceIdType.MESH
HIGHEST = lax.Precision.HIGHEST

SUBSETS = [(0,), (1,), (2,), (0, 1), (0, 2), (1, 2), (0, 1, 2)]
SIZES = [SIDE ** (3 - len(s)) for s in SUBSETS]
STARTS = [sum(SIZES[:i]) for i in range(7)]


def rows_for(tiles):
    rows = [8 * -(-tiles // (128 // size)) for size in SIZES]
    return rows, [sum(rows[:i]) for i in range(7)]


IN_ROWS, IN_AT = rows_for(32)
D_ROWS, D_AT = rows_for(4)


def lane_of(coords, outside):
    dims = tuple(d for d in range(3) if coords[d] == outside)
    rest = [coords[d] for d in range(3) if d not in dims]
    place = 0
    for c in rest:
        place = place * SIDE + c
    return place if not dims else 256 + STARTS[SUBSETS.index(dims)] + place


def shift_matrices(step):
    outside = -1 if step < 0 else SIDE
    span = range(-1, SIDE) if step < 0 else range(SIDE + 1)
    m = np.zeros((3, 384, 384), np.float32)
    for coords in itertools.product(span, repeat=3):
        for d in range(3):
            source = list(coords)
            source[d] += step
            if coords[d] != outside:
                m[d, lane_of(source, outside), lane_of(coords, outside)] = 1
    return m


def pick_matrix(edge):
    m = np.zeros((256, 128), np.float32)
    for dims, start in zip(SUBSETS, STARTS):
        rest = [d for d in range(3) if d not in dims]
        for place, digits in enumerate(itertools.product(range(SIDE), repeat=len(rest))):
            coords = [edge] * 3
            for d, digit in zip(rest, digits):
                coords[d] = digit
            m[lane_of(coords, None), start + place] = 1
    return m


def spread_matrix():
    m = np.zeros((27, 432), np.float32)
    for k in range(27):
        m[k, 16 * k : 16 * k + 12] = 1
    return m


def constant_rows():
    picks = np.zeros((256, 384), np.float32)
    picks[:, 0:128] = pick_matrix(SIDE - 1)
    picks[:, 128:256] = pick_matrix(0)
    return np.concatenate([*shift_matrices(-1), *shift_matrices(1), picks], axis=0)


def collect_matrix():
    m = np.zeros((432, 128), np.float32)
    for k in range(27):
        for c in range(4):
            m[16 * k + c, 32 * c + k] = 1
            m[16 * k + 4 + c, 32 * c + k] = 1
    return m


def iota(shape, dim):
    return lax.broadcasted_iota(jnp.int32, shape, dim)


def split(x, pieces):
    out = []
    for _ in range(pieces):
        piece = x.astype(BF16)
        out.append(piece)
        x = x - piece.astype(F32)
    return out


def dot(a, b, precision=None):
    return jnp.dot(a, b, preferred_element_type=F32, precision=precision)


def dot_t(a, b, precision=None):
    return lax.dot_general(a, b, (((1,), (1,)), ((), ())), preferred_element_type=F32, precision=precision)


def pack(tiles, buf, starts):
    lane = iota((8, 128), 1)
    for s in range(7):
        size = SIZES[s]
        per = 128 // size
        for block in range(-(-len(tiles) // per)):
            total = jnp.zeros((8, 128), F32)
            for i, tile in enumerate(tiles[block * per : (block + 1) * per]):
                moved = pltpu.roll(tile, (i * size - STARTS[s]) % 128, 1)
                total = jnp.where((lane >= i * size) & (lane < (i + 1) * size), moved, total)
            buf[starts[s] + 8 * block : starts[s] + 8 * block + 8, :] = total


def unpack(t, buf, starts, valid):
    lane = iota((8, 128), 1)
    total = jnp.zeros((8, 128), F32)
    for s in range(7):
        size = SIZES[s]
        per = 128 // size
        row = starts[s] + 8 * (t // per)
        moved = pltpu.roll(buf[row : row + 8, :], (STARTS[s] - (t % per) * size) % 128, 1)
        here = (lane >= STARTS[s]) & (lane < STARTS[s] + size) & (valid[s] > 0)
        total = jnp.where(here, moved, total)
    return total


def cell(i, j, l):
    return 16 * (25 * i + 5 * j + l)


def offsets(k):
    return (k // 9, k // 3 % 3, k % 3)


def bits(q):
    return (q >> 2 & 1, q >> 1 & 1, q & 1)


def level_kernel(
    x_hbm, w1_hbm, w2_hbm, g_hbm, table_hbm, spread_hbm, collect_hbm,
    lev_hbm, hid_hbm, one_hbm, two_hbm,
    x_ref, w1_ref, w2_ref, g_ref, table, spread_ref, collect_ref, load_sem,
    lev_ref, hid_ref, one_ref, two_ref, store_sem,
    xs, xc, hk, pre, back, send, recv, dsend, drecv, send_sem, recv_sem, dsend_sem, drecv_sem,
    one_own, one_parts, two_own, two_parts, two_sum, sum_in, sum_out,
):
    dp, where = lax.axis_index("dp"), lax.axis_index("space")
    coords = (where // 16, where // 4 % 4, where % 4)

    def neighbour(dims, step):
        moved = [(coords[d] + (step if d in dims else 0) + 4) % 4 for d in range(3)]
        return {"space": moved[0] * 16 + moved[1] * 4 + moved[2]}

    def flags(edge):
        inside = [jnp.where(coords[d] == edge, 0, 1) for d in range(3)]
        out = []
        for dims in SUBSETS:
            flag = 1
            for d in dims:
                flag = flag * inside[d]
            out.append(flag)
        return out

    def load(n, src, dst):
        copy = pltpu.make_async_copy(src, dst, load_sem.at[n])
        copy.start()
        return copy

    load_x = load(0, x_hbm, x_ref)
    picks, shifts = pl.ds(2304, 256), pl.ds(0, 2304)
    load_picks = load(1, table_hbm.at[picks], table.at[picks])
    loads = [
        load(2, w1_hbm, w1_ref),
        load(3, spread_hbm, spread_ref),
        load(4, w2_hbm, w2_ref),
        load(5, table_hbm.at[shifts], table.at[shifts]),
        load(6, g_hbm, g_ref),
        load(7, collect_hbm, collect_ref),
    ]

    def store(n, src, dst):
        copy = pltpu.make_async_copy(src, dst, store_sem.at[n])
        copy.start()
        return copy

    y, zc = where // 2 % 8, where // 16 * 2 + where % 2

    def on_dp(p):
        return {"dp": p}

    def on_y(p):
        return {"space": zc // 2 * 16 + p * 2 + zc % 2}

    def on_zc(p):
        return {"space": p // 2 * 16 + y * 2 + p % 2}

    barrier = pltpu.get_barrier_semaphore()
    for dims in SUBSETS:
        for step in (-1, 1):
            pl.semaphore_signal(barrier, inc=1, device_id=neighbour(dims, step), device_id_type=MESH)
    for me, device in ((dp, on_dp), (y, on_y), (zc, on_zc)):
        for j in range(1, 8):
            pl.semaphore_signal(barrier, inc=1, device_id=device((me + j) % 8), device_id_type=MESH)

    def rows16(n):
        return pl.ds(pl.multiple_of(16 * n, 16), 16)

    sent = []

    def exchange(stage, me, device, src, dst):
        def copy(j, to):
            p = (me + j) % 8
            return pltpu.make_async_remote_copy(
                src_ref=src(p),
                dst_ref=dst(to if to is not None else p),
                send_sem=sum_out.at[stage, j],
                recv_sem=sum_in.at[stage, to if to is not None else p],
                device_id=device(p),
                device_id_type=MESH,
            )

        for j in range(1, 8):
            sent.append(copy(j, me))
            sent[-1].start()

        def wait():
            for j in range(1, 8):
                copy(j, None).wait_recv()

        return wait

    def sum_of(parts):
        parts = [parts[16 * n : 16 * n + 16, :] for n in range(8)]
        while len(parts) > 1:
            parts = [parts[n] + parts[n + 1] for n in range(0, len(parts), 2)]
        return parts[0]

    load_x.wait()
    load_picks.wait()
    pick = table[2304:2560, 0:128]
    x = jnp.concatenate([x_ref[...], jnp.zeros((256, 40), F32)], axis=1)
    pieces = split(x, 3)
    picked = dot(pieces[0], pick) + dot(pieces[1], pick) + dot(pieces[2], pick)
    pack([picked[8 * t : 8 * t + 8] for t in range(32)], send, IN_AT)
    pl.semaphore_wait(barrier, 35)
    copies = []
    for s, dims in enumerate(SUBSETS):
        rows = pl.ds(IN_AT[s], IN_ROWS[s])
        copies.append(
            pltpu.make_async_remote_copy(
                src_ref=send.at[rows],
                dst_ref=recv.at[rows],
                send_sem=send_sem.at[s],
                recv_sem=recv_sem.at[s],
                device_id=neighbour(dims, 1),
                device_id_type=MESH,
            )
        )
        copies[-1].start()

    for copy in loads:
        copy.wait()
    w1 = dot(w1_ref[...], spread_ref[...], HIGHEST)
    w1 = jnp.where(iota((64, 432), 0) % 4 == iota((64, 432), 1) % 4, w1, 0.0)
    w1 = dot((iota((16, 64), 1) // 4 == iota((16, 64), 0)).astype(F32), w1, HIGHEST)
    slot = iota((16, 432), 1) // 4 % 4
    zero = jnp.zeros((16, 432), BF16)
    w1a, w1b, w1c = split(w1, 3)
    one_lhs = jnp.concatenate([w1a, jnp.where(slot < 2, w1b, zero), jnp.where(slot < 1, w1c, zero)], axis=0)
    eye = (iota((32, 32), 0) == iota((32, 32), 1)).astype(F32)
    two_lhs = jnp.concatenate(split(dot_t(eye, w2_ref[...], HIGHEST), 3), axis=0)
    back_rows = []
    for q in range(8):
        line = []
        for s in range(8):
            if s & ~q:
                line.append(jnp.zeros((16, 32), F32))
            else:
                k = 0
                for qb, sb in zip(bits(q), bits(s)):
                    k = 3 * k + (1 if qb == 0 else 0 if sb else 2)
                line.append(w2_ref[16 * k : 16 * k + 16, :])
        back_rows.append(jnp.concatenate(line, axis=1))
    back_lhs = jnp.concatenate(split(jnp.concatenate(back_rows, axis=0), 2), axis=0)

    for t in range(2):
        part = x[:, 128 * t : 128 * t + 128]
        xs[t, 0:256] = part
        xs[t, 256:512] = part
    upper = iota((8, 128), 0) < 4

    def gather(t):
        for g in range(64):
            index = [1 + 2 * (g >> (2 - d) & 1) + (g >> (5 - d) & 1) for d in range(3)]
            at = cell(*index)
            value = xs[t, pl.ds(g, 8, stride=64), :]
            hi, mid, lo = split(value, 3)
            first = jnp.where(upper, hi.astype(F32), mid.astype(F32))
            second = jnp.where(upper, lo.astype(F32), 0.0)
            xc[at : at + 16, 128 * t : 128 * t + 128] = jnp.concatenate([first, second], axis=0).astype(BF16)

    gather(0)
    gather(1)
    for copy in copies:
        copy.wait_recv()
    lower = flags(0)
    for t in range(32):
        tile = unpack(t, recv, IN_AT, lower)
        xs[2, 8 * t : 8 * t + 8] = tile
        xs[2, 256 + 8 * t : 264 + 8 * t] = tile
    gather(2)

    four, five = range(1, 5), range(5)
    for d, (ri, rj, rl) in enumerate([((4,), four, four), (five, (4,), four), (five, five, (4,))]):
        source = [cell(i, j, l) for i in ri for j in rj for l in rl]
        target = [at - cell(*[4 if e == d else 0 for e in range(3)]) for at in source]
        moved = dot(jnp.concatenate([xc[at : at + 16, :] for at in source], axis=0), table[384 * d : 384 * d + 384, :]).astype(BF16)
        for n, at in enumerate(target):
            xc[at : at + 16, :] = moved[16 * n : 16 * n + 16]

    def stacked(q, lanes):
        b = bits(q)
        tiles = []
        for k in range(27):
            at = cell(*[2 * b[d] + offsets(k)[d] for d in range(3)])
            tiles.append(xc[at : at + 16, 0:lanes])
        return jnp.concatenate(tiles, axis=0)

    def three(k):
        return 16 * (9 * k[0] + 3 * k[1] + k[2])

    for q in range(8):
        r = dot(one_lhs, stacked(q, 384))
        value = (r[32:48] + r[16:32]) + r[0:16]
        pre[q] = value[:, 0:256]
        hidden = jnp.where(value > 0, value, SLOPE * value)
        at = three([1 + b for b in bits(q)])
        for n, piece in enumerate(split(hidden, 3)):
            hk[n, at : at + 16, :] = piece

    two = range(1, 3)
    for d, (ri, rj, rl) in enumerate([((2,), two, two), (range(3), (2,), two), (range(3), range(3), (2,))]):
        source = [three((i, j, l)) for i in ri for j in rj for l in rl]
        rows = jnp.concatenate([hk[n, at : at + 16, :] for n in range(3) for at in source], axis=0)
        lanes = 384 if d < 2 else 256
        moved = dot(rows, table[384 * d : 384 * d + 384, 0:lanes]).astype(BF16)
        step = three([2 if e == d else 0 for e in range(3)])
        for n in range(3):
            for m, at in enumerate(source):
                row = 16 * (n * len(source) + m)
                hk[n, at - step : at - step + 16, 0:lanes] = moved[row : row + 16]

    r = dot(two_lhs, hk[0, :, 0:256])
    r2 = dot(two_lhs[0:64], hk[1, :, 0:256])
    r3 = dot(two_lhs[0:32], hk[2, :, 0:256])
    pre_two = ((r[64:96] + r2[32:64]) + r3 + (r[32:64] + r2[0:32])) + r[0:32]
    lev_ref[...] = jnp.where(pre_two > 0, pre_two, SLOPE * pre_two)[:, 0:CELLS]
    stores = [store(0, lev_ref, lev_hbm)]
    grad = jnp.concatenate([g_ref[...], jnp.zeros((32, 40), F32)], axis=1)
    delta = grad * jnp.where(pre_two > 0, 1.0, SLOPE)

    pieces = split(delta, 3)
    r = dot(jnp.concatenate(pieces, axis=0), table[2304:2560, 128:256])
    picked = (r[0:32] + r[32:64]) + r[64:96]
    pack([picked[8 * t : 8 * t + 8] for t in range(4)], dsend, D_AT)
    dcopies = []
    for s, dims in enumerate(SUBSETS):
        rows = pl.ds(D_AT[s], D_ROWS[s])
        dcopies.append(
            pltpu.make_async_remote_copy(
                src_ref=dsend.at[rows],
                dst_ref=drecv.at[rows],
                send_sem=dsend_sem.at[s],
                recv_sem=drecv_sem.at[s],
                device_id=neighbour(dims, -1),
                device_id_type=MESH,
            )
        )
        dcopies[-1].start()

    d1, d2 = pieces[0], pieces[1]
    r = dot_t(hk[0, :, 0:256], d1) + dot_t(hk[0, :, 0:256], d2) + dot_t(hk[1, :, 0:256], d1)
    r = jnp.concatenate([r, jnp.zeros((16, 32), F32)], axis=0)
    two_own[0:112, :] = jnp.concatenate([r[112 * n : 112 * n + 112] for n in range(4)], axis=1)
    two_own[112:128, :] = jnp.zeros((16, 128), F32)
    two_parts[0, rows16(dp), :] = two_own[rows16(dp), :]
    wait_two = exchange(0, dp, on_dp, lambda p: two_own.at[rows16(p)], lambda p: two_parts.at[0, rows16(p)])

    for copy in dcopies:
        copy.wait_recv()
    higher = flags(3)
    halo = jnp.concatenate([unpack(t, drecv, D_AT, higher) for t in range(4)], axis=0)
    both = jnp.concatenate(split(jnp.concatenate([delta, halo], axis=1), 2), axis=0)
    by_shift = {0: both}
    for d in range(3):
        bit = 4 >> d
        keys = sorted(by_shift)
        moved = dot(jnp.concatenate([by_shift[s] for s in keys], axis=0), table[1152 + 384 * d : 1536 + 384 * d, :]).astype(BF16)
        for n, s in enumerate(keys):
            by_shift[s | bit] = moved[64 * n : 64 * n + 64]
    da = jnp.concatenate([by_shift[s][0:32, 0:256] for s in range(8)], axis=0)
    db = jnp.concatenate([by_shift[s][32:64, 0:256] for s in range(8)], axis=0)
    r = dot(back_lhs, da)
    r = (r[128:256] + dot(back_lhs[0:128], db)) + r[0:128]
    ones = []
    for q in range(8):
        value = r[16 * q : 16 * q + 16]
        for t in range(2):
            back[t, pl.ds(q, 16, stride=8), :] = value[:, 128 * t : 128 * t + 128]
        ones.append(jnp.concatenate(split(value * jnp.where(pre[q] > 0, 1.0, SLOPE), 2), axis=0))
    hid_ref[...] = jnp.concatenate([back[0], back[1]], axis=1)[:, 0:CELLS]
    stores.append(store(1, hid_ref, hid_hbm))

    def reduce_two(stage, me, device):
        value = sum_of(two_parts.at[stage - 1])
        two_sum[stage - 1] = value
        two_parts[stage, rows16(me), :] = value
        return exchange(
            stage, me, device, lambda p: two_sum.at[stage - 1], lambda p: two_parts.at[stage, rows16(p)]
        )

    wait_two()
    wait_two = reduce_two(1, y, on_y)
    total = None
    for q in range(8):
        term = dot_t(stacked(q, 256), ones[q])
        total = term if total is None else total + term
    small = (iota((16, 32), 1) % 16 == iota((16, 32), 0)).astype(F32)
    one_own[0] = dot(dot_t(small, total, HIGHEST), collect_ref[...], HIGHEST)

    def reduce_one(stage, me, device):
        one_parts[stage, rows16(me), :] = one_own[stage]
        return exchange(
            4 + stage, me, device, lambda p: one_own.at[stage], lambda p: one_parts.at[stage, rows16(p)]
        )

    wait_one = reduce_one(0, dp, on_dp)
    wait_two()
    wait_two = reduce_two(2, zc, on_zc)
    wait_one()
    one_own[1] = sum_of(one_parts.at[0])
    wait_one = reduce_one(1, y, on_y)
    wait_two()
    wait_two = reduce_two(3, dp, on_dp)
    wait_one()
    one_own[2] = sum_of(one_parts.at[1])
    wait_one = reduce_one(2, zc, on_zc)
    wait_two()
    for n in range(4):
        count = 16 * min(7, 27 - 7 * n)
        two_ref[112 * n : 112 * n + count, :] = two_parts[3, 0:count, 32 * n : 32 * n + 32]
    stores.append(store(2, two_ref, two_hbm))
    wait_one()
    value = sum_of(one_parts.at[2])
    for c in range(4):
        one_ref[:, c, :] = value[:, 32 * c : 32 * c + 27]
    stores.append(store(3, one_ref, one_hbm))
    for copy in stores:
        copy.wait()
    for copy in copies + dcopies + sent:
        copy.wait_send()


def finish_kernel(*refs):
    sem = refs[-1]
    copies = [pltpu.make_async_copy(refs[n], refs[4 + n], sem.at[n]) for n in range(4)]
    for copy in copies:
        copy.start()
    for copy in copies:
        copy.wait()


def body(volume_in, filter_one, filter_two, out_grad):
    hbm = pl.BlockSpec(memory_space=pltpu.HBM)
    dma = pltpu.SemaphoreType.DMA
    shapes = [
        jax.ShapeDtypeStruct((32, CELLS), F32),
        jax.ShapeDtypeStruct((128, CELLS), F32),
        jax.ShapeDtypeStruct((16, 4, 27), F32),
        jax.ShapeDtypeStruct((432, 32), F32),
    ]
    results = pl.pallas_call(
        level_kernel,
        out_shape=shapes,
        in_specs=[hbm] * 7,
        out_specs=[hbm] * 4,
        scratch_shapes=[
            pltpu.VMEM((256, CELLS), F32),
            pltpu.VMEM((64, 27), F32),
            pltpu.VMEM((432, 32), F32),
            pltpu.VMEM((32, CELLS), F32),
            pltpu.VMEM((2560, 384), BF16),
            pltpu.VMEM((27, 432), F32),
            pltpu.VMEM((432, 128), F32),
            dma((8,)),
            pltpu.VMEM((32, CELLS), F32),
            pltpu.VMEM((128, CELLS), F32),
            pltpu.VMEM((16, 4, 27), F32),
            pltpu.VMEM((432, 32), F32),
            dma((4,)),
            pltpu.VMEM((3, 512, 128), F32),
            pltpu.VMEM((2000, 384), BF16),
            pltpu.VMEM((3, 432, 384), BF16),
            pltpu.VMEM((8, 16, 256), F32),
            pltpu.VMEM((2, 128, 128), F32),
            pltpu.VMEM((sum(IN_ROWS), 128), F32),
            pltpu.VMEM((sum(IN_ROWS), 128), F32),
            pltpu.VMEM((sum(D_ROWS), 128), F32),
            pltpu.VMEM((sum(D_ROWS), 128), F32),
            dma((7,)),
            dma((7,)),
            dma((7,)),
            dma((7,)),
            pltpu.VMEM((3, 16, 128), F32),
            pltpu.VMEM((3, 128, 128), F32),
            pltpu.VMEM((128, 128), F32),
            pltpu.VMEM((4, 128, 128), F32),
            pltpu.VMEM((3, 16, 128), F32),
            dma((7, 8)),
            dma((7, 8)),
        ],
        compiler_params=pltpu.CompilerParams(
            collective_id=0, has_side_effects=True, vmem_limit_bytes=60 * 2**20
        ),
    )(
        volume_in.reshape(256, CELLS),
        jnp.transpose(filter_one, (1, 2, 0)).reshape(64, 27),
        jnp.transpose(filter_two, (0, 2, 1)).reshape(432, 32),
        out_grad.reshape(32, CELLS),
        jnp.asarray(constant_rows(), BF16),
        jnp.asarray(spread_matrix(), F32),
        jnp.asarray(collect_matrix(), F32),
    )
    level, hidden, grad_one, grad_two = pl.pallas_call(
        finish_kernel,
        out_shape=shapes,
        in_specs=[hbm] * 4,
        out_specs=[hbm] * 4,
        scratch_shapes=[dma((4,))],
        compiler_params=pltpu.CompilerParams(vmem_limit_bytes=60 * 2**20),
    )(*results)
    return (
        level.reshape(1, 1, 32, CELLS),
        hidden.reshape(1, 1, 16, 8, CELLS),
        jnp.transpose(grad_one, (2, 0, 1)),
        jnp.transpose(grad_two.reshape(27, 16, 32), (0, 2, 1)),
    )


def solution(mesh):
    placed = (P("dp", "space", None, None, None), P(), P(), P("dp", "space", None, None))
    return jax.shard_map(
        body,
        mesh=mesh,
        in_specs=placed,
        out_specs=(P("dp", "space", None, None), P("dp", "space", None, None, None), P(), P()),
        check_vma=False,
    )
```

```python
import itertools

import jax
import jax.numpy as jnp
import numpy as np
from jax import lax
from jax.experimental import pallas as pl
from jax.experimental.pallas import tpu as pltpu
from jax.sharding import PartitionSpec as P

SLOPE = 0.3
SIDE = 6
CELLS = SIDE**3
BF16 = jnp.bfloat16
F32 = jnp.float32
MESH = pl.DeviceIdType.MESH
HIGHEST = lax.Precision.HIGHEST

SUBSETS = [(0,), (1,), (2,), (0, 1), (0, 2), (1, 2), (0, 1, 2)]
SIZES = [SIDE ** (3 - len(s)) for s in SUBSETS]
STARTS = [sum(SIZES[:i]) for i in range(7)]


def rows_for(counts):
    rows = [8 * -(-tiles // (128 // size)) for tiles, size in zip(counts, SIZES)]
    return rows, [sum(rows[:i]) for i in range(7)]


IN_ROWS, IN_AT = rows_for([24, 24, 24, 32, 32, 32, 32])
D_ROWS, D_AT = rows_for([4] * 7)


def lane_of(coords, outside):
    dims = tuple(d for d in range(3) if coords[d] == outside)
    rest = [coords[d] for d in range(3) if d not in dims]
    place = 0
    for c in rest:
        place = place * SIDE + c
    return place if not dims else 256 + STARTS[SUBSETS.index(dims)] + place


def shift_matrices(step):
    outside = -1 if step < 0 else SIDE
    span = range(-1, SIDE) if step < 0 else range(SIDE + 1)
    m = np.zeros((7, 384, 384), np.float32)
    for coords in itertools.product(span, repeat=3):
        for s, dims in enumerate(SUBSETS):
            source = [c + (step if d in dims else 0) for d, c in enumerate(coords)]
            if all(coords[d] != outside for d in dims):
                m[s, lane_of(source, outside), lane_of(coords, outside)] = 1
    return m


def pick_matrix(edge):
    m = np.zeros((256, 128), np.float32)
    for dims, start in zip(SUBSETS, STARTS):
        rest = [d for d in range(3) if d not in dims]
        for place, digits in enumerate(itertools.product(range(SIDE), repeat=len(rest))):
            coords = [edge] * 3
            for d, digit in zip(rest, digits):
                coords[d] = digit
            m[lane_of(coords, None), start + place] = 1
    return m


def spread_matrix():
    m = np.zeros((27, 432), np.float32)
    for k in range(27):
        m[k, 16 * k : 16 * k + 12] = 1
    return m


def constant_rows():
    picks = np.zeros((256, 384), np.float32)
    picks[:, 0:128] = pick_matrix(SIDE - 1)
    picks[:, 128:256] = pick_matrix(0)
    return np.concatenate([picks, *shift_matrices(-1), *shift_matrices(1)], axis=0)


def collect_matrix():
    m = np.zeros((432, 128), np.float32)
    for k in range(27):
        for c in range(4):
            m[16 * k + c, 32 * c + k] = 1
            m[16 * k + 4 + c, 32 * c + k] = 1
    return m


def iota(shape, dim):
    return lax.broadcasted_iota(jnp.int32, shape, dim)


def split(x, pieces):
    out = []
    for _ in range(pieces):
        piece = x.astype(BF16)
        out.append(piece)
        x = x - piece.astype(F32)
    return out


def dot(a, b, precision=None):
    return jnp.dot(a, b, preferred_element_type=F32, precision=precision)


def dot_t(a, b, precision=None):
    return lax.dot_general(a, b, (((1,), (1,)), ((), ())), preferred_element_type=F32, precision=precision)


def trimmed(tiles, d):
    weight = 4 >> d
    own = (iota((8, 128), 0) // weight) % 2 == 1
    other = 4 >> (d + 1) % 3
    out = []
    for t, tile in enumerate(tiles):
        if t & weight:
            out.append(tile)
        elif not t & other:
            out.append(jnp.where(own, tile, pltpu.roll(tiles[t | other], 8 - weight, 0)))
    return out


def trimmed_place(t, d):
    weight, other = 4 >> d, 4 >> (d + 1) % 3
    places = [n for n in range(32) if n & weight or not n & other]
    return (places.index(t), False) if t & weight else (places.index(t & ~other), bool(t & other))


def pack(tiles, buf, starts, trim=False):
    lane = iota((8, 128), 1)
    for s in range(7):
        size = SIZES[s]
        per = 128 // size
        these = trimmed(tiles, s) if trim and s < 3 else tiles
        for block in range(-(-len(these) // per)):
            total = jnp.zeros((8, 128), F32)
            for i, tile in enumerate(these[block * per : (block + 1) * per]):
                moved = pltpu.roll(tile, (i * size - STARTS[s]) % 128, 1)
                total = jnp.where((lane >= i * size) & (lane < (i + 1) * size), moved, total)
            buf[starts[s] + 8 * block : starts[s] + 8 * block + 8, :] = total


def unpack(t, buf, starts, valid, trim=False):
    lane = iota((8, 128), 1)
    total = jnp.zeros((8, 128), F32)
    for s in range(7):
        size = SIZES[s]
        per = 128 // size
        n, second = trimmed_place(t, s) if trim and s < 3 else (t, False)
        row = starts[s] + 8 * (n // per)
        moved = pltpu.roll(buf[row : row + 8, :], (STARTS[s] - (n % per) * size) % 128, 1)
        if second:
            moved = pltpu.roll(moved, 4 >> s, 0)
        here = (lane >= STARTS[s]) & (lane < STARTS[s] + size) & (valid[s] > 0)
        total = jnp.where(here, moved, total)
    return total


def cell(i, j, l):
    return 16 * (25 * i + 5 * j + l)


def offsets(k):
    return (k // 9, k // 3 % 3, k % 3)


def bits(q):
    return (q >> 2 & 1, q >> 1 & 1, q & 1)


def level_kernel(
    x_hbm, w1_hbm, w2_hbm, g_hbm, table_hbm, spread_hbm, collect_hbm,
    lev_hbm, hid_hbm, one_hbm, two_hbm,
    x_ref, w1_ref, w2_ref, g_ref, table, spread_ref, collect_ref, load_sem,
    lev_ref, hid_ref, one_ref, two_ref, store_sem,
    xs, xc, hk, pre, back, send, recv, dsend, drecv, send_sem, recv_sem, dsend_sem, drecv_sem,
    one_own, one_parts, two_own, two_parts, two_sum, sum_in, sum_out,
):
    dp, where = lax.axis_index("dp"), lax.axis_index("space")
    gx = lax.div(where, 16)
    rest = where - 16 * gx
    gy = lax.div(rest, 4)
    coords = (gx, gy, rest - 4 * gy)
    y = lax.div(rest, 2)
    core = rest - 2 * y

    def wrap(value, size):
        return jnp.where(value >= size, value - size, value)

    ups = [wrap(c + 1, 4) for c in coords]
    downs = [wrap(c + 3, 4) for c in coords]

    def neighbour(dims, step):
        moved = [(ups if step > 0 else downs)[d] if d in dims else coords[d] for d in range(3)]
        return {"space": moved[0] * 16 + moved[1] * 4 + moved[2]}

    def flags(edge):
        inside = [jnp.where(coords[d] == edge, 0, 1) for d in range(3)]
        out = []
        for dims in SUBSETS:
            flag = 1
            for d in dims:
                flag = flag * inside[d]
            out.append(flag)
        return out

    def load(n, src, dst):
        copy = pltpu.make_async_copy(src, dst, load_sem.at[n])
        copy.start()
        return copy

    load_x = load(0, x_hbm, x_ref)
    picks, shifts = pl.ds(0, 256), pl.ds(256, 5376)
    load_picks = load(1, table_hbm.at[picks], table.at[picks])
    loads = [
        load(2, w1_hbm, w1_ref),
        load(3, spread_hbm, spread_ref),
        load(4, w2_hbm, w2_ref),
        load(5, table_hbm.at[shifts], table.at[shifts]),
        load(6, g_hbm, g_ref),
        load(7, collect_hbm, collect_ref),
    ]

    def store(n, src, dst):
        copy = pltpu.make_async_copy(src, dst, store_sem.at[n])
        copy.start()
        return copy

    z_lo = lax.div(dp, 4)
    x_at, z_at = dp - 4 * z_lo, 2 * gx + z_lo
    xc_at = 2 * x_at + core
    xc_peers = []
    for j in range(4):
        p = wrap(x_at + j, 4)
        for c in (core, 1 - core):
            xc_peers.append((2 * p + c, {"dp": 4 * z_lo + p, "space": 16 * gx + 2 * y + c}))
    xc_peers = xc_peers[1:]
    y_peers = [(p, {"space": 16 * gx + 2 * p + core}) for p in (wrap(y + j, 8) for j in range(1, 8))]
    z_peers = []
    for j in range(1, 8):
        p = wrap(z_at + j, 8)
        high = lax.div(p, 2)
        z_peers.append((p, {"dp": 4 * (p - 2 * high) + x_at, "space": 16 * high + 2 * y + core}))

    barrier = pltpu.get_barrier_semaphore()
    for dims in SUBSETS:
        for step in (-1, 1):
            pl.semaphore_signal(barrier, inc=1, device_id=neighbour(dims, step), device_id_type=MESH)
    for _, device in xc_peers + z_peers:
        pl.semaphore_signal(barrier, inc=1, device_id=device, device_id_type=MESH)

    def rows16(n):
        return pl.ds(pl.multiple_of(16 * n, 16), 16)

    sent = []

    def exchange(stage, me, peers, src, dst):
        def copy(j, to):
            p, device = peers[j]
            return pltpu.make_async_remote_copy(
                src_ref=src(p),
                dst_ref=dst(to),
                send_sem=sum_out.at[stage, j],
                recv_sem=sum_in.at[stage, to],
                device_id=device,
                device_id_type=MESH,
            )

        for j in range(7):
            sent.append(copy(j, me))
            sent[-1].start()

        def wait():
            for j in range(7):
                copy(j, peers[j][0]).wait_recv()

        return wait

    def sum_of(parts):
        parts = [parts[16 * n : 16 * n + 16, :] for n in range(8)]
        while len(parts) > 1:
            parts = [parts[n] + parts[n + 1] for n in range(0, len(parts), 2)]
        return parts[0]

    load_x.wait()
    load_picks.wait()
    pick = table[0:256, 0:128]
    x = jnp.concatenate([x_ref[...], jnp.zeros((256, 40), F32)], axis=1)
    pieces = split(x, 3)
    picked = dot(pieces[0], pick) + dot(pieces[1], pick) + dot(pieces[2], pick)
    pack([picked[8 * t : 8 * t + 8] for t in range(32)], send, IN_AT, True)
    pl.semaphore_wait(barrier, 28)
    copies = []
    for s, dims in enumerate(SUBSETS):
        rows = pl.ds(IN_AT[s], IN_ROWS[s])
        copies.append(
            pltpu.make_async_remote_copy(
                src_ref=send.at[rows],
                dst_ref=recv.at[rows],
                send_sem=send_sem.at[s],
                recv_sem=recv_sem.at[s],
                device_id=neighbour(dims, 1),
                device_id_type=MESH,
            )
        )
        copies[-1].start()

    for copy in loads[0:3]:
        copy.wait()
    w1 = dot(w1_ref[...], spread_ref[...], HIGHEST)
    w1 = jnp.where(iota((64, 432), 0) % 4 == iota((64, 432), 1) % 4, w1, 0.0)
    w1 = dot((iota((16, 64), 1) // 4 == iota((16, 64), 0)).astype(F32), w1, HIGHEST)
    slot = iota((16, 432), 1) // 4 % 4
    zero = jnp.zeros((16, 432), BF16)
    w1a, w1b, w1c = split(w1, 3)
    large = jnp.where(slot == 0, w1a, zero)
    middle = jnp.where(slot == 0, w1b, jnp.where(slot == 1, w1a, zero))
    least = jnp.where(slot == 0, w1c, jnp.where(slot == 1, w1b, jnp.where(slot == 2, w1a, zero)))
    one_lhs = jnp.concatenate([large, middle, least], axis=0)
    eye = (iota((32, 32), 0) == iota((32, 32), 1)).astype(F32)
    two_lhs = jnp.concatenate(split(dot_t(eye, w2_ref[...], HIGHEST), 3), axis=0)
    back_rows = []
    for q in range(8):
        line = []
        for s in range(8):
            if s & ~q:
                line.append(jnp.zeros((16, 32), F32))
            else:
                k = 0
                for qb, sb in zip(bits(q), bits(s)):
                    k = 3 * k + (1 if qb == 0 else 0 if sb else 2)
                line.append(w2_ref[16 * k : 16 * k + 16, :])
        back_rows.append(jnp.concatenate(line, axis=1))
    back_lhs = jnp.concatenate(split(jnp.concatenate(back_rows, axis=0), 2), axis=0)

    for t in range(2):
        part = x[:, 128 * t : 128 * t + 128]
        xs[t, 0:256] = part
        xs[t, 256:512] = part
    upper = iota((8, 128), 0) < 4

    def gather(t):
        for g in range(64):
            index = [1 + 2 * (g >> (2 - d) & 1) + (g >> (5 - d) & 1) for d in range(3)]
            at = cell(*index)
            value = xs[t, pl.ds(g, 8, stride=64), :]
            hi, mid, lo = split(value, 3)
            first = jnp.where(upper, hi.astype(F32), mid.astype(F32))
            second = jnp.where(upper, lo.astype(F32), 0.0)
            xc[at : at + 16, 128 * t : 128 * t + 128] = jnp.concatenate([first, second], axis=0).astype(BF16)

    gather(0)
    gather(1)
    def down(s, first, last, lanes):
        return table[256 + 384 * s + first : 256 + 384 * s + last, 0:lanes]

    def up(s, first, last):
        return table[2944 + 384 * s + first : 2944 + 384 * s + last, 0:256]

    def shifted_cells(s):
        places = itertools.product(*[(4,) if d in SUBSETS[s] else range(1, 5) for d in range(3)])
        source = [cell(*place) for place in places]
        step = cell(*[4 if d in SUBSETS[s] else 0 for d in range(3)])
        return source, [at - step for at in source]

    for copy in loads[3:]:
        copy.wait()
    for s in range(7):
        source, target = shifted_cells(s)
        moved = dot(jnp.concatenate([xc[at : at + 16, 0:256] for at in source], axis=0), down(s, 0, 256, 256)).astype(BF16)
        for n, at in enumerate(target):
            xc[at : at + 16, 0:256] = moved[16 * n : 16 * n + 16]
    for copy in copies:
        copy.wait_recv()
    lower = flags(0)
    for t in range(32):
        tile = unpack(t, recv, IN_AT, lower, True)
        xs[2, 8 * t : 8 * t + 8] = tile
        xs[2, 256 + 8 * t : 264 + 8 * t] = tile
    gather(2)
    for s in range(7):
        source, target = shifted_cells(s)
        moved = dot(jnp.concatenate([xc[at : at + 16, 256:384] for at in source], axis=0), down(s, 256, 384, 384)).astype(BF16)
        for n, at in enumerate(target):
            xc[at : at + 16, 0:256] += moved[16 * n : 16 * n + 16, 0:256]
            xc[at : at + 16, 256:384] = moved[16 * n : 16 * n + 16, 256:384]

    def stacked(q, lanes):
        b = bits(q)
        tiles = []
        for k in range(27):
            at = cell(*[2 * b[d] + offsets(k)[d] for d in range(3)])
            tiles.append(xc[at : at + 16, 0:lanes])
        return jnp.concatenate(tiles, axis=0)

    def three(k):
        return 16 * (9 * k[0] + 3 * k[1] + k[2])

    for q in range(8):
        r = dot(one_lhs, stacked(q, 384))
        value = (r[32:48] + r[16:32]) + r[0:16]
        pre[q] = value[:, 0:256]
        hidden = jnp.where(value > 0, value, SLOPE * value)
        at = three([1 + b for b in bits(q)])
        for n, piece in enumerate(split(hidden, 3)):
            hk[n, at : at + 16, :] = piece

    for s, dims in enumerate(SUBSETS):
        places = itertools.product(*[(2,) if d in dims else (1, 2) for d in range(3)])
        source = [three(place) for place in places]
        rows = jnp.concatenate([hk[n, at : at + 16, :] for n in range(3) for at in source], axis=0)
        moved = dot(rows, down(s, 0, 384, 256)).astype(BF16)
        step = three([2 if d in dims else 0 for d in range(3)])
        for n in range(3):
            for m, at in enumerate(source):
                row = 16 * (n * len(source) + m)
                hk[n, at - step : at - step + 16, 0:256] = moved[row : row + 16]

    r = [dot(two_lhs[:, 144 * n : 144 * n + 144], hk[0, 144 * n : 144 * n + 144, 0:256]) for n in range(3)]
    r = (r[0] + r[1]) + r[2]
    r2 = dot(two_lhs[0:64], hk[1, :, 0:256])
    r3 = dot(two_lhs[0:32], hk[2, :, 0:256])
    pre_two = ((r[64:96] + r2[32:64]) + r3 + (r[32:64] + r2[0:32])) + r[0:32]
    lev_ref[...] = jnp.where(pre_two > 0, pre_two, SLOPE * pre_two)[:, 0:CELLS]
    stores = [store(0, lev_ref, lev_hbm)]
    grad = jnp.concatenate([g_ref[...], jnp.zeros((32, 40), F32)], axis=1)
    delta = grad * jnp.where(pre_two > 0, 1.0, SLOPE)

    pieces = split(delta, 3)
    r = dot(jnp.concatenate(pieces, axis=0), table[0:256, 128:256])
    picked = (r[0:32] + r[32:64]) + r[64:96]
    pack([picked[8 * t : 8 * t + 8] for t in range(4)], dsend, D_AT)
    dcopies = []
    for s, dims in enumerate(SUBSETS):
        rows = pl.ds(D_AT[s], D_ROWS[s])
        dcopies.append(
            pltpu.make_async_remote_copy(
                src_ref=dsend.at[rows],
                dst_ref=drecv.at[rows],
                send_sem=dsend_sem.at[s],
                recv_sem=drecv_sem.at[s],
                device_id=neighbour(dims, -1),
                device_id_type=MESH,
            )
        )
        dcopies[-1].start()

    d1, d2 = pieces[0], pieces[1]
    r = dot_t(hk[0, :, 0:256], d1) + dot_t(hk[0, :, 0:256], d2) + dot_t(hk[1, :, 0:256], d1)
    r = jnp.concatenate([r, jnp.zeros((16, 32), F32)], axis=0)
    two_own[0:112, :] = jnp.concatenate([r[112 * n : 112 * n + 112] for n in range(4)], axis=1)
    two_own[112:128, :] = jnp.zeros((16, 128), F32)
    two_parts[0, rows16(xc_at), :] = two_own[rows16(xc_at), :]
    wait_two = exchange(0, xc_at, xc_peers, lambda p: two_own.at[rows16(p)], lambda p: two_parts.at[0, rows16(p)])

    own = jnp.concatenate([d1, d2], axis=0)
    moved = [own] * 8
    for s, dims in enumerate(SUBSETS):
        moved[sum(4 >> d for d in dims)] = dot(own, up(s, 0, 256)).astype(BF16)
    for copy in dcopies:
        copy.wait_recv()
    higher = flags(3)
    halo = jnp.concatenate([unpack(t, drecv, D_AT, higher) for t in range(4)], axis=0)
    halo = jnp.concatenate(split(halo, 2), axis=0)
    for s, dims in enumerate(SUBSETS):
        n = sum(4 >> d for d in dims)
        moved[n] += dot(halo, up(s, 256, 384)).astype(BF16)
    da = jnp.concatenate([m[0:32] for m in moved], axis=0)
    db = jnp.concatenate([m[32:64] for m in moved], axis=0)
    r = dot(back_lhs, da)
    r = (r[128:256] + dot(back_lhs[0:128], db)) + r[0:128]
    ones = []
    for q in range(8):
        value = r[16 * q : 16 * q + 16]
        for t in range(2):
            back[t, pl.ds(q, 16, stride=8), :] = value[:, 128 * t : 128 * t + 128]
        ones.append(jnp.concatenate(split(value * jnp.where(pre[q] > 0, 1.0, SLOPE), 2), axis=0))
    hid_ref[...] = jnp.concatenate([back[0], back[1]], axis=1)[:, 0:CELLS]
    stores.append(store(1, hid_ref, hid_hbm))

    def reduce_two(stage, me, device):
        value = sum_of(two_parts.at[stage - 1])
        two_sum[stage - 1] = value
        two_parts[stage, rows16(me), :] = value
        return exchange(
            stage, me, device, lambda p: two_sum.at[stage - 1], lambda p: two_parts.at[stage, rows16(p)]
        )

    wait_two()
    wait_two = reduce_two(1, y, y_peers)
    total = None
    for q in range(8):
        term = dot_t(stacked(q, 256), ones[q])
        total = term if total is None else total + term
    small = (iota((16, 32), 1) % 16 == iota((16, 32), 0)).astype(F32)
    one_own[0] = dot(dot_t(small, total, HIGHEST), collect_ref[...], HIGHEST)

    def reduce_one(stage, me, device):
        one_parts[stage, rows16(me), :] = one_own[stage]
        return exchange(
            4 + stage, me, device, lambda p: one_own.at[stage], lambda p: one_parts.at[stage, rows16(p)]
        )

    wait_one = reduce_one(0, xc_at, xc_peers)
    wait_two()
    wait_two = reduce_two(2, z_at, z_peers)
    wait_one()
    one_own[1] = sum_of(one_parts.at[0])
    wait_one = reduce_one(1, y, y_peers)
    wait_two()
    wait_two = reduce_two(3, xc_at, xc_peers)
    wait_one()
    one_own[2] = sum_of(one_parts.at[1])
    wait_one = reduce_one(2, z_at, z_peers)
    wait_two()
    for n in range(4):
        count = 16 * min(7, 27 - 7 * n)
        two_ref[112 * n : 112 * n + count, :] = two_parts[3, 0:count, 32 * n : 32 * n + 32]
    stores.append(store(2, two_ref, two_hbm))
    wait_one()
    value = sum_of(one_parts.at[2])
    for c in range(4):
        one_ref[:, c, :] = value[:, 32 * c : 32 * c + 27]
    stores.append(store(3, one_ref, one_hbm))
    for copy in stores:
        copy.wait()
    for copy in copies + dcopies + sent:
        copy.wait_send()


def finish_kernel(*refs):
    in_sem, out_sem = refs[-2:]
    loads = [pltpu.make_async_copy(refs[n], refs[8 + n], in_sem.at[n]) for n in range(4)]
    stores = [pltpu.make_async_copy(refs[8 + n], refs[4 + n], out_sem.at[n]) for n in range(4)]
    for copy in loads:
        copy.start()
    for load, copy in zip(loads, stores):
        load.wait()
        copy.start()
    for copy in stores:
        copy.wait()


def body(volume_in, filter_one, filter_two, out_grad):
    hbm = pl.BlockSpec(memory_space=pltpu.HBM)
    dma = pltpu.SemaphoreType.DMA
    shapes = [
        jax.ShapeDtypeStruct((32, CELLS), F32),
        jax.ShapeDtypeStruct((128, CELLS), F32),
        jax.ShapeDtypeStruct((16, 4, 27), F32),
        jax.ShapeDtypeStruct((432, 32), F32),
    ]
    results = pl.pallas_call(
        level_kernel,
        out_shape=shapes,
        in_specs=[hbm] * 7,
        out_specs=[hbm] * 4,
        scratch_shapes=[
            pltpu.VMEM((256, CELLS), F32),
            pltpu.VMEM((64, 27), F32),
            pltpu.VMEM((432, 32), F32),
            pltpu.VMEM((32, CELLS), F32),
            pltpu.VMEM((5632, 384), BF16),
            pltpu.VMEM((27, 432), F32),
            pltpu.VMEM((432, 128), F32),
            dma((8,)),
            pltpu.VMEM((32, CELLS), F32),
            pltpu.VMEM((128, CELLS), F32),
            pltpu.VMEM((16, 4, 27), F32),
            pltpu.VMEM((432, 32), F32),
            dma((4,)),
            pltpu.VMEM((3, 512, 128), F32),
            pltpu.VMEM((2000, 384), BF16),
            pltpu.VMEM((3, 432, 384), BF16),
            pltpu.VMEM((8, 16, 256), F32),
            pltpu.VMEM((2, 128, 128), F32),
            pltpu.VMEM((sum(IN_ROWS), 128), F32),
            pltpu.VMEM((sum(IN_ROWS), 128), F32),
            pltpu.VMEM((sum(D_ROWS), 128), F32),
            pltpu.VMEM((sum(D_ROWS), 128), F32),
            dma((7,)),
            dma((7,)),
            dma((7,)),
            dma((7,)),
            pltpu.VMEM((3, 16, 128), F32),
            pltpu.VMEM((3, 128, 128), F32),
            pltpu.VMEM((128, 128), F32),
            pltpu.VMEM((4, 128, 128), F32),
            pltpu.VMEM((3, 16, 128), F32),
            dma((7, 8)),
            dma((7, 8)),
        ],
        compiler_params=pltpu.CompilerParams(
            collective_id=0, has_side_effects=True, vmem_limit_bytes=60 * 2**20
        ),
    )(
        volume_in.reshape(256, CELLS),
        jnp.transpose(filter_one, (1, 2, 0)).reshape(64, 27),
        jnp.transpose(filter_two, (0, 2, 1)).reshape(432, 32),
        out_grad.reshape(32, CELLS),
        jnp.asarray(constant_rows(), BF16),
        jnp.asarray(spread_matrix(), F32),
        jnp.asarray(collect_matrix(), F32),
    )
    level, hidden, grad_one, grad_two = pl.pallas_call(
        finish_kernel,
        out_shape=shapes,
        in_specs=[hbm] * 4,
        out_specs=[hbm] * 4,
        scratch_shapes=[*(pltpu.VMEM(shape.shape, F32) for shape in shapes), dma((4,)), dma((4,))],
        compiler_params=pltpu.CompilerParams(vmem_limit_bytes=60 * 2**20),
    )(*results)
    return (
        level.reshape(1, 1, 32, CELLS),
        hidden.reshape(1, 1, 16, 8, CELLS),
        jnp.transpose(grad_one, (2, 0, 1)),
        jnp.transpose(grad_two.reshape(27, 16, 32), (0, 2, 1)),
    )


def solution(mesh):
    placed = (P("dp", "space", None, None, None), P(), P(), P("dp", "space", None, None))
    return jax.shard_map(
        body,
        mesh=mesh,
        in_specs=placed,
        out_specs=(P("dp", "space", None, None), P("dp", "space", None, None, None), P(), P()),
        check_vma=False,
    )
```

```python
import itertools

import jax
import jax.numpy as jnp
import numpy as np
from jax import lax
from jax.experimental import pallas as pl
from jax.experimental.pallas import tpu as pltpu
from jax.sharding import PartitionSpec as P

SLOPE = 0.3
SIDE = 6
CELLS = SIDE**3
BF16 = jnp.bfloat16
F32 = jnp.float32
MESH = pl.DeviceIdType.MESH
HIGHEST = lax.Precision.HIGHEST

SUBSETS = [(0,), (1,), (2,), (0, 1), (0, 2), (1, 2), (0, 1, 2)]
SIZES = [SIDE ** (3 - len(s)) for s in SUBSETS]
STARTS = [sum(SIZES[:i]) for i in range(7)]


def rows_for(counts):
    rows = [8 * -(-tiles // (128 // size)) for tiles, size in zip(counts, SIZES)]
    return rows, [sum(rows[:i]) for i in range(7)]


IN_ROWS, IN_AT = rows_for([24, 24, 24, 32, 32, 32, 32])
D_ROWS, D_AT = rows_for([4] * 7)


def lane_of(coords, outside):
    dims = tuple(d for d in range(3) if coords[d] == outside)
    rest = [coords[d] for d in range(3) if d not in dims]
    place = 0
    for c in rest:
        place = place * SIDE + c
    return place if not dims else 256 + STARTS[SUBSETS.index(dims)] + place


def down_matrices():
    m = np.zeros((7, 384, 384), np.float32)
    for coords in itertools.product(range(-1, SIDE), repeat=3):
        for s, dims in enumerate(SUBSETS):
            source = [c - (d in dims) for d, c in enumerate(coords)]
            if all(coords[d] != -1 for d in dims):
                m[s, lane_of(source, -1), lane_of(coords, -1)] = 1
    return m


def up_matrices():
    m = np.zeros((7, 384, 384), np.float32)
    for coords in itertools.product(range(-1, SIDE), repeat=3):
        for s, dims in enumerate(SUBSETS):
            source = [c + (d in dims) for d, c in enumerate(coords)]
            if min(source) >= 0 and (min(coords) >= 0 or max(source) < SIDE):
                m[s, lane_of(source, SIDE), lane_of(coords, -1)] = 1
    return m


def pick_matrix(edge):
    m = np.zeros((256, 128), np.float32)
    for dims, start in zip(SUBSETS, STARTS):
        rest = [d for d in range(3) if d not in dims]
        for place, digits in enumerate(itertools.product(range(SIDE), repeat=len(rest))):
            coords = [edge] * 3
            for d, digit in zip(rest, digits):
                coords[d] = digit
            m[lane_of(coords, None), start + place] = 1
    return m


def spread_matrix():
    m = np.zeros((27, 432), np.float32)
    for k in range(27):
        m[k, 16 * k : 16 * k + 12] = 1
    return m


def constant_rows():
    picks = np.zeros((256, 384), np.float32)
    picks[:, 0:128] = pick_matrix(SIDE - 1)
    picks[:, 128:256] = pick_matrix(0)
    return np.concatenate([picks, *down_matrices(), *up_matrices()], axis=0)


def collect_matrix():
    m = np.zeros((432, 128), np.float32)
    for k in range(27):
        for c in range(4):
            m[16 * k + c, 32 * c + k] = 1
            m[16 * k + 4 + c, 32 * c + k] = 1
    return m


def iota(shape, dim):
    return lax.broadcasted_iota(jnp.int32, shape, dim)


def split(x, pieces):
    out = []
    for _ in range(pieces):
        piece = x.astype(BF16)
        out.append(piece)
        x = x - piece.astype(F32)
    return out


def dot(a, b, precision=None):
    return jnp.dot(a, b, preferred_element_type=F32, precision=precision)


def dot_t(a, b, precision=None):
    return lax.dot_general(a, b, (((1,), (1,)), ((), ())), preferred_element_type=F32, precision=precision)


def trimmed(tiles, d):
    weight = 4 >> d
    own = (iota((8, 128), 0) // weight) % 2 == 1
    other = 4 >> (d + 1) % 3
    out = []
    for t, tile in enumerate(tiles):
        if t & weight:
            out.append(tile)
        elif not t & other:
            out.append(jnp.where(own, tile, pltpu.roll(tiles[t | other], 8 - weight, 0)))
    return out


def trimmed_place(t, d):
    weight, other = 4 >> d, 4 >> (d + 1) % 3
    places = [n for n in range(32) if n & weight or not n & other]
    return (places.index(t), False) if t & weight else (places.index(t & ~other), bool(t & other))


def pack(tiles, buf, starts, trim=False):
    lane = iota((8, 128), 1)
    for s in range(7):
        size = SIZES[s]
        per = 128 // size
        these = trimmed(tiles, s) if trim and s < 3 else tiles
        for block in range(-(-len(these) // per)):
            total = jnp.zeros((8, 128), F32)
            for i, tile in enumerate(these[block * per : (block + 1) * per]):
                moved = pltpu.roll(tile, (i * size - STARTS[s]) % 128, 1)
                total = jnp.where((lane >= i * size) & (lane < (i + 1) * size), moved, total)
            buf[starts[s] + 8 * block : starts[s] + 8 * block + 8, :] = total


def unpack(t, buf, starts, valid, trim=False):
    lane = iota((8, 128), 1)
    total = jnp.zeros((8, 128), F32)
    for s in range(7):
        size = SIZES[s]
        per = 128 // size
        n, second = trimmed_place(t, s) if trim and s < 3 else (t, False)
        row = starts[s] + 8 * (n // per)
        moved = pltpu.roll(buf[row : row + 8, :], (STARTS[s] - (n % per) * size) % 128, 1)
        if second:
            moved = pltpu.roll(moved, 4 >> s, 0)
        here = (lane >= STARTS[s]) & (lane < STARTS[s] + size) & (valid[s] > 0)
        total = jnp.where(here, moved, total)
    return total


def cell(i, j, l):
    return 16 * (25 * i + 5 * j + l)


def offsets(k):
    return (k // 9, k // 3 % 3, k % 3)


def bits(q):
    return (q >> 2 & 1, q >> 1 & 1, q & 1)


def level_kernel(
    x_hbm, w1_hbm, w2_hbm, g_hbm, table_hbm, spread_hbm, collect_hbm,
    lev_hbm, hid_hbm, one_hbm, two_hbm,
    x_ref, w1_ref, w2_ref, g_ref, table, spread_ref, collect_ref, load_sem,
    lev_ref, hid_ref, one_ref, two_ref, store_sem,
    xs, xc, hk, pre, back, send, recv, dsend, drecv, send_sem, recv_sem, dsend_sem, drecv_sem,
    one_own, one_parts, two_own, two_parts, two_sum, sum_in, sum_out,
):
    dp, where = lax.axis_index("dp"), lax.axis_index("space")
    gx = lax.div(where, 16)
    rest = where - 16 * gx
    gy = lax.div(rest, 4)
    coords = (gx, gy, rest - 4 * gy)
    y = lax.div(rest, 2)
    core = rest - 2 * y

    def wrap(value, size):
        return jnp.where(value >= size, value - size, value)

    ups = [wrap(c + 1, 4) for c in coords]
    downs = [wrap(c + 3, 4) for c in coords]

    def neighbour(dims, step):
        moved = [(ups if step > 0 else downs)[d] if d in dims else coords[d] for d in range(3)]
        return {"space": moved[0] * 16 + moved[1] * 4 + moved[2]}

    def flags(edge):
        inside = [jnp.where(coords[d] == edge, 0, 1) for d in range(3)]
        out = []
        for dims in SUBSETS:
            flag = 1
            for d in dims:
                flag = flag * inside[d]
            out.append(flag)
        return out

    def load(n, src, dst):
        copy = pltpu.make_async_copy(src, dst, load_sem.at[n])
        copy.start()
        return copy

    load_x = load(0, x_hbm, x_ref)

    def store(n, src, dst):
        copy = pltpu.make_async_copy(src, dst, store_sem.at[n])
        copy.start()
        return copy

    z_lo = lax.div(dp, 4)
    x_at, z_at = dp - 4 * z_lo, 2 * gx + z_lo
    xc_at = 2 * x_at + core
    xc_peers = []
    for j in range(4):
        p = wrap(x_at + j, 4)
        for c in (core, 1 - core):
            xc_peers.append((2 * p + c, {"dp": 4 * z_lo + p, "space": 16 * gx + 2 * y + c}))
    xc_peers = xc_peers[1:]
    y_peers = [(p, {"space": 16 * gx + 2 * p + core}) for p in (wrap(y + j, 8) for j in range(1, 8))]
    z_peers = []
    for j in range(1, 8):
        p = wrap(z_at + j, 8)
        high = lax.div(p, 2)
        z_peers.append((p, {"dp": 4 * (p - 2 * high) + x_at, "space": 16 * high + 2 * y + core}))

    barrier = pltpu.get_barrier_semaphore()
    for dims in SUBSETS[::-1]:
        for step in (-1, 1):
            pl.semaphore_signal(barrier, inc=1, device_id=neighbour(dims, step), device_id_type=MESH)
    for _, device in z_peers + y_peers + xc_peers:
        pl.semaphore_signal(barrier, inc=1, device_id=device, device_id_type=MESH)
    picks, shifts = pl.ds(0, 256), pl.ds(256, 5376)
    load_picks = load(1, table_hbm.at[picks], table.at[picks])
    loads = [
        load(2, w1_hbm, w1_ref),
        load(3, spread_hbm, spread_ref),
        load(4, w2_hbm, w2_ref),
        load(5, table_hbm.at[shifts], table.at[shifts]),
        load(6, g_hbm, g_ref),
        load(7, collect_hbm, collect_ref),
    ]


    def rows16(n):
        return pl.ds(pl.multiple_of(16 * n, 16), 16)

    sent = []

    def exchange(stage, me, peers, src, dst):
        def copy(j, to):
            p, device = peers[j]
            return pltpu.make_async_remote_copy(
                src_ref=src(p),
                dst_ref=dst(to),
                send_sem=sum_out.at[stage, j],
                recv_sem=sum_in.at[stage, to],
                device_id=device,
                device_id_type=MESH,
            )

        for j in range(7):
            sent.append(copy(j, me))
            sent[-1].start()

        def wait():
            for j in range(7):
                copy(j, peers[j][0]).wait_recv()

        return wait

    def sum_of(parts):
        parts = [parts[16 * n : 16 * n + 16, :] for n in range(8)]
        while len(parts) > 1:
            parts = [parts[n] + parts[n + 1] for n in range(0, len(parts), 2)]
        return parts[0]

    load_x.wait()
    load_picks.wait()
    pick = table[0:256, 0:128]
    x = jnp.concatenate([x_ref[...], jnp.zeros((256, 40), F32)], axis=1)
    pieces = split(x, 3)
    picked = dot(pieces[0], pick) + dot(pieces[1], pick) + dot(pieces[2], pick)
    pack([picked[8 * t : 8 * t + 8] for t in range(32)], send, IN_AT, True)
    pl.semaphore_wait(barrier, 35)
    copies = []
    for s, dims in reversed(list(enumerate(SUBSETS))):
        rows = pl.ds(IN_AT[s], IN_ROWS[s])
        copies.append(
            pltpu.make_async_remote_copy(
                src_ref=send.at[rows],
                dst_ref=recv.at[rows],
                send_sem=send_sem.at[s],
                recv_sem=recv_sem.at[s],
                device_id=neighbour(dims, 1),
                device_id_type=MESH,
            )
        )
        copies[-1].start()

    for copy in loads[0:3]:
        copy.wait()
    w1 = dot(w1_ref[...], spread_ref[...], HIGHEST)
    w1 = jnp.where(iota((64, 432), 0) % 4 == iota((64, 432), 1) % 4, w1, 0.0)
    w1 = dot((iota((16, 64), 1) // 4 == iota((16, 64), 0)).astype(F32), w1, HIGHEST)
    slot = iota((16, 432), 1) // 4 % 4
    zero = jnp.zeros((16, 432), BF16)
    w1a, w1b, w1c = split(w1, 3)
    large = jnp.where(slot == 0, w1a, zero)
    middle = jnp.where(slot == 0, w1b, jnp.where(slot == 1, w1a, zero))
    least = jnp.where(slot == 0, w1c, jnp.where(slot == 1, w1b, jnp.where(slot == 2, w1a, zero)))
    one_lhs = jnp.concatenate([large, middle, least], axis=0)
    eye = (iota((32, 32), 0) == iota((32, 32), 1)).astype(F32)
    two_lhs = jnp.concatenate(split(dot_t(eye, w2_ref[...], HIGHEST), 3), axis=0)
    back_rows = []
    for q in range(8):
        line = []
        for s in range(8):
            if s & ~q:
                line.append(jnp.zeros((16, 32), F32))
            else:
                k = 0
                for qb, sb in zip(bits(q), bits(s)):
                    k = 3 * k + (1 if qb == 0 else 0 if sb else 2)
                line.append(w2_ref[16 * k : 16 * k + 16, :])
        back_rows.append(jnp.concatenate(line, axis=1))
    back_lhs = jnp.concatenate(split(jnp.concatenate(back_rows, axis=0), 2), axis=0)

    for t in range(2):
        part = x[:, 128 * t : 128 * t + 128]
        xs[t, 0:256] = part
        xs[t, 256:512] = part
    upper = iota((8, 128), 0) < 4

    def gather(t):
        for g in range(64):
            index = [1 + 2 * (g >> (2 - d) & 1) + (g >> (5 - d) & 1) for d in range(3)]
            at = cell(*index)
            value = xs[t, pl.ds(g, 8, stride=64), :]
            hi, mid, lo = split(value, 3)
            first = jnp.where(upper, hi.astype(F32), mid.astype(F32))
            second = jnp.where(upper, lo.astype(F32), 0.0)
            xc[at : at + 16, 128 * t : 128 * t + 128] = jnp.concatenate([first, second], axis=0).astype(BF16)

    gather(0)
    gather(1)
    def down(s, first, last, lanes):
        return table[256 + 384 * s + first : 256 + 384 * s + last, 0:lanes]

    def up(s, first, last, lanes):
        return table[2944 + 384 * s + first : 2944 + 384 * s + last, 0:lanes]

    def shifted_cells(s):
        places = itertools.product(*[(4,) if d in SUBSETS[s] else range(1, 5) for d in range(3)])
        source = [cell(*place) for place in places]
        step = cell(*[4 if d in SUBSETS[s] else 0 for d in range(3)])
        return source, [at - step for at in source]

    for copy in loads[3:]:
        copy.wait()
    for s in range(7):
        source, target = shifted_cells(s)
        moved = dot(jnp.concatenate([xc[at : at + 16, 0:256] for at in source], axis=0), down(s, 0, 256, 256)).astype(BF16)
        for n, at in enumerate(target):
            xc[at : at + 16, 0:256] = moved[16 * n : 16 * n + 16]
    for copy in copies:
        copy.wait_recv()
    lower = flags(0)
    for t in range(32):
        tile = unpack(t, recv, IN_AT, lower, True)
        xs[2, 8 * t : 8 * t + 8] = tile
        xs[2, 256 + 8 * t : 264 + 8 * t] = tile
    gather(2)
    for s in range(7):
        source, target = shifted_cells(s)
        moved = dot(jnp.concatenate([xc[at : at + 16, 256:384] for at in source], axis=0), down(s, 256, 384, 384)).astype(BF16)
        for n, at in enumerate(target):
            xc[at : at + 16, 0:256] += moved[16 * n : 16 * n + 16, 0:256]
            xc[at : at + 16, 256:384] = moved[16 * n : 16 * n + 16, 256:384]

    def stacked(q, first, last):
        b = bits(q)
        tiles = []
        for k in range(27):
            at = cell(*[2 * b[d] + offsets(k)[d] for d in range(3)])
            tiles.append(xc[at : at + 16, first:last])
        return jnp.concatenate(tiles, axis=0)

    def three(k):
        return 16 * (9 * k[0] + 3 * k[1] + k[2])

    for q in range(8):
        r = dot(one_lhs, stacked(q, 0, 384))
        value = (r[32:48] + r[16:32]) + r[0:16]
        pre[q] = value
        hidden = jnp.where(value > 0, value, SLOPE * value)
        at = three([1 + b for b in bits(q)])
        for n, piece in enumerate(split(hidden, 3)):
            hk[n, at : at + 16, :] = piece

    for s, dims in enumerate(SUBSETS):
        places = itertools.product(*[(2,) if d in dims else (1, 2) for d in range(3)])
        source = [three(place) for place in places]
        rows = jnp.concatenate([hk[n, at : at + 16, :] for n in range(3) for at in source], axis=0)
        moved = dot(rows, down(s, 0, 384, 256)).astype(BF16)
        step = three([2 if d in dims else 0 for d in range(3)])
        for n in range(3):
            for m, at in enumerate(source):
                row = 16 * (n * len(source) + m)
                hk[n, at - step : at - step + 16, 0:256] = moved[row : row + 16]

    r = [dot(two_lhs[:, 144 * n : 144 * n + 144], hk[0, 144 * n : 144 * n + 144, 0:256]) for n in range(3)]
    r = (r[0] + r[1]) + r[2]
    r2 = dot(two_lhs[0:64], hk[1, :, 0:256])
    r3 = dot(two_lhs[0:32], hk[2, :, 0:256])
    pre_two = ((r[64:96] + r2[32:64]) + r3 + (r[32:64] + r2[0:32])) + r[0:32]
    lev_ref[...] = jnp.where(pre_two > 0, pre_two, SLOPE * pre_two)[:, 0:CELLS]
    stores = [store(0, lev_ref, lev_hbm)]
    grad = jnp.concatenate([g_ref[...], jnp.zeros((32, 40), F32)], axis=1)
    delta = grad * jnp.where(pre_two > 0, 1.0, SLOPE)

    pieces = split(delta, 3)
    d1, d2 = pieces[0], pieces[1]
    r = dot_t(hk[0, :, 0:256], d1) + dot_t(hk[0, :, 0:256], d2) + dot_t(hk[1, :, 0:256], d1)
    r = jnp.concatenate([r, jnp.zeros((16, 32), F32)], axis=0)
    two_own[0:112, :] = jnp.concatenate([r[112 * n : 112 * n + 112] for n in range(4)], axis=1)
    two_own[112:128, :] = jnp.zeros((16, 128), F32)
    two_parts[0, rows16(xc_at), :] = two_own[rows16(xc_at), :]
    wait_two = exchange(0, xc_at, xc_peers, lambda p: two_own.at[rows16(p)], lambda p: two_parts.at[0, rows16(p)])

    own = jnp.concatenate([d1, d2], axis=0)
    moved = [jnp.concatenate([own, jnp.zeros((64, 128), BF16)], axis=1)] * 8
    for s, dims in enumerate(SUBSETS):
        moved[sum(4 >> d for d in dims)] = dot(own, up(s, 0, 256, 384)).astype(BF16)

    def through_filter(moved):
        r = dot(back_lhs, jnp.concatenate([m[0:32] for m in moved], axis=0))
        low = dot(back_lhs[0:128], jnp.concatenate([m[32:64] for m in moved], axis=0))
        return (r[128:256] + low) + r[0:128]

    given = through_filter(moved)
    ones = []
    for q in range(8):
        value = given[16 * q : 16 * q + 16] * jnp.where(pre[q] > 0, 1.0, SLOPE)
        ones.append(jnp.concatenate(split(value, 2), axis=0))

    total = None
    for q in range(8):
        term = dot_t(stacked(q, 0, 256), ones[q][:, 0:256])
        total = term if total is None else total + term
    for pair in ((1, 2), (3, 4), (5, 6), (7,)):
        left = jnp.concatenate([stacked(q, 256, 384) for q in pair], axis=1)
        total = total + dot_t(left, jnp.concatenate([ones[q][:, 256:384] for q in pair], axis=1))
    small = (iota((16, 32), 1) % 16 == iota((16, 32), 0)).astype(BF16)
    parts = [dot_t(small, piece) for piece in split(total, 3)]
    r = dot(jnp.concatenate(split((parts[2] + parts[1]) + parts[0], 3), axis=0), collect_ref[...])
    one_own[0] = (r[32:48] + r[16:32]) + r[0:16]

    def reduce_one(stage, me, peers):
        one_parts[stage, rows16(me), :] = one_own[stage]
        return exchange(
            4 + stage, me, peers, lambda p: one_own.at[stage], lambda p: one_parts.at[stage, rows16(p)]
        )

    def reduce_two(stage, me, peers):
        value = sum_of(two_parts.at[stage - 1])
        two_sum[stage - 1] = value
        two_parts[stage, rows16(me), :] = value
        return exchange(
            stage, me, peers, lambda p: two_sum.at[stage - 1], lambda p: two_parts.at[stage, rows16(p)]
        )

    wait_one = reduce_one(0, xc_at, xc_peers)

    r = dot(jnp.concatenate(pieces, axis=0), table[0:256, 128:256])
    picked = (r[0:32] + r[32:64]) + r[64:96]
    pack([picked[8 * t : 8 * t + 8] for t in range(4)], dsend, D_AT)
    dcopies = []
    for s, dims in reversed(list(enumerate(SUBSETS))):
        rows = pl.ds(D_AT[s], D_ROWS[s])
        dcopies.append(
            pltpu.make_async_remote_copy(
                src_ref=dsend.at[rows],
                dst_ref=drecv.at[rows],
                send_sem=dsend_sem.at[s],
                recv_sem=drecv_sem.at[s],
                device_id=neighbour(dims, -1),
                device_id_type=MESH,
            )
        )
        dcopies[-1].start()

    wait_two()
    wait_two = reduce_two(1, y, y_peers)
    wait_one()
    one_own[1] = sum_of(one_parts.at[0])
    wait_one = reduce_one(1, y, y_peers)
    wait_two()
    wait_two = reduce_two(2, z_at, z_peers)
    wait_one()
    one_own[2] = sum_of(one_parts.at[1])
    wait_one = reduce_one(2, z_at, z_peers)

    for copy in dcopies:
        copy.wait_recv()
    higher = flags(3)
    halo = jnp.concatenate([unpack(t, drecv, D_AT, higher) for t in range(4)], axis=0)
    halo = jnp.concatenate(split(halo, 2), axis=0)
    moved = [jnp.zeros((64, 256), BF16)] * 8
    for s, dims in enumerate(SUBSETS):
        moved[sum(4 >> d for d in dims)] = dot(halo, up(s, 256, 384, 256)).astype(BF16)
    value = given[:, 0:256] + through_filter(moved)
    for q in range(8):
        for t in range(2):
            back[t, pl.ds(q, 16, stride=8), :] = value[16 * q : 16 * q + 16, 128 * t : 128 * t + 128]
    hid_ref[...] = jnp.concatenate([back[0], back[1]], axis=1)[:, 0:CELLS]
    stores.append(store(1, hid_ref, hid_hbm))

    wait_two()
    wait_two = reduce_two(3, xc_at, xc_peers)
    wait_one()
    value = sum_of(one_parts.at[2])
    for c in range(4):
        one_ref[:, c, :] = value[:, 32 * c : 32 * c + 27]
    stores.append(store(3, one_ref, one_hbm))
    wait_two()
    for n in range(4):
        count = 16 * min(7, 27 - 7 * n)
        two_ref[112 * n : 112 * n + count, :] = two_parts[3, 0:count, 32 * n : 32 * n + 32]
    stores.append(store(2, two_ref, two_hbm))
    for copy in stores:
        copy.wait()
    for copy in copies + dcopies + sent:
        copy.wait_send()


def finish_kernel(*refs):
    in_sem, out_sem = refs[-2:]
    loads = [pltpu.make_async_copy(refs[n], refs[8 + n], in_sem.at[n]) for n in range(4)]
    stores = [pltpu.make_async_copy(refs[8 + n], refs[4 + n], out_sem.at[n]) for n in range(4)]
    for copy in loads:
        copy.start()
    for load, copy in zip(loads, stores):
        load.wait()
        copy.start()
    for copy in stores:
        copy.wait()


def body(volume_in, filter_one, filter_two, out_grad):
    hbm = pl.BlockSpec(memory_space=pltpu.HBM)
    dma = pltpu.SemaphoreType.DMA
    shapes = [
        jax.ShapeDtypeStruct((32, CELLS), F32),
        jax.ShapeDtypeStruct((128, CELLS), F32),
        jax.ShapeDtypeStruct((16, 4, 27), F32),
        jax.ShapeDtypeStruct((432, 32), F32),
    ]
    results = pl.pallas_call(
        level_kernel,
        out_shape=shapes,
        in_specs=[hbm] * 7,
        out_specs=[hbm] * 4,
        scratch_shapes=[
            pltpu.VMEM((256, CELLS), F32),
            pltpu.VMEM((64, 27), F32),
            pltpu.VMEM((432, 32), F32),
            pltpu.VMEM((32, CELLS), F32),
            pltpu.VMEM((5632, 384), BF16),
            pltpu.VMEM((27, 432), F32),
            pltpu.VMEM((432, 128), BF16),
            dma((8,)),
            pltpu.VMEM((32, CELLS), F32),
            pltpu.VMEM((128, CELLS), F32),
            pltpu.VMEM((16, 4, 27), F32),
            pltpu.VMEM((432, 32), F32),
            dma((4,)),
            pltpu.VMEM((3, 512, 128), F32),
            pltpu.VMEM((2000, 384), BF16),
            pltpu.VMEM((3, 432, 384), BF16),
            pltpu.VMEM((8, 16, 384), F32),
            pltpu.VMEM((2, 128, 128), F32),
            pltpu.VMEM((sum(IN_ROWS), 128), F32),
            pltpu.VMEM((sum(IN_ROWS), 128), F32),
            pltpu.VMEM((sum(D_ROWS), 128), F32),
            pltpu.VMEM((sum(D_ROWS), 128), F32),
            dma((7,)),
            dma((7,)),
            dma((7,)),
            dma((7,)),
            pltpu.VMEM((3, 16, 128), F32),
            pltpu.VMEM((3, 128, 128), F32),
            pltpu.VMEM((128, 128), F32),
            pltpu.VMEM((4, 128, 128), F32),
            pltpu.VMEM((3, 16, 128), F32),
            dma((7, 8)),
            dma((7, 8)),
        ],
        compiler_params=pltpu.CompilerParams(
            collective_id=0, has_side_effects=True, vmem_limit_bytes=60 * 2**20
        ),
    )(
        volume_in.reshape(256, CELLS),
        jnp.transpose(filter_one, (1, 2, 0)).reshape(64, 27),
        jnp.transpose(filter_two, (0, 2, 1)).reshape(432, 32),
        out_grad.reshape(32, CELLS),
        jnp.asarray(constant_rows(), BF16),
        jnp.asarray(spread_matrix(), F32),
        jnp.asarray(collect_matrix(), BF16),
    )
    level, hidden, grad_one, grad_two = pl.pallas_call(
        finish_kernel,
        out_shape=shapes,
        in_specs=[hbm] * 4,
        out_specs=[hbm] * 4,
        scratch_shapes=[*(pltpu.VMEM(shape.shape, F32) for shape in shapes), dma((4,)), dma((4,))],
        compiler_params=pltpu.CompilerParams(vmem_limit_bytes=60 * 2**20),
    )(*results)
    return (
        level.reshape(1, 1, 32, CELLS),
        hidden.reshape(1, 1, 16, 8, CELLS),
        jnp.transpose(grad_one, (2, 0, 1)),
        jnp.transpose(grad_two.reshape(27, 16, 32), (0, 2, 1)),
    )


def solution(mesh):
    placed = (P("dp", "space", None, None, None), P(), P(), P("dp", "space", None, None))
    return jax.shard_map(
        body,
        mesh=mesh,
        in_specs=placed,
        out_specs=(P("dp", "space", None, None), P("dp", "space", None, None, None), P(), P()),
        check_vma=False,
    )
```

```python
import itertools

import jax
import jax.numpy as jnp
import numpy as np
from jax import lax
from jax.experimental import pallas as pl
from jax.experimental.pallas import tpu as pltpu
from jax.sharding import PartitionSpec as P

SLOPE = 0.3
SIDE = 6
CELLS = SIDE**3
BF16 = jnp.bfloat16
F32 = jnp.float32
MESH = pl.DeviceIdType.MESH
HIGHEST = lax.Precision.HIGHEST

SUBSETS = [(0,), (1,), (2,), (0, 1), (0, 2), (1, 2), (0, 1, 2)]
SIZES = [SIDE ** (3 - len(s)) for s in SUBSETS]
STARTS = [sum(SIZES[:i]) for i in range(7)]


def rows_for(counts):
    rows = [8 * -(-tiles // (128 // size)) for tiles, size in zip(counts, SIZES)]
    return rows, [sum(rows[:i]) for i in range(7)]


IN_ROWS, IN_AT = rows_for([24, 24, 24, 32, 32, 32, 32])
D_ROWS, D_AT = rows_for([4] * 7)


def lane_of(coords, outside):
    dims = tuple(d for d in range(3) if coords[d] == outside)
    rest = [coords[d] for d in range(3) if d not in dims]
    place = 0
    for c in rest:
        place = place * SIDE + c
    return place if not dims else 256 + STARTS[SUBSETS.index(dims)] + place


def down_matrices():
    m = np.zeros((7, 384, 384), np.float32)
    for coords in itertools.product(range(-1, SIDE), repeat=3):
        for s, dims in enumerate(SUBSETS):
            source = [c - (d in dims) for d, c in enumerate(coords)]
            if all(coords[d] != -1 for d in dims):
                m[s, lane_of(source, -1), lane_of(coords, -1)] = 1
    return m


def up_matrices():
    m = np.zeros((7, 384, 384), np.float32)
    for coords in itertools.product(range(-1, SIDE), repeat=3):
        for s, dims in enumerate(SUBSETS):
            source = [c + (d in dims) for d, c in enumerate(coords)]
            if min(source) >= 0 and (min(coords) >= 0 or max(source) < SIDE):
                m[s, lane_of(source, SIDE), lane_of(coords, -1)] = 1
    return m


def pick_matrix(edge):
    m = np.zeros((256, 128), np.float32)
    for dims, start in zip(SUBSETS, STARTS):
        rest = [d for d in range(3) if d not in dims]
        for place, digits in enumerate(itertools.product(range(SIDE), repeat=len(rest))):
            coords = [edge] * 3
            for d, digit in zip(rest, digits):
                coords[d] = digit
            m[lane_of(coords, None), start + place] = 1
    return m


def spread_matrix():
    m = np.zeros((27, 432), np.float32)
    for k in range(27):
        m[k, 16 * k : 16 * k + 12] = 1
    return m


def constant_rows():
    picks = np.zeros((256, 384), np.float32)
    picks[:, 0:128] = pick_matrix(SIDE - 1)
    picks[:, 128:256] = pick_matrix(0)
    return np.concatenate([picks, *down_matrices(), *up_matrices()], axis=0)


def collect_matrix():
    m = np.zeros((432, 128), np.float32)
    for k in range(27):
        for c in range(4):
            m[16 * k + c, 32 * c + k] = 1
            m[16 * k + 4 + c, 32 * c + k] = 1
    return m


def iota(shape, dim):
    return lax.broadcasted_iota(jnp.int32, shape, dim)


def split(x, pieces):
    out = []
    for _ in range(pieces):
        piece = x.astype(BF16)
        out.append(piece)
        x = x - piece.astype(F32)
    return out


def dot(a, b, precision=None):
    return jnp.dot(a, b, preferred_element_type=F32, precision=precision)


def dot_t(a, b, precision=None):
    return lax.dot_general(a, b, (((1,), (1,)), ((), ())), preferred_element_type=F32, precision=precision)


def trimmed(tiles, d):
    weight = 4 >> d
    own = (iota((8, 128), 0) // weight) % 2 == 1
    other = 4 >> (d + 1) % 3
    out = []
    for t, tile in enumerate(tiles):
        if t & weight:
            out.append(tile)
        elif not t & other:
            out.append(jnp.where(own, tile, pltpu.roll(tiles[t | other], 8 - weight, 0)))
    return out


def trimmed_place(t, d):
    weight, other = 4 >> d, 4 >> (d + 1) % 3
    places = [n for n in range(32) if n & weight or not n & other]
    return (places.index(t), False) if t & weight else (places.index(t & ~other), bool(t & other))


def pack(tiles, buf, starts, trim=False):
    lane = iota((8, 128), 1)
    for s in range(7):
        size = SIZES[s]
        per = 128 // size
        these = trimmed(tiles, s) if trim and s < 3 else tiles
        for block in range(-(-len(these) // per)):
            total = jnp.zeros((8, 128), F32)
            for i, tile in enumerate(these[block * per : (block + 1) * per]):
                moved = pltpu.roll(tile, (i * size - STARTS[s]) % 128, 1)
                total = jnp.where((lane >= i * size) & (lane < (i + 1) * size), moved, total)
            buf[starts[s] + 8 * block : starts[s] + 8 * block + 8, :] = total


def unpack(t, buf, starts, valid, trim=False):
    lane = iota((8, 128), 1)
    total = jnp.zeros((8, 128), F32)
    for s in range(7):
        size = SIZES[s]
        per = 128 // size
        n, second = trimmed_place(t, s) if trim and s < 3 else (t, False)
        row = starts[s] + 8 * (n // per)
        moved = pltpu.roll(buf[row : row + 8, :], (STARTS[s] - (n % per) * size) % 128, 1)
        if second:
            moved = pltpu.roll(moved, 4 >> s, 0)
        here = (lane >= STARTS[s]) & (lane < STARTS[s] + size) & (valid[s] > 0)
        total = jnp.where(here, moved, total)
    return total


def cell(i, j, l):
    return 16 * (25 * i + 5 * j + l)


def offsets(k):
    return (k // 9, k // 3 % 3, k % 3)


def bits(q):
    return (q >> 2 & 1, q >> 1 & 1, q & 1)


def level_kernel(
    x_hbm, w1_hbm, w2_hbm, g_hbm, table_hbm, spread_hbm, collect_hbm,
    lev_ref, hid_ref, one_ref, two_ref,
    x_ref, w1_ref, w2_ref, g_ref, table, spread_ref, collect_ref, load_sem,
    xs, xc, hk, pre, back, send, recv, dsend, drecv, send_sem, recv_sem, dsend_sem, drecv_sem,
    one_own, one_parts, two_own, two_parts, two_sum, sum_in, sum_out,
):
    dp, where = lax.axis_index("dp"), lax.axis_index("space")
    gx = lax.div(where, 16)
    rest = where - 16 * gx
    gy = lax.div(rest, 4)
    coords = (gx, gy, rest - 4 * gy)
    y = lax.div(rest, 2)
    core = rest - 2 * y

    def wrap(value, size):
        return jnp.where(value >= size, value - size, value)

    ups = [wrap(c + 1, 4) for c in coords]
    downs = [wrap(c + 3, 4) for c in coords]

    def neighbour(dims, step):
        moved = [(ups if step > 0 else downs)[d] if d in dims else coords[d] for d in range(3)]
        return {"space": moved[0] * 16 + moved[1] * 4 + moved[2]}

    def flags(edge):
        inside = [jnp.where(coords[d] == edge, 0, 1) for d in range(3)]
        out = []
        for dims in SUBSETS:
            flag = 1
            for d in dims:
                flag = flag * inside[d]
            out.append(flag)
        return out

    def load(n, src, dst):
        copy = pltpu.make_async_copy(src, dst, load_sem.at[n])
        copy.start()
        return copy

    load_x = load(0, x_hbm, x_ref)

    z_lo = lax.div(dp, 4)
    x_at, z_at = dp - 4 * z_lo, 2 * gx + z_lo
    xc_at = 2 * x_at + core
    xc_peers = []
    for j in range(4):
        p = wrap(x_at + j, 4)
        for c in (core, 1 - core):
            xc_peers.append((2 * p + c, {"dp": 4 * z_lo + p, "space": 16 * gx + 2 * y + c}))
    xc_peers = xc_peers[1:]
    y_peers = [(p, {"space": 16 * gx + 2 * p + core}) for p in (wrap(y + j, 8) for j in range(1, 8))]
    z_peers = []
    for j in range(1, 8):
        p = wrap(z_at + j, 8)
        high = lax.div(p, 2)
        z_peers.append((p, {"dp": 4 * (p - 2 * high) + x_at, "space": 16 * high + 2 * y + core}))

    barrier = pltpu.get_barrier_semaphore()
    for dims in SUBSETS[::-1]:
        for step in (-1, 1):
            pl.semaphore_signal(barrier, inc=1, device_id=neighbour(dims, step), device_id_type=MESH)
    for _, device in z_peers + y_peers + xc_peers:
        pl.semaphore_signal(barrier, inc=1, device_id=device, device_id_type=MESH)
    picks, shifts = pl.ds(0, 256), pl.ds(256, 5376)
    load_picks = load(1, table_hbm.at[picks], table.at[picks])
    loads = [
        load(2, w1_hbm, w1_ref),
        load(3, spread_hbm, spread_ref),
        load(4, w2_hbm, w2_ref),
        load(5, table_hbm.at[shifts], table.at[shifts]),
        load(6, g_hbm, g_ref),
        load(7, collect_hbm, collect_ref),
    ]


    def rows16(n):
        return pl.ds(pl.multiple_of(16 * n, 16), 16)

    sent = []

    def exchange(stage, me, peers, src, dst):
        def copy(j, to):
            p, device = peers[j]
            return pltpu.make_async_remote_copy(
                src_ref=src(p),
                dst_ref=dst(to),
                send_sem=sum_out.at[stage, j],
                recv_sem=sum_in.at[stage, to],
                device_id=device,
                device_id_type=MESH,
            )

        for j in range(7):
            sent.append(copy(j, me))
            sent[-1].start()

        def wait():
            for j in range(7):
                copy(j, peers[j][0]).wait_recv()

        return wait

    def sum_of(parts):
        parts = [parts[16 * n : 16 * n + 16, :] for n in range(8)]
        while len(parts) > 1:
            parts = [parts[n] + parts[n + 1] for n in range(0, len(parts), 2)]
        return parts[0]

    load_x.wait()
    load_picks.wait()
    pick = table[0:256, 0:128]
    x = jnp.concatenate([x_ref[...], jnp.zeros((256, 40), F32)], axis=1)
    pieces = split(x, 3)
    picked = dot(pieces[0], pick) + dot(pieces[1], pick) + dot(pieces[2], pick)
    pack([picked[8 * t : 8 * t + 8] for t in range(32)], send, IN_AT, True)
    pl.semaphore_wait(barrier, 35)
    copies = []
    for s, dims in reversed(list(enumerate(SUBSETS))):
        rows = pl.ds(IN_AT[s], IN_ROWS[s])
        copies.append(
            pltpu.make_async_remote_copy(
                src_ref=send.at[rows],
                dst_ref=recv.at[rows],
                send_sem=send_sem.at[s],
                recv_sem=recv_sem.at[s],
                device_id=neighbour(dims, 1),
                device_id_type=MESH,
            )
        )
        copies[-1].start()

    for copy in loads[0:3]:
        copy.wait()
    w1 = dot(w1_ref[...], spread_ref[...], HIGHEST)
    w1 = jnp.where(iota((64, 432), 0) % 4 == iota((64, 432), 1) % 4, w1, 0.0)
    w1 = dot((iota((16, 64), 1) // 4 == iota((16, 64), 0)).astype(F32), w1, HIGHEST)
    slot = iota((16, 432), 1) // 4 % 4
    zero = jnp.zeros((16, 432), BF16)
    w1a, w1b, w1c = split(w1, 3)
    large = jnp.where(slot == 0, w1a, zero)
    middle = jnp.where(slot == 0, w1b, jnp.where(slot == 1, w1a, zero))
    least = jnp.where(slot == 0, w1c, jnp.where(slot == 1, w1b, jnp.where(slot == 2, w1a, zero)))
    one_lhs = jnp.concatenate([large, middle, least], axis=0)
    eye = (iota((32, 32), 0) == iota((32, 32), 1)).astype(F32)
    two_lhs = jnp.concatenate(split(dot_t(eye, w2_ref[...], HIGHEST), 3), axis=0)
    back_rows = []
    for q in range(8):
        line = []
        for s in range(8):
            if s & ~q:
                line.append(jnp.zeros((16, 32), F32))
            else:
                k = 0
                for qb, sb in zip(bits(q), bits(s)):
                    k = 3 * k + (1 if qb == 0 else 0 if sb else 2)
                line.append(w2_ref[16 * k : 16 * k + 16, :])
        back_rows.append(jnp.concatenate(line, axis=1))
    back_lhs = jnp.concatenate(split(jnp.concatenate(back_rows, axis=0), 2), axis=0)

    for t in range(2):
        part = x[:, 128 * t : 128 * t + 128]
        xs[t, 0:256] = part
        xs[t, 256:512] = part
    upper = iota((8, 128), 0) < 4

    def gather(t):
        for g in range(64):
            index = [1 + 2 * (g >> (2 - d) & 1) + (g >> (5 - d) & 1) for d in range(3)]
            at = cell(*index)
            value = xs[t, pl.ds(g, 8, stride=64), :]
            hi, mid, lo = split(value, 3)
            first = jnp.where(upper, hi.astype(F32), mid.astype(F32))
            second = jnp.where(upper, lo.astype(F32), 0.0)
            xc[at : at + 16, 128 * t : 128 * t + 128] = jnp.concatenate([first, second], axis=0).astype(BF16)

    gather(0)
    gather(1)
    def down(s, first, last, lanes):
        return table[256 + 384 * s + first : 256 + 384 * s + last, 0:lanes]

    def up(s, first, last, lanes):
        return table[2944 + 384 * s + first : 2944 + 384 * s + last, 0:lanes]

    def shifted_cells(s):
        places = itertools.product(*[(4,) if d in SUBSETS[s] else range(1, 5) for d in range(3)])
        source = [cell(*place) for place in places]
        step = cell(*[4 if d in SUBSETS[s] else 0 for d in range(3)])
        return source, [at - step for at in source]

    for copy in loads[3:]:
        copy.wait()
    for s in range(7):
        source, target = shifted_cells(s)
        moved = dot(jnp.concatenate([xc[at : at + 16, 0:256] for at in source], axis=0), down(s, 0, 256, 256)).astype(BF16)
        for n, at in enumerate(target):
            xc[at : at + 16, 0:256] = moved[16 * n : 16 * n + 16]
    for copy in copies:
        copy.wait_recv()
    lower = flags(0)
    for t in range(32):
        tile = unpack(t, recv, IN_AT, lower, True)
        xs[2, 8 * t : 8 * t + 8] = tile
        xs[2, 256 + 8 * t : 264 + 8 * t] = tile
    gather(2)
    for s in range(7):
        source, target = shifted_cells(s)
        moved = dot(jnp.concatenate([xc[at : at + 16, 256:384] for at in source], axis=0), down(s, 256, 384, 384)).astype(BF16)
        for n, at in enumerate(target):
            xc[at : at + 16, 0:256] += moved[16 * n : 16 * n + 16, 0:256]
            xc[at : at + 16, 256:384] = moved[16 * n : 16 * n + 16, 256:384]

    def stacked(q, first, last):
        b = bits(q)
        tiles = []
        for k in range(27):
            at = cell(*[2 * b[d] + offsets(k)[d] for d in range(3)])
            tiles.append(xc[at : at + 16, first:last])
        return jnp.concatenate(tiles, axis=0)

    def three(k):
        return 16 * (9 * k[0] + 3 * k[1] + k[2])

    for q in range(8):
        r = dot(one_lhs, stacked(q, 0, 384))
        value = (r[32:48] + r[16:32]) + r[0:16]
        pre[q] = value
        hidden = jnp.where(value > 0, value, SLOPE * value)
        at = three([1 + b for b in bits(q)])
        for n, piece in enumerate(split(hidden, 3)):
            hk[n, at : at + 16, :] = piece

    for s, dims in enumerate(SUBSETS):
        places = itertools.product(*[(2,) if d in dims else (1, 2) for d in range(3)])
        source = [three(place) for place in places]
        rows = jnp.concatenate([hk[n, at : at + 16, :] for n in range(3) for at in source], axis=0)
        moved = dot(rows, down(s, 0, 384, 256)).astype(BF16)
        step = three([2 if d in dims else 0 for d in range(3)])
        for n in range(3):
            for m, at in enumerate(source):
                row = 16 * (n * len(source) + m)
                hk[n, at - step : at - step + 16, 0:256] = moved[row : row + 16]

    r = [dot(two_lhs[:, 144 * n : 144 * n + 144], hk[0, 144 * n : 144 * n + 144, 0:256]) for n in range(3)]
    r = (r[0] + r[1]) + r[2]
    r2 = dot(two_lhs[0:64], hk[1, :, 0:256])
    r3 = dot(two_lhs[0:32], hk[2, :, 0:256])
    pre_two = ((r[64:96] + r2[32:64]) + r3 + (r[32:64] + r2[0:32])) + r[0:32]
    lev_ref[...] = jnp.where(pre_two > 0, pre_two, SLOPE * pre_two)[:, 0:CELLS]
    grad = jnp.concatenate([g_ref[...], jnp.zeros((32, 40), F32)], axis=1)
    delta = grad * jnp.where(pre_two > 0, 1.0, SLOPE)

    pieces = split(delta, 3)
    d1, d2 = pieces[0], pieces[1]
    r = dot_t(hk[0, :, 0:256], d1) + dot_t(hk[0, :, 0:256], d2) + dot_t(hk[1, :, 0:256], d1)
    r = jnp.concatenate([r, jnp.zeros((16, 32), F32)], axis=0)
    two_own[0:112, :] = jnp.concatenate([r[112 * n : 112 * n + 112] for n in range(4)], axis=1)
    two_own[112:128, :] = jnp.zeros((16, 128), F32)
    two_parts[0, rows16(xc_at), :] = two_own[rows16(xc_at), :]
    wait_two = exchange(0, xc_at, xc_peers, lambda p: two_own.at[rows16(p)], lambda p: two_parts.at[0, rows16(p)])

    own = jnp.concatenate([d1, d2], axis=0)
    moved = [jnp.concatenate([own, jnp.zeros((64, 128), BF16)], axis=1)] * 8
    for s, dims in enumerate(SUBSETS):
        moved[sum(4 >> d for d in dims)] = dot(own, up(s, 0, 256, 384)).astype(BF16)

    def through_filter(moved):
        r = dot(back_lhs, jnp.concatenate([m[0:32] for m in moved], axis=0))
        low = dot(back_lhs[0:128], jnp.concatenate([m[32:64] for m in moved], axis=0))
        return (r[128:256] + low) + r[0:128]

    given = through_filter(moved)
    ones = []
    for q in range(8):
        value = given[16 * q : 16 * q + 16] * jnp.where(pre[q] > 0, 1.0, SLOPE)
        ones.append(jnp.concatenate(split(value, 2), axis=0))

    total = None
    for q in range(8):
        term = dot_t(stacked(q, 0, 256), ones[q][:, 0:256])
        total = term if total is None else total + term
    for pair in ((1, 2), (3, 4), (5, 6), (7,)):
        left = jnp.concatenate([stacked(q, 256, 384) for q in pair], axis=1)
        total = total + dot_t(left, jnp.concatenate([ones[q][:, 256:384] for q in pair], axis=1))
    small = (iota((16, 32), 1) % 16 == iota((16, 32), 0)).astype(BF16)
    parts = [dot_t(small, piece) for piece in split(total, 3)]
    r = dot(jnp.concatenate(split((parts[2] + parts[1]) + parts[0], 3), axis=0), collect_ref[...])
    one_own[0] = (r[32:48] + r[16:32]) + r[0:16]

    def reduce_one(stage, me, peers):
        one_parts[stage, rows16(me), :] = one_own[stage]
        return exchange(
            4 + stage, me, peers, lambda p: one_own.at[stage], lambda p: one_parts.at[stage, rows16(p)]
        )

    def reduce_two(stage, me, peers):
        value = sum_of(two_parts.at[stage - 1])
        two_sum[stage - 1] = value
        two_parts[stage, rows16(me), :] = value
        return exchange(
            stage, me, peers, lambda p: two_sum.at[stage - 1], lambda p: two_parts.at[stage, rows16(p)]
        )

    wait_one = reduce_one(0, xc_at, xc_peers)

    r = dot(jnp.concatenate(pieces, axis=0), table[0:256, 128:256])
    picked = (r[0:32] + r[32:64]) + r[64:96]
    pack([picked[8 * t : 8 * t + 8] for t in range(4)], dsend, D_AT)
    dcopies = []
    for s, dims in reversed(list(enumerate(SUBSETS))):
        rows = pl.ds(D_AT[s], D_ROWS[s])
        dcopies.append(
            pltpu.make_async_remote_copy(
                src_ref=dsend.at[rows],
                dst_ref=drecv.at[rows],
                send_sem=dsend_sem.at[s],
                recv_sem=drecv_sem.at[s],
                device_id=neighbour(dims, -1),
                device_id_type=MESH,
            )
        )
        dcopies[-1].start()

    wait_two()
    wait_two = reduce_two(1, y, y_peers)
    wait_one()
    one_own[1] = sum_of(one_parts.at[0])
    wait_one = reduce_one(1, y, y_peers)
    wait_two()
    wait_two = reduce_two(2, z_at, z_peers)
    wait_one()
    one_own[2] = sum_of(one_parts.at[1])
    wait_one = reduce_one(2, z_at, z_peers)

    for copy in dcopies:
        copy.wait_recv()
    higher = flags(3)
    halo = jnp.concatenate([unpack(t, drecv, D_AT, higher) for t in range(4)], axis=0)
    halo = jnp.concatenate(split(halo, 2), axis=0)
    moved = [jnp.zeros((64, 256), BF16)] * 8
    for s, dims in enumerate(SUBSETS):
        moved[sum(4 >> d for d in dims)] = dot(halo, up(s, 256, 384, 256)).astype(BF16)
    value = given[:, 0:256] + through_filter(moved)
    for q in range(8):
        for t in range(2):
            back[t, pl.ds(q, 16, stride=8), :] = value[16 * q : 16 * q + 16, 128 * t : 128 * t + 128]
    hid_ref[...] = jnp.concatenate([back[0], back[1]], axis=1)[:, 0:CELLS]

    wait_two()
    wait_two = reduce_two(3, xc_at, xc_peers)
    wait_one()
    value = sum_of(one_parts.at[2])
    for c in range(4):
        one_ref[:, c, :] = value[:, 32 * c : 32 * c + 27]
    wait_two()
    for n in range(4):
        count = 16 * min(7, 27 - 7 * n)
        two_ref[112 * n : 112 * n + count, :] = two_parts[3, 0:count, 32 * n : 32 * n + 32]
    for copy in copies + dcopies + sent:
        copy.wait_send()


def finish_kernel(*refs):
    copies = [pltpu.make_async_copy(refs[n], refs[4 + n], refs[8].at[n]) for n in range(4)]
    for copy in copies:
        copy.start()
    for copy in copies:
        copy.wait()


def body(volume_in, filter_one, filter_two, out_grad):
    hbm = pl.BlockSpec(memory_space=pltpu.HBM)
    vmem = pl.BlockSpec(memory_space=pltpu.VMEM)
    dma = pltpu.SemaphoreType.DMA
    shapes = [
        jax.ShapeDtypeStruct((32, CELLS), F32),
        jax.ShapeDtypeStruct((128, CELLS), F32),
        jax.ShapeDtypeStruct((16, 4, 27), F32),
        jax.ShapeDtypeStruct((432, 32), F32),
    ]
    operands = (
        volume_in.reshape(256, CELLS),
        jnp.transpose(filter_one, (1, 2, 0)).reshape(64, 27),
        jnp.transpose(filter_two, (0, 2, 1)).reshape(432, 32),
        out_grad.reshape(32, CELLS),
        jnp.asarray(constant_rows(), BF16),
        jnp.asarray(spread_matrix(), F32),
        jnp.asarray(collect_matrix(), BF16),
    )
    results = pl.pallas_call(
        level_kernel,
        out_shape=[pltpu.VMEM(shape.shape, F32) for shape in shapes],
        in_specs=[hbm] * 7,
        out_specs=[vmem] * 4,
        scratch_shapes=[
            pltpu.VMEM((256, CELLS), F32),
            pltpu.VMEM((64, 27), F32),
            pltpu.VMEM((432, 32), F32),
            pltpu.VMEM((32, CELLS), F32),
            pltpu.VMEM((5632, 384), BF16),
            pltpu.VMEM((27, 432), F32),
            pltpu.VMEM((432, 128), BF16),
            dma((8,)),
            pltpu.VMEM((3, 512, 128), F32),
            pltpu.VMEM((2000, 384), BF16),
            pltpu.VMEM((3, 432, 384), BF16),
            pltpu.VMEM((8, 16, 384), F32),
            pltpu.VMEM((2, 128, 128), F32),
            pltpu.VMEM((sum(IN_ROWS), 128), F32),
            pltpu.VMEM((sum(IN_ROWS), 128), F32),
            pltpu.VMEM((sum(D_ROWS), 128), F32),
            pltpu.VMEM((sum(D_ROWS), 128), F32),
            dma((7,)),
            dma((7,)),
            dma((7,)),
            dma((7,)),
            pltpu.VMEM((3, 16, 128), F32),
            pltpu.VMEM((3, 128, 128), F32),
            pltpu.VMEM((128, 128), F32),
            pltpu.VMEM((4, 128, 128), F32),
            pltpu.VMEM((3, 16, 128), F32),
            dma((7, 8)),
            dma((7, 8)),
        ],
        compiler_params=pltpu.CompilerParams(
            collective_id=0, has_side_effects=True, vmem_limit_bytes=40 * 2**20
        ),
    )(*(pltpu.with_memory_space_constraint(operand, pltpu.HBM) for operand in operands))
    level, hidden, grad_one, grad_two = pl.pallas_call(
        finish_kernel,
        out_shape=shapes,
        in_specs=[vmem] * 4,
        out_specs=[hbm] * 4,
        scratch_shapes=[dma((4,))],
        compiler_params=pltpu.CompilerParams(vmem_limit_bytes=40 * 2**20),
    )(*results)
    return (
        level.reshape(1, 1, 32, CELLS),
        hidden.reshape(1, 1, 16, 8, CELLS),
        jnp.transpose(grad_one, (2, 0, 1)),
        jnp.transpose(grad_two.reshape(27, 16, 32), (0, 2, 1)),
    )


def solution(mesh):
    placed = (P("dp", "space", None, None, None), P(), P(), P("dp", "space", None, None))
    return jax.shard_map(
        body,
        mesh=mesh,
        in_specs=placed,
        out_specs=(P("dp", "space", None, None), P("dp", "space", None, None, None), P(), P()),
        check_vma=False,
    )
```

```python
import itertools

import jax
import jax.numpy as jnp
import numpy as np
from jax import lax
from jax.experimental import pallas as pl
from jax.experimental.pallas import tpu as pltpu
from jax.sharding import PartitionSpec as P

SLOPE = 0.3
SIDE = 6
CELLS = SIDE**3
BF16 = jnp.bfloat16
F32 = jnp.float32
MESH = pl.DeviceIdType.MESH
HIGHEST = lax.Precision.HIGHEST

SUBSETS = [(0,), (1,), (2,), (0, 1), (0, 2), (1, 2), (0, 1, 2)]
SIZES = [SIDE ** (3 - len(s)) for s in SUBSETS]
STARTS = [sum(SIZES[:i]) for i in range(7)]


def rows_for(counts):
    rows = [8 * -(-tiles // (128 // size)) for tiles, size in zip(counts, SIZES)]
    return rows, [sum(rows[:i]) for i in range(7)]


IN_ROWS, IN_AT = rows_for([24, 24, 24, 32, 32, 32, 32])
D_ROWS, D_AT = rows_for([4] * 7)


def lane_of(coords, outside):
    dims = tuple(d for d in range(3) if coords[d] == outside)
    rest = [coords[d] for d in range(3) if d not in dims]
    place = 0
    for c in rest:
        place = place * SIDE + c
    return place if not dims else 256 + STARTS[SUBSETS.index(dims)] + place


def down_matrices():
    m = np.zeros((7, 384, 384), np.float32)
    for coords in itertools.product(range(-1, SIDE), repeat=3):
        for s, dims in enumerate(SUBSETS):
            source = [c - (d in dims) for d, c in enumerate(coords)]
            if all(coords[d] != -1 for d in dims):
                m[s, lane_of(source, -1), lane_of(coords, -1)] = 1
    return m


def up_matrices():
    m = np.zeros((7, 384, 384), np.float32)
    for coords in itertools.product(range(-1, SIDE), repeat=3):
        for s, dims in enumerate(SUBSETS):
            source = [c + (d in dims) for d, c in enumerate(coords)]
            if min(source) >= 0 and (min(coords) >= 0 or max(source) < SIDE):
                m[s, lane_of(source, SIDE), lane_of(coords, -1)] = 1
    return m


def pick_matrix(edge):
    m = np.zeros((256, 128), np.float32)
    for dims, start in zip(SUBSETS, STARTS):
        rest = [d for d in range(3) if d not in dims]
        for place, digits in enumerate(itertools.product(range(SIDE), repeat=len(rest))):
            coords = [edge] * 3
            for d, digit in zip(rest, digits):
                coords[d] = digit
            m[lane_of(coords, None), start + place] = 1
    return m


def spread_matrix():
    m = np.zeros((27, 432), np.float32)
    for k in range(27):
        m[k, 16 * k : 16 * k + 12] = 1
    return m


def constant_rows():
    picks = np.zeros((256, 384), np.float32)
    picks[:, 0:128] = pick_matrix(SIDE - 1)
    picks[:, 128:256] = pick_matrix(0)
    return np.concatenate([picks, *down_matrices(), *up_matrices()], axis=0)


def collect_matrix():
    m = np.zeros((432, 128), np.float32)
    for k in range(27):
        for c in range(4):
            m[16 * k + c, 32 * c + k] = 1
            m[16 * k + 4 + c, 32 * c + k] = 1
    return m


def iota(shape, dim):
    return lax.broadcasted_iota(jnp.int32, shape, dim)


def split(x, pieces):
    out = []
    for _ in range(pieces):
        piece = x.astype(BF16)
        out.append(piece)
        x = x - piece.astype(F32)
    return out


def dot(a, b, precision=None):
    return jnp.dot(a, b, preferred_element_type=F32, precision=precision)


def dot_t(a, b, precision=None):
    return lax.dot_general(a, b, (((1,), (1,)), ((), ())), preferred_element_type=F32, precision=precision)


def trimmed(tiles, d):
    weight = 4 >> d
    own = (iota((8, 128), 0) // weight) % 2 == 1
    other = 4 >> (d + 1) % 3
    out = []
    for t, tile in enumerate(tiles):
        if t & weight:
            out.append(tile)
        elif not t & other:
            out.append(jnp.where(own, tile, pltpu.roll(tiles[t | other], 8 - weight, 0)))
    return out


def trimmed_place(t, d):
    weight, other = 4 >> d, 4 >> (d + 1) % 3
    places = [n for n in range(32) if n & weight or not n & other]
    return (places.index(t), False) if t & weight else (places.index(t & ~other), bool(t & other))


def pack(tiles, buf, starts, trim=False):
    lane = iota((8, 128), 1)
    for s in range(7):
        size = SIZES[s]
        per = 128 // size
        these = trimmed(tiles, s) if trim and s < 3 else tiles
        for block in range(-(-len(these) // per)):
            total = jnp.zeros((8, 128), F32)
            for i, tile in enumerate(these[block * per : (block + 1) * per]):
                moved = pltpu.roll(tile, (i * size - STARTS[s]) % 128, 1)
                total = jnp.where((lane >= i * size) & (lane < (i + 1) * size), moved, total)
            buf[starts[s] + 8 * block : starts[s] + 8 * block + 8, :] = total


def unpack(t, buf, starts, valid, trim=False):
    lane = iota((8, 128), 1)
    total = jnp.zeros((8, 128), F32)
    for s in range(7):
        size = SIZES[s]
        per = 128 // size
        n, second = trimmed_place(t, s) if trim and s < 3 else (t, False)
        row = starts[s] + 8 * (n // per)
        moved = pltpu.roll(buf[row : row + 8, :], (STARTS[s] - (n % per) * size) % 128, 1)
        if second:
            moved = pltpu.roll(moved, 4 >> s, 0)
        here = (lane >= STARTS[s]) & (lane < STARTS[s] + size) & (valid[s] > 0)
        total = jnp.where(here, moved, total)
    return total


def cell(i, j, l):
    return 16 * (25 * i + 5 * j + l)


def offsets(k):
    return (k // 9, k // 3 % 3, k % 3)


def bits(q):
    return (q >> 2 & 1, q >> 1 & 1, q & 1)


def level_kernel(
    x_hbm, w1_hbm, w2_hbm, g_hbm, table_hbm, spread_hbm, collect_hbm,
    lev_ref, hid_ref, one_ref, two_ref,
    x_ref, w1_ref, w2_ref, g_ref, table, spread_ref, collect_ref, load_sem,
    xs, xc, hk, pre, back, send, recv, dsend, drecv, send_sem, recv_sem, dsend_sem, drecv_sem,
    one_own, one_parts, two_own, two_parts, two_sum, sum_in, sum_out,
):
    dp, where = lax.axis_index("dp"), lax.axis_index("space")
    gx = lax.div(where, 16)
    rest = where - 16 * gx
    gy = lax.div(rest, 4)
    coords = (gx, gy, rest - 4 * gy)
    y = lax.div(rest, 2)
    core = rest - 2 * y

    def wrap(value, size):
        return jnp.where(value >= size, value - size, value)

    ups = [wrap(c + 1, 4) for c in coords]
    downs = [wrap(c + 3, 4) for c in coords]

    def neighbour(dims, step):
        moved = [(ups if step > 0 else downs)[d] if d in dims else coords[d] for d in range(3)]
        return {"space": moved[0] * 16 + moved[1] * 4 + moved[2]}

    def flags(edge):
        inside = [jnp.where(coords[d] == edge, 0, 1) for d in range(3)]
        out = []
        for dims in SUBSETS:
            flag = 1
            for d in dims:
                flag = flag * inside[d]
            out.append(flag)
        return out

    def load(n, src, dst):
        copy = pltpu.make_async_copy(src, dst, load_sem.at[n])
        copy.start()
        return copy

    load_x = load(0, x_hbm, x_ref)

    z_lo = lax.div(dp, 4)
    x_at, z_at = dp - 4 * z_lo, 2 * gx + z_lo
    xc_at = 2 * x_at + core
    xc_peers = []
    for j in (2, 1, 3, 0):
        p = wrap(x_at + j, 4)
        for c in (1 - core, core):
            xc_peers.append((2 * p + c, {"dp": 4 * z_lo + p, "space": 16 * gx + 2 * y + c}))
    xc_peers = xc_peers[:-1]
    y_peers = [(p, {"space": 16 * gx + 2 * p + core}) for p in (wrap(y + j, 8) for j in (4, 3, 5, 2, 6, 1, 7))]
    z_peers = []
    for j in (4, 3, 5, 2, 6, 1, 7):
        p = wrap(z_at + j, 8)
        high = lax.div(p, 2)
        z_peers.append((p, {"dp": 4 * (p - 2 * high) + x_at, "space": 16 * high + 2 * y + core}))

    barrier = pltpu.get_barrier_semaphore()
    for dims in SUBSETS[::-1]:
        for step in (-1, 1):
            pl.semaphore_signal(barrier, inc=1, device_id=neighbour(dims, step), device_id_type=MESH)
    for _, device in z_peers + y_peers + xc_peers:
        pl.semaphore_signal(barrier, inc=1, device_id=device, device_id_type=MESH)
    picks, shifts = pl.ds(0, 256), pl.ds(256, 5376)
    load_picks = load(1, table_hbm.at[picks], table.at[picks])
    loads = [
        load(2, w1_hbm, w1_ref),
        load(3, spread_hbm, spread_ref),
        load(4, w2_hbm, w2_ref),
        load(5, table_hbm.at[shifts], table.at[shifts]),
        load(6, g_hbm, g_ref),
        load(7, collect_hbm, collect_ref),
    ]


    def rows16(n):
        return pl.ds(pl.multiple_of(16 * n, 16), 16)

    sent = []

    def exchange(stage, me, peers, src, dst):
        def copy(j, to):
            p, device = peers[j]
            return pltpu.make_async_remote_copy(
                src_ref=src(p),
                dst_ref=dst(to),
                send_sem=sum_out.at[stage, j],
                recv_sem=sum_in.at[stage, to],
                device_id=device,
                device_id_type=MESH,
            )

        for j in range(7):
            sent.append(copy(j, me))
            sent[-1].start()

        def wait():
            for j in range(7):
                copy(j, peers[j][0]).wait_recv()

        return wait

    def sum_of(parts):
        parts = [parts[16 * n : 16 * n + 16, :] for n in range(8)]
        while len(parts) > 1:
            parts = [parts[n] + parts[n + 1] for n in range(0, len(parts), 2)]
        return parts[0]

    load_x.wait()
    load_picks.wait()
    pick = table[0:256, 0:128]
    x = jnp.concatenate([x_ref[...], jnp.zeros((256, 40), F32)], axis=1)
    pieces = split(x, 3)
    picked = dot(pieces[0], pick) + dot(pieces[1], pick) + dot(pieces[2], pick)
    pack([picked[8 * t : 8 * t + 8] for t in range(32)], send, IN_AT, True)
    pl.semaphore_wait(barrier, 35)
    copies = []
    for s, dims in reversed(list(enumerate(SUBSETS))):
        rows = pl.ds(IN_AT[s], IN_ROWS[s])
        copies.append(
            pltpu.make_async_remote_copy(
                src_ref=send.at[rows],
                dst_ref=recv.at[rows],
                send_sem=send_sem.at[s],
                recv_sem=recv_sem.at[s],
                device_id=neighbour(dims, 1),
                device_id_type=MESH,
            )
        )
        copies[-1].start()

    for copy in loads[0:3]:
        copy.wait()
    w1 = dot(w1_ref[...], spread_ref[...], HIGHEST)
    w1 = jnp.where(iota((64, 432), 0) % 4 == iota((64, 432), 1) % 4, w1, 0.0)
    w1 = dot((iota((16, 64), 1) // 4 == iota((16, 64), 0)).astype(F32), w1, HIGHEST)
    slot = iota((16, 432), 1) // 4 % 4
    zero = jnp.zeros((16, 432), BF16)
    w1a, w1b, w1c = split(w1, 3)
    large = jnp.where(slot == 0, w1a, zero)
    middle = jnp.where(slot == 0, w1b, jnp.where(slot == 1, w1a, zero))
    least = jnp.where(slot == 0, w1c, jnp.where(slot == 1, w1b, jnp.where(slot == 2, w1a, zero)))
    one_lhs = jnp.concatenate([large, middle, least], axis=0)
    eye = (iota((32, 32), 0) == iota((32, 32), 1)).astype(F32)
    two_lhs = jnp.concatenate(split(dot_t(eye, w2_ref[...], HIGHEST), 3), axis=0)
    back_rows = []
    for q in range(8):
        line = []
        for s in range(8):
            if s & ~q:
                line.append(jnp.zeros((16, 32), F32))
            else:
                k = 0
                for qb, sb in zip(bits(q), bits(s)):
                    k = 3 * k + (1 if qb == 0 else 0 if sb else 2)
                line.append(w2_ref[16 * k : 16 * k + 16, :])
        back_rows.append(jnp.concatenate(line, axis=1))
    back_lhs = jnp.concatenate(split(jnp.concatenate(back_rows, axis=0), 2), axis=0)

    for t in range(2):
        part = x[:, 128 * t : 128 * t + 128]
        xs[t, 0:256] = part
        xs[t, 256:512] = part
    upper = iota((8, 128), 0) < 4

    def gather(t):
        for g in range(64):
            index = [1 + 2 * (g >> (2 - d) & 1) + (g >> (5 - d) & 1) for d in range(3)]
            at = cell(*index)
            value = xs[t, pl.ds(g, 8, stride=64), :]
            hi, mid, lo = split(value, 3)
            first = jnp.where(upper, hi.astype(F32), mid.astype(F32))
            second = jnp.where(upper, lo.astype(F32), 0.0)
            xc[at : at + 16, 128 * t : 128 * t + 128] = jnp.concatenate([first, second], axis=0).astype(BF16)

    gather(0)
    gather(1)
    def down(s, first, last, lanes):
        return table[256 + 384 * s + first : 256 + 384 * s + last, 0:lanes]

    def up(s, first, last, lanes):
        return table[2944 + 384 * s + first : 2944 + 384 * s + last, 0:lanes]

    def shifted_cells(s):
        places = itertools.product(*[(4,) if d in SUBSETS[s] else range(1, 5) for d in range(3)])
        source = [cell(*place) for place in places]
        step = cell(*[4 if d in SUBSETS[s] else 0 for d in range(3)])
        return source, [at - step for at in source]

    for copy in loads[3:]:
        copy.wait()
    for s in range(7):
        source, target = shifted_cells(s)
        moved = dot(jnp.concatenate([xc[at : at + 16, 0:256] for at in source], axis=0), down(s, 0, 256, 256)).astype(BF16)
        for n, at in enumerate(target):
            xc[at : at + 16, 0:256] = moved[16 * n : 16 * n + 16]
    for copy in copies:
        copy.wait_recv()
    lower = flags(0)
    for t in range(32):
        tile = unpack(t, recv, IN_AT, lower, True)
        xs[2, 8 * t : 8 * t + 8] = tile
        xs[2, 256 + 8 * t : 264 + 8 * t] = tile
    gather(2)
    for s in range(7):
        source, target = shifted_cells(s)
        moved = dot(jnp.concatenate([xc[at : at + 16, 256:384] for at in source], axis=0), down(s, 256, 384, 384)).astype(BF16)
        for n, at in enumerate(target):
            xc[at : at + 16, 0:256] += moved[16 * n : 16 * n + 16, 0:256]
            xc[at : at + 16, 256:384] = moved[16 * n : 16 * n + 16, 256:384]

    def stacked(q, first, last):
        b = bits(q)
        tiles = []
        for k in range(27):
            at = cell(*[2 * b[d] + offsets(k)[d] for d in range(3)])
            tiles.append(xc[at : at + 16, first:last])
        return jnp.concatenate(tiles, axis=0)

    def three(k):
        return 16 * (9 * k[0] + 3 * k[1] + k[2])

    for q in range(8):
        r = dot(one_lhs, stacked(q, 0, 384))
        value = (r[32:48] + r[16:32]) + r[0:16]
        pre[q] = value
        hidden = jnp.where(value > 0, value, SLOPE * value)
        at = three([1 + b for b in bits(q)])
        for n, piece in enumerate(split(hidden, 3)):
            hk[n, at : at + 16, :] = piece

    for s, dims in enumerate(SUBSETS):
        places = itertools.product(*[(2,) if d in dims else (1, 2) for d in range(3)])
        source = [three(place) for place in places]
        rows = jnp.concatenate([hk[n, at : at + 16, :] for n in range(3) for at in source], axis=0)
        moved = dot(rows, down(s, 0, 384, 256)).astype(BF16)
        step = three([2 if d in dims else 0 for d in range(3)])
        for n in range(3):
            for m, at in enumerate(source):
                row = 16 * (n * len(source) + m)
                hk[n, at - step : at - step + 16, 0:256] = moved[row : row + 16]

    r = [dot(two_lhs[:, 144 * n : 144 * n + 144], hk[0, 144 * n : 144 * n + 144, 0:256]) for n in range(3)]
    r = (r[0] + r[1]) + r[2]
    r2 = dot(two_lhs[0:64], hk[1, :, 0:256])
    r3 = dot(two_lhs[0:32], hk[2, :, 0:256])
    pre_two = ((r[64:96] + r2[32:64]) + r3 + (r[32:64] + r2[0:32])) + r[0:32]
    lev_ref[...] = jnp.where(pre_two > 0, pre_two, SLOPE * pre_two)[:, 0:CELLS]
    grad = jnp.concatenate([g_ref[...], jnp.zeros((32, 40), F32)], axis=1)
    delta = grad * jnp.where(pre_two > 0, 1.0, SLOPE)

    pieces = split(delta, 3)
    d1, d2 = pieces[0], pieces[1]
    r = dot_t(hk[0, :, 0:256], d1) + dot_t(hk[0, :, 0:256], d2) + dot_t(hk[1, :, 0:256], d1)
    r = jnp.concatenate([r, jnp.zeros((16, 32), F32)], axis=0)
    two_own[0:112, :] = jnp.concatenate([r[112 * n : 112 * n + 112] for n in range(4)], axis=1)
    two_own[112:128, :] = jnp.zeros((16, 128), F32)
    two_parts[0, rows16(xc_at), :] = two_own[rows16(xc_at), :]
    wait_two = exchange(0, xc_at, xc_peers, lambda p: two_own.at[rows16(p)], lambda p: two_parts.at[0, rows16(p)])

    own = jnp.concatenate([d1, d2], axis=0)
    moved = [jnp.concatenate([own, jnp.zeros((64, 128), BF16)], axis=1)] * 8
    for s, dims in enumerate(SUBSETS):
        moved[sum(4 >> d for d in dims)] = dot(own, up(s, 0, 256, 384)).astype(BF16)

    def through_filter(moved):
        r = dot(back_lhs, jnp.concatenate([m[0:32] for m in moved], axis=0))
        low = dot(back_lhs[0:128], jnp.concatenate([m[32:64] for m in moved], axis=0))
        return (r[128:256] + low) + r[0:128]

    given = through_filter(moved)
    ones = []
    for q in range(8):
        value = given[16 * q : 16 * q + 16] * jnp.where(pre[q] > 0, 1.0, SLOPE)
        ones.append(jnp.concatenate(split(value, 2), axis=0))

    total = None
    for q in range(8):
        term = dot_t(stacked(q, 0, 256), ones[q][:, 0:256])
        total = term if total is None else total + term
    for pair in ((1, 2), (3, 4), (5, 6), (7,)):
        left = jnp.concatenate([stacked(q, 256, 384) for q in pair], axis=1)
        total = total + dot_t(left, jnp.concatenate([ones[q][:, 256:384] for q in pair], axis=1))
    def reduce_one(stage, me, peers):
        one_parts[stage, rows16(me), :] = one_own[stage]
        return exchange(
            4 + stage, me, peers, lambda p: one_own.at[stage], lambda p: one_parts.at[stage, rows16(p)]
        )

    def reduce_two(stage, me, peers):
        value = sum_of(two_parts.at[stage - 1])
        two_sum[stage - 1] = value
        two_parts[stage, rows16(me), :] = value
        return exchange(
            stage, me, peers, lambda p: two_sum.at[stage - 1], lambda p: two_parts.at[stage, rows16(p)]
        )

    wait_two()
    wait_two = reduce_two(1, y, y_peers)
    small = (iota((16, 32), 1) % 16 == iota((16, 32), 0)).astype(BF16)
    parts = [dot_t(small, piece) for piece in split(total, 3)]
    r = dot(jnp.concatenate(split((parts[2] + parts[1]) + parts[0], 3), axis=0), collect_ref[...])
    one_own[0] = (r[32:48] + r[16:32]) + r[0:16]

    wait_one = reduce_one(0, xc_at, xc_peers)

    r = dot(jnp.concatenate(pieces, axis=0), table[0:256, 128:256])
    picked = (r[0:32] + r[32:64]) + r[64:96]
    pack([picked[8 * t : 8 * t + 8] for t in range(4)], dsend, D_AT)
    dcopies = []
    for s, dims in reversed(list(enumerate(SUBSETS))):
        rows = pl.ds(D_AT[s], D_ROWS[s])
        dcopies.append(
            pltpu.make_async_remote_copy(
                src_ref=dsend.at[rows],
                dst_ref=drecv.at[rows],
                send_sem=dsend_sem.at[s],
                recv_sem=drecv_sem.at[s],
                device_id=neighbour(dims, -1),
                device_id_type=MESH,
            )
        )
        dcopies[-1].start()

    wait_one()
    one_own[1] = sum_of(one_parts.at[0])
    wait_one = reduce_one(1, y, y_peers)
    wait_two()
    wait_two = reduce_two(2, z_at, z_peers)
    wait_one()
    one_own[2] = sum_of(one_parts.at[1])
    wait_one = reduce_one(2, z_at, z_peers)

    for copy in dcopies:
        copy.wait_recv()
    higher = flags(3)
    halo = jnp.concatenate([unpack(t, drecv, D_AT, higher) for t in range(4)], axis=0)
    halo = jnp.concatenate(split(halo, 2), axis=0)
    moved = [jnp.zeros((64, 256), BF16)] * 8
    for s, dims in enumerate(SUBSETS):
        moved[sum(4 >> d for d in dims)] = dot(halo, up(s, 256, 384, 256)).astype(BF16)
    value = given[:, 0:256] + through_filter(moved)
    for q in range(8):
        for t in range(2):
            back[t, pl.ds(q, 16, stride=8), :] = value[16 * q : 16 * q + 16, 128 * t : 128 * t + 128]
    hid_ref[...] = jnp.concatenate([back[0], back[1]], axis=1)[:, 0:CELLS]

    wait_two()
    wait_two = reduce_two(3, xc_at, xc_peers)
    wait_one()
    value = sum_of(one_parts.at[2])
    for c in range(4):
        one_ref[:, c, :] = value[:, 32 * c : 32 * c + 27]
    wait_two()
    for n in range(4):
        count = 16 * min(7, 27 - 7 * n)
        two_ref[112 * n : 112 * n + count, :] = two_parts[3, 0:count, 32 * n : 32 * n + 32]
    for copy in copies + dcopies + sent:
        copy.wait_send()


def finish_kernel(*refs):
    copies = [pltpu.make_async_copy(refs[n], refs[4 + n], refs[8].at[n]) for n in range(4)]
    for copy in copies:
        copy.start()
    for copy in copies:
        copy.wait()


def body(volume_in, filter_one, filter_two, out_grad):
    hbm = pl.BlockSpec(memory_space=pltpu.HBM)
    vmem = pl.BlockSpec(memory_space=pltpu.VMEM)
    dma = pltpu.SemaphoreType.DMA
    shapes = [
        jax.ShapeDtypeStruct((32, CELLS), F32),
        jax.ShapeDtypeStruct((128, CELLS), F32),
        jax.ShapeDtypeStruct((16, 4, 27), F32),
        jax.ShapeDtypeStruct((432, 32), F32),
    ]
    operands = (
        volume_in.reshape(256, CELLS),
        jnp.transpose(filter_one, (1, 2, 0)).reshape(64, 27),
        jnp.transpose(filter_two, (0, 2, 1)).reshape(432, 32),
        out_grad.reshape(32, CELLS),
        jnp.asarray(constant_rows(), BF16),
        jnp.asarray(spread_matrix(), F32),
        jnp.asarray(collect_matrix(), BF16),
    )
    results = pl.pallas_call(
        level_kernel,
        out_shape=[pltpu.VMEM(shape.shape, F32) for shape in shapes],
        in_specs=[hbm] * 7,
        out_specs=[vmem] * 4,
        scratch_shapes=[
            pltpu.VMEM((256, CELLS), F32),
            pltpu.VMEM((64, 27), F32),
            pltpu.VMEM((432, 32), F32),
            pltpu.VMEM((32, CELLS), F32),
            pltpu.VMEM((5632, 384), BF16),
            pltpu.VMEM((27, 432), F32),
            pltpu.VMEM((432, 128), BF16),
            dma((8,)),
            pltpu.VMEM((3, 512, 128), F32),
            pltpu.VMEM((2000, 384), BF16),
            pltpu.VMEM((3, 432, 384), BF16),
            pltpu.VMEM((8, 16, 384), F32),
            pltpu.VMEM((2, 128, 128), F32),
            pltpu.VMEM((sum(IN_ROWS), 128), F32),
            pltpu.VMEM((sum(IN_ROWS), 128), F32),
            pltpu.VMEM((sum(D_ROWS), 128), F32),
            pltpu.VMEM((sum(D_ROWS), 128), F32),
            dma((7,)),
            dma((7,)),
            dma((7,)),
            dma((7,)),
            pltpu.VMEM((3, 16, 128), F32),
            pltpu.VMEM((3, 128, 128), F32),
            pltpu.VMEM((128, 128), F32),
            pltpu.VMEM((4, 128, 128), F32),
            pltpu.VMEM((3, 16, 128), F32),
            dma((7, 8)),
            dma((7, 8)),
        ],
        compiler_params=pltpu.CompilerParams(
            collective_id=0, has_side_effects=True, vmem_limit_bytes=40 * 2**20
        ),
    )(*(pltpu.with_memory_space_constraint(operand, pltpu.HBM) for operand in operands))
    level, hidden, grad_one, grad_two = pl.pallas_call(
        finish_kernel,
        out_shape=shapes,
        in_specs=[vmem] * 4,
        out_specs=[hbm] * 4,
        scratch_shapes=[dma((4,))],
        compiler_params=pltpu.CompilerParams(vmem_limit_bytes=40 * 2**20),
    )(*results)
    return (
        level.reshape(1, 1, 32, CELLS),
        hidden.reshape(1, 1, 16, 8, CELLS),
        jnp.transpose(grad_one, (2, 0, 1)),
        jnp.transpose(grad_two.reshape(27, 16, 32), (0, 2, 1)),
    )


def solution(mesh):
    placed = (P("dp", "space", None, None, None), P(), P(), P("dp", "space", None, None))
    return jax.shard_map(
        body,
        mesh=mesh,
        in_specs=placed,
        out_specs=(P("dp", "space", None, None), P("dp", "space", None, None, None), P(), P()),
        check_vma=False,
    )
```

```python
import itertools

import jax
import jax.numpy as jnp
import numpy as np
from jax import lax
from jax.experimental import pallas as pl
from jax.experimental.pallas import tpu as pltpu
from jax.sharding import PartitionSpec as P

SLOPE = 0.3
SIDE = 6
CELLS = SIDE**3
BF16 = jnp.bfloat16
F32 = jnp.float32
MESH = pl.DeviceIdType.MESH
HIGHEST = lax.Precision.HIGHEST

SUBSETS = [(0,), (1,), (2,), (0, 1), (0, 2), (1, 2), (0, 1, 2)]
SIZES = [SIDE ** (3 - len(s)) for s in SUBSETS]
STARTS = [sum(SIZES[:i]) for i in range(7)]


def rows_for(counts):
    rows = [8 * -(-tiles // (128 // size)) for tiles, size in zip(counts, SIZES)]
    return rows, [sum(rows[:i]) for i in range(7)]


IN_ROWS, IN_AT = rows_for([24, 24, 24, 32, 32, 32, 32])
D_ROWS, D_AT = rows_for([4] * 7)


def lane_of(coords, outside):
    dims = tuple(d for d in range(3) if coords[d] == outside)
    rest = [coords[d] for d in range(3) if d not in dims]
    place = 0
    for c in rest:
        place = place * SIDE + c
    return place if not dims else 256 + STARTS[SUBSETS.index(dims)] + place


def down_matrices():
    m = np.zeros((7, 384, 384), np.float32)
    for coords in itertools.product(range(-1, SIDE), repeat=3):
        for s, dims in enumerate(SUBSETS):
            source = [c - (d in dims) for d, c in enumerate(coords)]
            if all(coords[d] != -1 for d in dims):
                m[s, lane_of(source, -1), lane_of(coords, -1)] = 1
    return m


def up_matrices():
    m = np.zeros((7, 384, 384), np.float32)
    for coords in itertools.product(range(-1, SIDE), repeat=3):
        for s, dims in enumerate(SUBSETS):
            source = [c + (d in dims) for d, c in enumerate(coords)]
            if min(source) >= 0 and (min(coords) >= 0 or max(source) < SIDE):
                m[s, lane_of(source, SIDE), lane_of(coords, -1)] = 1
    return m


def pick_matrix(edge):
    m = np.zeros((256, 128), np.float32)
    for dims, start in zip(SUBSETS, STARTS):
        rest = [d for d in range(3) if d not in dims]
        for place, digits in enumerate(itertools.product(range(SIDE), repeat=len(rest))):
            coords = [edge] * 3
            for d, digit in zip(rest, digits):
                coords[d] = digit
            m[lane_of(coords, None), start + place] = 1
    return m


def spread_matrix():
    m = np.zeros((32, 432), np.float32)
    for k in range(27):
        m[k, 16 * k : 16 * k + 12] = 1
    return m


def constant_rows():
    picks = np.zeros((256, 384), np.float32)
    picks[:, 0:128] = pick_matrix(SIDE - 1)
    picks[:, 128:256] = pick_matrix(0)
    return np.concatenate([picks, *down_matrices(), *up_matrices()], axis=0)


def collect_matrix():
    m = np.zeros((432, 128), np.float32)
    for k in range(27):
        for c in range(4):
            m[16 * k + c, 32 * c + k] = 1
            m[16 * k + 4 + c, 32 * c + k] = 1
    return m


def iota(shape, dim):
    return lax.broadcasted_iota(jnp.int32, shape, dim)


def split(x, pieces):
    out = []
    for _ in range(pieces):
        piece = x.astype(BF16)
        out.append(piece)
        x = x - piece.astype(F32)
    return out


def dot(a, b, precision=None):
    return jnp.dot(a, b, preferred_element_type=F32, precision=precision)


def dot_t(a, b, precision=None):
    return lax.dot_general(a, b, (((1,), (1,)), ((), ())), preferred_element_type=F32, precision=precision)


def trimmed(tiles, d):
    weight = 4 >> d
    own = (iota((8, 128), 0) // weight) % 2 == 1
    other = 4 >> (d + 1) % 3
    out = []
    for t, tile in enumerate(tiles):
        if t & weight:
            out.append(tile)
        elif not t & other:
            out.append(jnp.where(own, tile, pltpu.roll(tiles[t | other], 8 - weight, 0)))
    return out


def trimmed_place(t, d):
    weight, other = 4 >> d, 4 >> (d + 1) % 3
    places = [n for n in range(32) if n & weight or not n & other]
    return (places.index(t), False) if t & weight else (places.index(t & ~other), bool(t & other))


def pack(tiles, buf, starts, trim=False):
    lane = iota((8, 128), 1)
    for s in range(7):
        size = SIZES[s]
        per = 128 // size
        these = trimmed(tiles, s) if trim and s < 3 else tiles
        for block in range(-(-len(these) // per)):
            total = jnp.zeros((8, 128), F32)
            for i, tile in enumerate(these[block * per : (block + 1) * per]):
                moved = pltpu.roll(tile, (i * size - STARTS[s]) % 128, 1)
                total = jnp.where((lane >= i * size) & (lane < (i + 1) * size), moved, total)
            buf[starts[s] + 8 * block : starts[s] + 8 * block + 8, :] = total


def halo_masks(valid):
    lane = iota((8, 128), 1)
    return [(lane >= STARTS[s]) & (lane < STARTS[s] + SIZES[s]) & (valid[s] > 0) for s in range(7)]


def unpack(t, buf, starts, masks, trim=False):
    total = jnp.zeros((8, 128), F32)
    for s in range(7):
        size = SIZES[s]
        per = 128 // size
        n, second = trimmed_place(t, s) if trim and s < 3 else (t, False)
        row = starts[s] + 8 * (n // per)
        moved = pltpu.roll(buf[row : row + 8, :], (STARTS[s] - (n % per) * size) % 128, 1)
        if second:
            moved = pltpu.roll(moved, 4 >> s, 0)
        total = jnp.where(masks[s], moved, total)
    return total


def cell(i, j, l):
    return 16 * (25 * i + 5 * j + l)


def offsets(k):
    return (k // 9, k // 3 % 3, k % 3)


def bits(q):
    return (q >> 2 & 1, q >> 1 & 1, q & 1)


def level_kernel(
    x_hbm, w1_hbm, w2_hbm, g_hbm, table_hbm, spread_hbm, collect_hbm,
    lev_ref, hid_ref, one_ref, two_ref,
    x_ref, w1_ref, w2_ref, g_ref, table, spread_ref, collect_ref, load_sem,
    xs, xc, xd, hk, pre, back, send, recv, dsend, drecv, send_sem, recv_sem, dsend_sem, drecv_sem,
    one_own, one_parts, two_own, two_parts, two_sum, sum_in, sum_out,
):
    dp, where = lax.axis_index("dp"), lax.axis_index("space")
    gx = lax.div(where, 16)
    rest = where - 16 * gx
    gy = lax.div(rest, 4)
    coords = (gx, gy, rest - 4 * gy)
    y = lax.div(rest, 2)
    core = rest - 2 * y

    def wrap(value, size):
        return jnp.where(value >= size, value - size, value)

    ups = [wrap(c + 1, 4) for c in coords]
    downs = [wrap(c + 3, 4) for c in coords]

    def neighbour(dims, step):
        moved = [(ups if step > 0 else downs)[d] if d in dims else coords[d] for d in range(3)]
        return {"space": moved[0] * 16 + moved[1] * 4 + moved[2]}

    def flags(edge):
        inside = [jnp.where(coords[d] == edge, 0, 1) for d in range(3)]
        out = []
        for dims in SUBSETS:
            flag = 1
            for d in dims:
                flag = flag * inside[d]
            out.append(flag)
        return out

    def load(n, src, dst):
        copy = pltpu.make_async_copy(src, dst, load_sem.at[n])
        copy.start()
        return copy

    load_x = load(0, x_hbm, x_ref)

    z_lo = lax.div(dp, 4)
    x_at, z_at = dp - 4 * z_lo, 2 * gx + z_lo
    xc_at = 2 * x_at + core
    xc_peers = []
    for j in (2, 1, 3, 0):
        p = wrap(x_at + j, 4)
        for c in (1 - core, core):
            xc_peers.append((2 * p + c, {"dp": 4 * z_lo + p, "space": 16 * gx + 2 * y + c}))
    xc_peers = xc_peers[:-1]
    y_peers = [(p, {"space": 16 * gx + 2 * p + core}) for p in (wrap(y + j, 8) for j in (4, 3, 5, 2, 6, 1, 7))]
    z_peers = []
    for j in (4, 3, 5, 2, 6, 1, 7):
        p = wrap(z_at + j, 8)
        high = lax.div(p, 2)
        z_peers.append((p, {"dp": 4 * (p - 2 * high) + x_at, "space": 16 * high + 2 * y + core}))

    barrier = pltpu.get_barrier_semaphore()
    for dims in SUBSETS[::-1]:
        for step in (-1, 1):
            pl.semaphore_signal(barrier, inc=1, device_id=neighbour(dims, step), device_id_type=MESH)
    for _, device in z_peers + y_peers + xc_peers:
        pl.semaphore_signal(barrier, inc=1, device_id=device, device_id_type=MESH)
    picks, shifts = pl.ds(0, 256), pl.ds(256, 5376)
    load_picks = load(1, table_hbm.at[picks], table.at[picks])
    loads = [
        load(2, w1_hbm, w1_ref),
        load(3, spread_hbm, spread_ref),
        load(4, w2_hbm, w2_ref),
        load(5, table_hbm.at[shifts], table.at[shifts]),
        load(6, g_hbm, g_ref),
        load(7, collect_hbm, collect_ref),
    ]


    def rows16(n):
        return pl.ds(pl.multiple_of(16 * n, 16), 16)

    sent = []

    def exchange(stage, me, peers, src, dst):
        def copy(j, to):
            p, device = peers[j]
            return pltpu.make_async_remote_copy(
                src_ref=src(p),
                dst_ref=dst(to),
                send_sem=sum_out.at[stage, j],
                recv_sem=sum_in.at[stage, to],
                device_id=device,
                device_id_type=MESH,
            )

        for j in range(7):
            sent.append(copy(j, me))
            sent[-1].start()

        def wait():
            for j in range(7):
                copy(j, peers[j][0]).wait_recv()

        return wait

    def sum_of(parts):
        parts = [parts[16 * n : 16 * n + 16, :] for n in range(8)]
        while len(parts) > 1:
            parts = [parts[n] + parts[n + 1] for n in range(0, len(parts), 2)]
        return parts[0]

    load_x.wait()
    load_picks.wait()
    pick = table[0:256, 0:128]
    x = jnp.concatenate([x_ref[...], jnp.zeros((256, 40), F32)], axis=1)
    pieces = split(x, 3)
    picked = dot(pieces[0], pick) + dot(pieces[1], pick) + dot(pieces[2], pick)
    pack([picked[8 * t : 8 * t + 8] for t in range(32)], send, IN_AT, True)
    pl.semaphore_wait(barrier, 35)
    copies = []
    for s, dims in reversed(list(enumerate(SUBSETS))):
        rows = pl.ds(IN_AT[s], IN_ROWS[s])
        copies.append(
            pltpu.make_async_remote_copy(
                src_ref=send.at[rows],
                dst_ref=recv.at[rows],
                send_sem=send_sem.at[s],
                recv_sem=recv_sem.at[s],
                device_id=neighbour(dims, 1),
                device_id_type=MESH,
            )
        )
        copies[-1].start()

    for copy in loads[0:3]:
        copy.wait()
    own_rows = (iota((16, 64), 1) // 4 == iota((16, 64), 0)).astype(BF16)
    own_lanes = iota((64, 432), 0) % 4 == iota((64, 432), 1) % 4
    wide = dot(jnp.concatenate(split(w1_ref[...], 3), axis=0), spread_ref[0:27, :])
    wide = [jnp.where(own_lanes, wide[64 * n : 64 * n + 64], 0.0).astype(BF16) for n in range(3)]
    w1a, w1b, w1c = [dot(own_rows, piece).astype(BF16) for piece in wide]
    slot = iota((16, 432), 1) // 4 % 4
    zero = jnp.zeros((16, 432), BF16)
    large = jnp.where(slot == 0, w1a, zero)
    middle = jnp.where(slot == 0, w1b, jnp.where(slot == 1, w1a, zero))
    least = jnp.where(slot == 0, w1c, jnp.where(slot == 1, w1b, jnp.where(slot == 2, w1a, zero)))
    one_lhs = jnp.concatenate([large, middle, least], axis=0)
    eye = (iota((32, 32), 0) == iota((32, 32), 1)).astype(BF16)
    two_lhs = jnp.concatenate([dot_t(eye, piece).astype(BF16) for piece in split(w2_ref[...], 3)], axis=0)
    back_rows = []
    for q in range(8):
        line = []
        for s in range(8):
            if s & ~q:
                line.append(jnp.zeros((16, 32), F32))
            else:
                k = 0
                for qb, sb in zip(bits(q), bits(s)):
                    k = 3 * k + (1 if qb == 0 else 0 if sb else 2)
                line.append(w2_ref[16 * k : 16 * k + 16, :])
        back_rows.append(jnp.concatenate(line, axis=1))
    back_lhs = jnp.concatenate(split(jnp.concatenate(back_rows, axis=0), 2), axis=0)

    for t in range(2):
        part = x[:, 128 * t : 128 * t + 128]
        xs[t, 0:256] = part
        xs[t, 256:512] = part
    upper = iota((8, 128), 0) < 4

    def gather(t):
        for g in range(64):
            index = [1 + 2 * (g >> (2 - d) & 1) + (g >> (5 - d) & 1) for d in range(3)]
            at = cell(*index)
            value = xs[t, pl.ds(g, 8, stride=64), :]
            hi, mid, lo = split(value, 3)
            first = jnp.where(upper, hi.astype(F32), mid.astype(F32))
            second = jnp.where(upper, lo.astype(F32), 0.0)
            xc[at : at + 16, 128 * t : 128 * t + 128] = jnp.concatenate([first, second], axis=0).astype(BF16)

    gather(0)
    gather(1)
    def down(s, first, last, lanes):
        return table[256 + 384 * s + first : 256 + 384 * s + last, 0:lanes]

    def up(s, first, last, lanes):
        return table[2944 + 384 * s + first : 2944 + 384 * s + last, 0:lanes]

    def shifted_cells(s):
        places = itertools.product(*[(4,) if d in SUBSETS[s] else range(1, 5) for d in range(3)])
        source = [cell(*place) for place in places]
        step = cell(*[4 if d in SUBSETS[s] else 0 for d in range(3)])
        return source, [at - step for at in source]

    for copy in loads[3:]:
        copy.wait()
    for s in range(7):
        source, target = shifted_cells(s)
        moved = dot(jnp.concatenate([xc[at : at + 16, 0:256] for at in source], axis=0), down(s, 0, 256, 256)).astype(BF16)
        for n, at in enumerate(target):
            xc[at : at + 16, 0:256] = moved[16 * n : 16 * n + 16]
    def stacked(q, first, last):
        b = bits(q)
        tiles = []
        for k in range(27):
            at = cell(*[2 * b[d] + offsets(k)[d] for d in range(3)])
            tiles.append(xc[at : at + 16, first:last])
        return jnp.concatenate(tiles, axis=0)

    def level_one(left, right):
        r = dot(left, right)
        return (r[32:48] + r[16:32]) + r[0:16]

    shifted, lefts = [], []
    for q in range(8):
        pre[q, :, 0:256] = level_one(one_lhs, stacked(q, 0, 256))
        shifted.append([k for k in range(27) if any(o == 0 and b == 0 for o, b in zip(offsets(k), bits(q)))])
        if shifted[q]:
            wide = one_lhs.astype(F32)
            left = jnp.concatenate([wide[:, 16 * k : 16 * k + 16] for k in shifted[q]], axis=1)
            lefts.append(left.astype(BF16))
    for copy in copies:
        copy.wait_recv()
    lower = halo_masks(flags(0))
    for t in range(32):
        tile = unpack(t, recv, IN_AT, lower, True)
        xs[2, 8 * t : 8 * t + 8] = tile
        xs[2, 256 + 8 * t : 264 + 8 * t] = tile
    gather(2)
    for s in range(7):
        source, target = shifted_cells(s)
        moved = dot(jnp.concatenate([xc[at : at + 16, 256:384] for at in source], axis=0), down(s, 256, 384, 384)).astype(BF16)
        for n, at in enumerate(target):
            xd[at : at + 16, :] = moved[16 * n : 16 * n + 16, 0:256]
            xc[at : at + 16, 256:384] = moved[16 * n : 16 * n + 16, 256:384]

    def three(k):
        return 16 * (9 * k[0] + 3 * k[1] + k[2])

    for q in range(8):
        value = pre[q, :, 0:256]
        if shifted[q]:
            tiles = []
            for k in shifted[q]:
                at = cell(*[2 * b + o for b, o in zip(bits(q), offsets(k))])
                tiles.append(xd[at : at + 16, :])
            value = value + level_one(lefts[q], jnp.concatenate(tiles, axis=0))
        edge = level_one(one_lhs, stacked(q, 256, 384)) if q else jnp.zeros((16, 128), F32)
        value = jnp.concatenate([value, edge], axis=1)
        pre[q] = value
        hidden = jnp.where(value > 0, value, SLOPE * value)
        at = three([1 + b for b in bits(q)])
        for n, piece in enumerate(split(hidden, 3)):
            hk[n, at : at + 16, :] = piece

    for s, dims in enumerate(SUBSETS):
        places = itertools.product(*[(2,) if d in dims else (1, 2) for d in range(3)])
        source = [three(place) for place in places]
        rows = jnp.concatenate([hk[n, at : at + 16, :] for n in range(3) for at in source], axis=0)
        moved = dot(rows, down(s, 0, 384, 256)).astype(BF16)
        step = three([2 if d in dims else 0 for d in range(3)])
        for n in range(3):
            for m, at in enumerate(source):
                row = 16 * (n * len(source) + m)
                hk[n, at - step : at - step + 16, 0:256] = moved[row : row + 16]

    r = [dot(two_lhs[:, 144 * n : 144 * n + 144], hk[0, 144 * n : 144 * n + 144, 0:256]) for n in range(3)]
    r = (r[0] + r[1]) + r[2]
    r2 = dot(two_lhs[0:64], hk[1, :, 0:256])
    r3 = dot(two_lhs[0:32], hk[2, :, 0:256])
    pre_two = ((r[64:96] + r2[32:64]) + r3 + (r[32:64] + r2[0:32])) + r[0:32]
    lev_ref[...] = jnp.where(pre_two > 0, pre_two, SLOPE * pre_two)[:, 0:CELLS]
    grad = jnp.concatenate([g_ref[...], jnp.zeros((32, 40), F32)], axis=1)
    delta = grad * jnp.where(pre_two > 0, 1.0, SLOPE)

    pieces = split(delta, 3)
    d1, d2 = pieces[0], pieces[1]
    r = dot_t(hk[0, :, 0:256], d1) + dot_t(hk[0, :, 0:256], d2) + dot_t(hk[1, :, 0:256], d1)
    r = jnp.concatenate([r, jnp.zeros((16, 32), F32)], axis=0)
    two_own[0:112, :] = jnp.concatenate([r[112 * n : 112 * n + 112] for n in range(4)], axis=1)
    two_own[112:128, :] = jnp.zeros((16, 128), F32)
    two_parts[0, rows16(xc_at), :] = two_own[rows16(xc_at), :]
    wait_two = exchange(0, xc_at, xc_peers, lambda p: two_own.at[rows16(p)], lambda p: two_parts.at[0, rows16(p)])

    for s in range(7):
        for at in shifted_cells(s)[1]:
            xc[at : at + 16, 0:256] += xd[at : at + 16, :]

    own = jnp.concatenate([d1, d2], axis=0)
    moved = [jnp.concatenate([own, jnp.zeros((64, 128), BF16)], axis=1)] * 8
    for s, dims in enumerate(SUBSETS):
        moved[sum(4 >> d for d in dims)] = dot(own, up(s, 0, 256, 384)).astype(BF16)

    def through_filter(moved):
        r = dot(back_lhs, jnp.concatenate([m[0:32] for m in moved], axis=0))
        low = dot(back_lhs[0:128], jnp.concatenate([m[32:64] for m in moved], axis=0))
        return (r[128:256] + low) + r[0:128]

    given = through_filter(moved)
    ones = []
    for q in range(8):
        value = given[16 * q : 16 * q + 16] * jnp.where(pre[q] > 0, 1.0, SLOPE)
        ones.append(jnp.concatenate(split(value, 2), axis=0))

    total = None
    for q in range(8):
        term = dot_t(stacked(q, 0, 256), ones[q][:, 0:256])
        total = term if total is None else total + term
    for pair in ((1, 2), (3, 4), (5, 6), (7,)):
        left = jnp.concatenate([stacked(q, 256, 384) for q in pair], axis=1)
        total = total + dot_t(left, jnp.concatenate([ones[q][:, 256:384] for q in pair], axis=1))
    def reduce_one(stage, me, peers):
        one_parts[stage, rows16(me), :] = one_own[stage]
        return exchange(
            4 + stage, me, peers, lambda p: one_own.at[stage], lambda p: one_parts.at[stage, rows16(p)]
        )

    def reduce_two(stage, me, peers):
        value = sum_of(two_parts.at[stage - 1])
        two_sum[stage - 1] = value
        two_parts[stage, rows16(me), :] = value
        return exchange(
            stage, me, peers, lambda p: two_sum.at[stage - 1], lambda p: two_parts.at[stage, rows16(p)]
        )

    wait_two()
    wait_two = reduce_two(1, y, y_peers)
    small = (iota((16, 32), 1) % 16 == iota((16, 32), 0)).astype(BF16)
    parts = [dot_t(small, piece) for piece in split(total, 3)]
    r = dot(jnp.concatenate(split((parts[2] + parts[1]) + parts[0], 3), axis=0), collect_ref[...])
    one_own[0] = (r[32:48] + r[16:32]) + r[0:16]

    wait_one = reduce_one(0, xc_at, xc_peers)

    r = dot(jnp.concatenate(pieces, axis=0), table[0:256, 128:256])
    picked = (r[0:32] + r[32:64]) + r[64:96]
    pack([picked[8 * t : 8 * t + 8] for t in range(4)], dsend, D_AT)
    dcopies = []
    for s, dims in reversed(list(enumerate(SUBSETS))):
        rows = pl.ds(D_AT[s], D_ROWS[s])
        dcopies.append(
            pltpu.make_async_remote_copy(
                src_ref=dsend.at[rows],
                dst_ref=drecv.at[rows],
                send_sem=dsend_sem.at[s],
                recv_sem=drecv_sem.at[s],
                device_id=neighbour(dims, -1),
                device_id_type=MESH,
            )
        )
        dcopies[-1].start()

    wait_one()
    one_own[1] = sum_of(one_parts.at[0])
    wait_one = reduce_one(1, y, y_peers)
    wait_two()
    wait_two = reduce_two(2, z_at, z_peers)
    wait_one()
    one_own[2] = sum_of(one_parts.at[1])
    wait_one = reduce_one(2, z_at, z_peers)

    for copy in dcopies:
        copy.wait_recv()
    higher = halo_masks(flags(3))
    halo = jnp.concatenate([unpack(t, drecv, D_AT, higher) for t in range(4)], axis=0)
    halo = jnp.concatenate(split(halo, 2), axis=0)
    moved = [jnp.zeros((64, 256), BF16)] * 8
    for s, dims in enumerate(SUBSETS):
        moved[sum(4 >> d for d in dims)] = dot(halo, up(s, 256, 384, 256)).astype(BF16)
    value = given[:, 0:256] + through_filter(moved)
    for q in range(8):
        for t in range(2):
            back[t, pl.ds(q, 16, stride=8), :] = value[16 * q : 16 * q + 16, 128 * t : 128 * t + 128]
    hid_ref[...] = jnp.concatenate([back[0], back[1]], axis=1)[:, 0:CELLS]

    wait_two()
    wait_two = reduce_two(3, xc_at, xc_peers)
    wait_one()
    value = sum_of(one_parts.at[2])
    for c in range(4):
        one_ref[:, c, :] = value[:, 32 * c : 32 * c + 27]
    wait_two()
    for n in range(4):
        count = 16 * min(7, 27 - 7 * n)
        two_ref[112 * n : 112 * n + count, :] = two_parts[3, 0:count, 32 * n : 32 * n + 32]
    for copy in copies + dcopies + sent:
        copy.wait_send()


def finish_kernel(*refs):
    copies = [pltpu.make_async_copy(refs[n], refs[4 + n], refs[8].at[n]) for n in range(4)]
    for copy in copies:
        copy.start()
    for copy in copies:
        copy.wait()


def body(volume_in, filter_one, filter_two, out_grad):
    hbm = pl.BlockSpec(memory_space=pltpu.HBM)
    vmem = pl.BlockSpec(memory_space=pltpu.VMEM)
    dma = pltpu.SemaphoreType.DMA
    shapes = [
        jax.ShapeDtypeStruct((32, CELLS), F32),
        jax.ShapeDtypeStruct((128, CELLS), F32),
        jax.ShapeDtypeStruct((16, 4, 27), F32),
        jax.ShapeDtypeStruct((432, 32), F32),
    ]
    operands = (
        volume_in.reshape(256, CELLS),
        jnp.transpose(filter_one, (1, 2, 0)).reshape(64, 27),
        jnp.transpose(filter_two, (0, 2, 1)).reshape(432, 32),
        out_grad.reshape(32, CELLS),
        jnp.asarray(constant_rows(), BF16),
        jnp.asarray(spread_matrix(), BF16),
        jnp.asarray(collect_matrix(), BF16),
    )
    results = pl.pallas_call(
        level_kernel,
        out_shape=[pltpu.VMEM(shape.shape, F32) for shape in shapes],
        in_specs=[hbm] * 7,
        out_specs=[vmem] * 4,
        scratch_shapes=[
            pltpu.VMEM((256, CELLS), F32),
            pltpu.VMEM((64, 27), F32),
            pltpu.VMEM((432, 32), F32),
            pltpu.VMEM((32, CELLS), F32),
            pltpu.VMEM((5632, 384), BF16),
            pltpu.VMEM((32, 432), BF16),
            pltpu.VMEM((432, 128), BF16),
            dma((8,)),
            pltpu.VMEM((3, 512, 128), F32),
            pltpu.VMEM((2000, 384), BF16),
            pltpu.VMEM((2000, 256), BF16),
            pltpu.VMEM((3, 432, 384), BF16),
            pltpu.VMEM((8, 16, 384), F32),
            pltpu.VMEM((2, 128, 128), F32),
            pltpu.VMEM((sum(IN_ROWS), 128), F32),
            pltpu.VMEM((sum(IN_ROWS), 128), F32),
            pltpu.VMEM((sum(D_ROWS), 128), F32),
            pltpu.VMEM((sum(D_ROWS), 128), F32),
            dma((7,)),
            dma((7,)),
            dma((7,)),
            dma((7,)),
            pltpu.VMEM((3, 16, 128), F32),
            pltpu.VMEM((3, 128, 128), F32),
            pltpu.VMEM((128, 128), F32),
            pltpu.VMEM((4, 128, 128), F32),
            pltpu.VMEM((3, 16, 128), F32),
            dma((7, 8)),
            dma((7, 8)),
        ],
        compiler_params=pltpu.CompilerParams(
            collective_id=0, has_side_effects=True, vmem_limit_bytes=40 * 2**20
        ),
    )(*(pltpu.with_memory_space_constraint(operand, pltpu.HBM) for operand in operands))
    level, hidden, grad_one, grad_two = pl.pallas_call(
        finish_kernel,
        out_shape=shapes,
        in_specs=[vmem] * 4,
        out_specs=[hbm] * 4,
        scratch_shapes=[dma((4,))],
        compiler_params=pltpu.CompilerParams(vmem_limit_bytes=40 * 2**20),
    )(*results)
    return (
        level.reshape(1, 1, 32, CELLS),
        hidden.reshape(1, 1, 16, 8, CELLS),
        jnp.transpose(grad_one, (2, 0, 1)),
        jnp.transpose(grad_two.reshape(27, 16, 32), (0, 2, 1)),
    )


def solution(mesh):
    placed = (P("dp", "space", None, None, None), P(), P(), P("dp", "space", None, None))
    return jax.shard_map(
        body,
        mesh=mesh,
        in_specs=placed,
        out_specs=(P("dp", "space", None, None), P("dp", "space", None, None, None), P(), P()),
        check_vma=False,
    )
```

```python
import itertools

import jax
import jax.numpy as jnp
import numpy as np
from jax import lax
from jax.experimental import pallas as pl
from jax.experimental.pallas import tpu as pltpu
from jax.sharding import PartitionSpec as P

SLOPE = 0.3
SIDE = 6
CELLS = SIDE**3
BF16 = jnp.bfloat16
F32 = jnp.float32
MESH = pl.DeviceIdType.MESH
HIGHEST = lax.Precision.HIGHEST

SUBSETS = [(0,), (1,), (2,), (0, 1), (0, 2), (1, 2), (0, 1, 2)]
SIZES = [SIDE ** (3 - len(s)) for s in SUBSETS]
STARTS = [sum(SIZES[:i]) for i in range(7)]


def rows_for(counts):
    rows = [8 * -(-tiles // (128 // size)) for tiles, size in zip(counts, SIZES)]
    return rows, [sum(rows[:i]) for i in range(7)]


IN_ROWS, IN_AT = rows_for([24, 24, 24, 32, 32, 32, 32])
D_ROWS, D_AT = rows_for([4] * 7)


def lane_of(coords, outside):
    dims = tuple(d for d in range(3) if coords[d] == outside)
    rest = [coords[d] for d in range(3) if d not in dims]
    place = 0
    for c in rest:
        place = place * SIDE + c
    return place if not dims else 256 + STARTS[SUBSETS.index(dims)] + place


def down_matrices():
    m = np.zeros((7, 384, 384), np.float32)
    for coords in itertools.product(range(-1, SIDE), repeat=3):
        for s, dims in enumerate(SUBSETS):
            source = [c - (d in dims) for d, c in enumerate(coords)]
            if all(coords[d] != -1 for d in dims):
                m[s, lane_of(source, -1), lane_of(coords, -1)] = 1
    return m


def up_matrices():
    m = np.zeros((7, 384, 384), np.float32)
    for coords in itertools.product(range(-1, SIDE), repeat=3):
        for s, dims in enumerate(SUBSETS):
            source = [c + (d in dims) for d, c in enumerate(coords)]
            if min(source) >= 0 and (min(coords) >= 0 or max(source) < SIDE):
                m[s, lane_of(source, SIDE), lane_of(coords, -1)] = 1
    return m


def pick_matrix(edge):
    m = np.zeros((256, 128), np.float32)
    for dims, start in zip(SUBSETS, STARTS):
        rest = [d for d in range(3) if d not in dims]
        for place, digits in enumerate(itertools.product(range(SIDE), repeat=len(rest))):
            coords = [edge] * 3
            for d, digit in zip(rest, digits):
                coords[d] = digit
            m[lane_of(coords, None), start + place] = 1
    return m


def spread_matrix():
    m = np.zeros((32, 432), np.float32)
    for k in range(27):
        m[k, 16 * k : 16 * k + 12] = 1
    return m


def constant_rows():
    picks = np.zeros((256, 384), np.float32)
    picks[:, 0:128] = pick_matrix(SIDE - 1)
    picks[:, 128:256] = pick_matrix(0)
    return np.concatenate([picks, *down_matrices(), *up_matrices()], axis=0)


def collect_matrix():
    m = np.zeros((432, 128), np.float32)
    for k in range(27):
        for c in range(4):
            m[16 * k + c, 32 * c + k] = 1
            m[16 * k + 4 + c, 32 * c + k] = 1
    return m


def iota(shape, dim):
    return lax.broadcasted_iota(jnp.int32, shape, dim)


def split(x, pieces):
    out = []
    for _ in range(pieces):
        piece = x.astype(BF16)
        out.append(piece)
        x = x - piece.astype(F32)
    return out


def dot(a, b, precision=None):
    return jnp.dot(a, b, preferred_element_type=F32, precision=precision)


def dot_t(a, b, precision=None):
    return lax.dot_general(a, b, (((1,), (1,)), ((), ())), preferred_element_type=F32, precision=precision)


def trimmed(tiles, d):
    weight = 4 >> d
    own = (iota((8, 128), 0) // weight) % 2 == 1
    other = 4 >> (d + 1) % 3
    out = []
    for t, tile in enumerate(tiles):
        if t & weight:
            out.append(tile)
        elif not t & other:
            out.append(jnp.where(own, tile, pltpu.roll(tiles[t | other], 8 - weight, 0)))
    return out


def trimmed_place(t, d):
    weight, other = 4 >> d, 4 >> (d + 1) % 3
    places = [n for n in range(32) if n & weight or not n & other]
    return (places.index(t), False) if t & weight else (places.index(t & ~other), bool(t & other))


def pack(tiles, buf, starts, trim=False):
    lane = iota((8, 128), 1)
    for s in range(7):
        size = SIZES[s]
        per = 128 // size
        these = trimmed(tiles, s) if trim and s < 3 else tiles
        for block in range(-(-len(these) // per)):
            total = jnp.zeros((8, 128), F32)
            for i, tile in enumerate(these[block * per : (block + 1) * per]):
                moved = pltpu.roll(tile, (i * size - STARTS[s]) % 128, 1)
                total = jnp.where((lane >= i * size) & (lane < (i + 1) * size), moved, total)
            buf[starts[s] + 8 * block : starts[s] + 8 * block + 8, :] = total


def halo_masks(valid):
    lane = iota((8, 128), 1)
    return [(lane >= STARTS[s]) & (lane < STARTS[s] + SIZES[s]) & (valid[s] > 0) for s in range(7)]


def unpack(t, buf, starts, masks, trim=False):
    total = jnp.zeros((8, 128), F32)
    for s in range(7):
        size = SIZES[s]
        per = 128 // size
        n, second = trimmed_place(t, s) if trim and s < 3 else (t, False)
        row = starts[s] + 8 * (n // per)
        moved = pltpu.roll(buf[row : row + 8, :], (STARTS[s] - (n % per) * size) % 128, 1)
        if second:
            moved = pltpu.roll(moved, 4 >> s, 0)
        total = jnp.where(masks[s], moved, total)
    return total


def cell(i, j, l):
    return 16 * (25 * i + 5 * j + l)


def offsets(k):
    return (k // 9, k // 3 % 3, k % 3)


def bits(q):
    return (q >> 2 & 1, q >> 1 & 1, q & 1)


def level_kernel(
    x_hbm, w1_hbm, w2_hbm, g_hbm, table_hbm, spread_hbm, collect_hbm,
    lev_ref, hid_ref, one_ref, two_ref,
    x_ref, w1_ref, w2_ref, g_ref, table, spread_ref, collect_ref, load_sem,
    xs, xc, xd, hk, pre, back, send, recv, dsend, drecv, send_sem, recv_sem, dsend_sem, drecv_sem,
    one_own, one_parts, two_own, two_parts, two_sum, sum_in, sum_out,
):
    dp, where = lax.axis_index("dp"), lax.axis_index("space")
    gx = lax.div(where, 16)
    rest = where - 16 * gx
    gy = lax.div(rest, 4)
    coords = (gx, gy, rest - 4 * gy)
    y = lax.div(rest, 2)
    core = rest - 2 * y

    def wrap(value, size):
        return jnp.where(value >= size, value - size, value)

    ups = [wrap(c + 1, 4) for c in coords]
    downs = [wrap(c + 3, 4) for c in coords]

    def neighbour(dims, step):
        moved = [(ups if step > 0 else downs)[d] if d in dims else coords[d] for d in range(3)]
        return {"space": moved[0] * 16 + moved[1] * 4 + moved[2]}

    def flags(edge):
        inside = [jnp.where(coords[d] == edge, 0, 1) for d in range(3)]
        out = []
        for dims in SUBSETS:
            flag = 1
            for d in dims:
                flag = flag * inside[d]
            out.append(flag)
        return out

    def load(n, src, dst):
        copy = pltpu.make_async_copy(src, dst, load_sem.at[n])
        copy.start()
        return copy

    load_x = load(0, x_hbm, x_ref)

    z_lo = lax.div(dp, 4)
    x_at, z_at = dp - 4 * z_lo, 2 * gx + z_lo
    xc_at = 2 * x_at + core
    xc_peers = []
    for j in (2, 1, 3, 0):
        p = wrap(x_at + j, 4)
        for c in (1 - core, core):
            xc_peers.append((2 * p + c, {"dp": 4 * z_lo + p, "space": 16 * gx + 2 * y + c}))
    xc_peers = xc_peers[:-1]
    y_peers = [(p, {"space": 16 * gx + 2 * p + core}) for p in (wrap(y + j, 8) for j in (4, 3, 5, 2, 6, 1, 7))]
    z_peers = []
    for j in (4, 3, 5, 2, 6, 1, 7):
        p = wrap(z_at + j, 8)
        high = lax.div(p, 2)
        z_peers.append((p, {"dp": 4 * (p - 2 * high) + x_at, "space": 16 * high + 2 * y + core}))

    barrier = pltpu.get_barrier_semaphore()
    for dims in SUBSETS[::-1]:
        for step in (-1, 1):
            pl.semaphore_signal(barrier, inc=1, device_id=neighbour(dims, step), device_id_type=MESH)
    for _, device in z_peers[1:3] + z_peers[5:7] + xc_peers[:-1]:
        pl.semaphore_signal(barrier, inc=1, device_id=device, device_id_type=MESH)
    picks, shifts = pl.ds(0, 256), pl.ds(256, 5376)
    load_picks = load(1, table_hbm.at[picks], table.at[picks])
    loads = [
        load(2, w1_hbm, w1_ref),
        load(3, spread_hbm, spread_ref),
        load(4, w2_hbm, w2_ref),
        load(5, table_hbm.at[shifts], table.at[shifts]),
        load(6, g_hbm, g_ref),
        load(7, collect_hbm, collect_ref),
    ]


    def rows16(n):
        return pl.ds(pl.multiple_of(16 * n, 16), 16)

    sent = []

    def exchange(stage, me, peers, src, dst):
        def copy(j, to):
            p, device = peers[j]
            return pltpu.make_async_remote_copy(
                src_ref=src(p),
                dst_ref=dst(to),
                send_sem=sum_out.at[stage, j],
                recv_sem=sum_in.at[stage, to],
                device_id=device,
                device_id_type=MESH,
            )

        for j in range(7):
            sent.append(copy(j, me))
            sent[-1].start()

        def wait():
            for j in range(7):
                copy(j, peers[j][0]).wait_recv()

        return wait

    def sum_of(parts):
        parts = [parts[16 * n : 16 * n + 16, :] for n in range(8)]
        while len(parts) > 1:
            parts = [parts[n] + parts[n + 1] for n in range(0, len(parts), 2)]
        return parts[0]

    load_x.wait()
    load_picks.wait()
    pick = table[0:256, 0:128]
    x = jnp.concatenate([x_ref[...], jnp.zeros((256, 40), F32)], axis=1)
    pieces = split(x, 3)
    picked = dot(pieces[0], pick) + dot(pieces[1], pick) + dot(pieces[2], pick)
    pack([picked[8 * t : 8 * t + 8] for t in range(32)], send, IN_AT, True)
    pl.semaphore_wait(barrier, 24)
    copies = []
    for s, dims in reversed(list(enumerate(SUBSETS))):
        rows = pl.ds(IN_AT[s], IN_ROWS[s])
        copies.append(
            pltpu.make_async_remote_copy(
                src_ref=send.at[rows],
                dst_ref=recv.at[rows],
                send_sem=send_sem.at[s],
                recv_sem=recv_sem.at[s],
                device_id=neighbour(dims, 1),
                device_id_type=MESH,
            )
        )
        copies[-1].start()

    for copy in loads[0:3]:
        copy.wait()
    own_rows = (iota((16, 64), 1) // 4 == iota((16, 64), 0)).astype(BF16)
    own_lanes = iota((64, 432), 0) % 4 == iota((64, 432), 1) % 4
    wide = dot(jnp.concatenate(split(w1_ref[...], 3), axis=0), spread_ref[0:27, :])
    wide = [jnp.where(own_lanes, wide[64 * n : 64 * n + 64], 0.0).astype(BF16) for n in range(3)]
    w1a, w1b, w1c = [dot(own_rows, piece).astype(BF16) for piece in wide]
    slot = iota((16, 432), 1) // 4 % 4
    zero = jnp.zeros((16, 432), BF16)
    large = jnp.where(slot == 0, w1a, zero)
    middle = jnp.where(slot == 0, w1b, jnp.where(slot == 1, w1a, zero))
    least = jnp.where(slot == 0, w1c, jnp.where(slot == 1, w1b, jnp.where(slot == 2, w1a, zero)))
    one_lhs = jnp.concatenate([large, middle, least], axis=0)
    eye = (iota((32, 32), 0) == iota((32, 32), 1)).astype(BF16)
    two_lhs = jnp.concatenate([dot_t(eye, piece).astype(BF16) for piece in split(w2_ref[...], 3)], axis=0)
    back_rows = []
    for q in range(8):
        line = []
        for s in range(8):
            if s & ~q:
                line.append(jnp.zeros((16, 32), F32))
            else:
                k = 0
                for qb, sb in zip(bits(q), bits(s)):
                    k = 3 * k + (1 if qb == 0 else 0 if sb else 2)
                line.append(w2_ref[16 * k : 16 * k + 16, :])
        back_rows.append(jnp.concatenate(line, axis=1))
    back_lhs = jnp.concatenate(split(jnp.concatenate(back_rows, axis=0), 2), axis=0)

    for t in range(2):
        part = x[:, 128 * t : 128 * t + 128]
        xs[t, 0:256] = part
        xs[t, 256:512] = part
    upper = iota((8, 128), 0) < 4

    def gather(t):
        for g in range(64):
            index = [1 + 2 * (g >> (2 - d) & 1) + (g >> (5 - d) & 1) for d in range(3)]
            at = cell(*index)
            value = xs[t, pl.ds(g, 8, stride=64), :]
            hi, mid, lo = split(value, 3)
            first = jnp.where(upper, hi.astype(F32), mid.astype(F32))
            second = jnp.where(upper, lo.astype(F32), 0.0)
            xc[at : at + 16, 128 * t : 128 * t + 128] = jnp.concatenate([first, second], axis=0).astype(BF16)

    gather(0)
    gather(1)
    def down(s, first, last, lanes):
        return table[256 + 384 * s + first : 256 + 384 * s + last, 0:lanes]

    def up(s, first, last, lanes):
        return table[2944 + 384 * s + first : 2944 + 384 * s + last, 0:lanes]

    def shifted_cells(s):
        places = itertools.product(*[(4,) if d in SUBSETS[s] else range(1, 5) for d in range(3)])
        source = [cell(*place) for place in places]
        step = cell(*[4 if d in SUBSETS[s] else 0 for d in range(3)])
        return source, [at - step for at in source]

    for copy in loads[3:]:
        copy.wait()
    for s in range(7):
        source, target = shifted_cells(s)
        moved = dot(jnp.concatenate([xc[at : at + 16, 0:256] for at in source], axis=0), down(s, 0, 256, 256)).astype(BF16)
        for n, at in enumerate(target):
            xc[at : at + 16, 0:256] = moved[16 * n : 16 * n + 16]
    def stacked(q, first, last):
        b = bits(q)
        tiles = []
        for k in range(27):
            at = cell(*[2 * b[d] + offsets(k)[d] for d in range(3)])
            tiles.append(xc[at : at + 16, first:last])
        return jnp.concatenate(tiles, axis=0)

    def level_one(left, right):
        r = dot(left, right)
        return (r[32:48] + r[16:32]) + r[0:16]

    shifted, lefts = [], []
    for q in range(8):
        pre[q, :, 0:256] = level_one(one_lhs, stacked(q, 0, 256))
        shifted.append([k for k in range(27) if any(o == 0 and b == 0 for o, b in zip(offsets(k), bits(q)))])
        if shifted[q]:
            wide = one_lhs.astype(F32)
            left = jnp.concatenate([wide[:, 16 * k : 16 * k + 16] for k in shifted[q]], axis=1)
            lefts.append(left.astype(BF16))
    for copy in copies:
        copy.wait_recv()
    lower = halo_masks(flags(0))
    for t in range(32):
        tile = unpack(t, recv, IN_AT, lower, True)
        xs[2, 8 * t : 8 * t + 8] = tile
        xs[2, 256 + 8 * t : 264 + 8 * t] = tile
    gather(2)
    for s in range(7):
        source, target = shifted_cells(s)
        moved = dot(jnp.concatenate([xc[at : at + 16, 256:384] for at in source], axis=0), down(s, 256, 384, 384)).astype(BF16)
        for n, at in enumerate(target):
            xd[at : at + 16, :] = moved[16 * n : 16 * n + 16, 0:256]
            xc[at : at + 16, 256:384] = moved[16 * n : 16 * n + 16, 256:384]

    def three(k):
        return 16 * (9 * k[0] + 3 * k[1] + k[2])

    for q in range(8):
        value = pre[q, :, 0:256]
        if shifted[q]:
            tiles = []
            for k in shifted[q]:
                at = cell(*[2 * b + o for b, o in zip(bits(q), offsets(k))])
                tiles.append(xd[at : at + 16, :])
            value = value + level_one(lefts[q], jnp.concatenate(tiles, axis=0))
        edge = level_one(one_lhs, stacked(q, 256, 384)) if q else jnp.zeros((16, 128), F32)
        value = jnp.concatenate([value, edge], axis=1)
        pre[q] = value
        hidden = jnp.where(value > 0, value, SLOPE * value)
        at = three([1 + b for b in bits(q)])
        for n, piece in enumerate(split(hidden, 3)):
            hk[n, at : at + 16, :] = piece

    for s, dims in enumerate(SUBSETS):
        places = itertools.product(*[(2,) if d in dims else (1, 2) for d in range(3)])
        source = [three(place) for place in places]
        rows = jnp.concatenate([hk[n, at : at + 16, :] for n in range(3) for at in source], axis=0)
        moved = dot(rows, down(s, 0, 384, 256)).astype(BF16)
        step = three([2 if d in dims else 0 for d in range(3)])
        for n in range(3):
            for m, at in enumerate(source):
                row = 16 * (n * len(source) + m)
                hk[n, at - step : at - step + 16, 0:256] = moved[row : row + 16]

    r = [dot(two_lhs[:, 144 * n : 144 * n + 144], hk[0, 144 * n : 144 * n + 144, 0:256]) for n in range(3)]
    r = (r[0] + r[1]) + r[2]
    r2 = dot(two_lhs[0:64], hk[1, :, 0:256])
    r3 = dot(two_lhs[0:32], hk[2, :, 0:256])
    pre_two = ((r[64:96] + r2[32:64]) + r3 + (r[32:64] + r2[0:32])) + r[0:32]
    lev_ref[...] = jnp.where(pre_two > 0, pre_two, SLOPE * pre_two)[:, 0:CELLS]
    grad = jnp.concatenate([g_ref[...], jnp.zeros((32, 40), F32)], axis=1)
    delta = grad * jnp.where(pre_two > 0, 1.0, SLOPE)

    pieces = split(delta, 3)
    d1, d2 = pieces[0], pieces[1]
    r = dot_t(hk[0, :, 0:256], d1) + dot_t(hk[0, :, 0:256], d2) + dot_t(hk[1, :, 0:256], d1)
    r = jnp.concatenate([r, jnp.zeros((16, 32), F32)], axis=0)
    two_own[0:112, :] = jnp.concatenate([r[112 * n : 112 * n + 112] for n in range(4)], axis=1)
    two_own[112:128, :] = jnp.zeros((16, 128), F32)
    two_parts[0, rows16(xc_at), :] = two_own[rows16(xc_at), :]
    wait_two = exchange(0, xc_at, xc_peers, lambda p: two_own.at[rows16(p)], lambda p: two_parts.at[0, rows16(p)])

    for s in range(7):
        for at in shifted_cells(s)[1]:
            xc[at : at + 16, 0:256] += xd[at : at + 16, :]

    own = jnp.concatenate([d1, d2], axis=0)
    moved = [jnp.concatenate([own, jnp.zeros((64, 128), BF16)], axis=1)] * 8
    for s, dims in enumerate(SUBSETS):
        moved[sum(4 >> d for d in dims)] = dot(own, up(s, 0, 256, 384)).astype(BF16)

    def through_filter(moved):
        r = dot(back_lhs, jnp.concatenate([m[0:32] for m in moved], axis=0))
        low = dot(back_lhs[0:128], jnp.concatenate([m[32:64] for m in moved], axis=0))
        return (r[128:256] + low) + r[0:128]

    given = through_filter(moved)
    ones = []
    for q in range(8):
        value = given[16 * q : 16 * q + 16] * jnp.where(pre[q] > 0, 1.0, SLOPE)
        ones.append(jnp.concatenate(split(value, 2), axis=0))

    total = None
    for q in range(8):
        term = dot_t(stacked(q, 0, 256), ones[q][:, 0:256])
        total = term if total is None else total + term
    for pair in ((1, 2), (3, 4), (5, 6), (7,)):
        left = jnp.concatenate([stacked(q, 256, 384) for q in pair], axis=1)
        total = total + dot_t(left, jnp.concatenate([ones[q][:, 256:384] for q in pair], axis=1))
    def reduce_one(stage, me, peers):
        one_parts[stage, rows16(me), :] = one_own[stage]
        return exchange(
            4 + stage, me, peers, lambda p: one_own.at[stage], lambda p: one_parts.at[stage, rows16(p)]
        )

    def reduce_two(stage, me, peers):
        value = sum_of(two_parts.at[stage - 1])
        two_sum[stage - 1] = value
        two_parts[stage, rows16(me), :] = value
        return exchange(
            stage, me, peers, lambda p: two_sum.at[stage - 1], lambda p: two_parts.at[stage, rows16(p)]
        )

    wait_two()
    wait_two = reduce_two(1, y, y_peers)
    small = (iota((16, 32), 1) % 16 == iota((16, 32), 0)).astype(BF16)
    parts = [dot_t(small, piece) for piece in split(total, 3)]
    r = dot(jnp.concatenate(split((parts[2] + parts[1]) + parts[0], 3), axis=0), collect_ref[...])
    one_own[0] = (r[32:48] + r[16:32]) + r[0:16]

    wait_one = reduce_one(0, xc_at, xc_peers)

    r = dot(jnp.concatenate(pieces, axis=0), table[0:256, 128:256])
    picked = (r[0:32] + r[32:64]) + r[64:96]
    pack([picked[8 * t : 8 * t + 8] for t in range(4)], dsend, D_AT)
    dcopies = []
    for s, dims in reversed(list(enumerate(SUBSETS))):
        rows = pl.ds(D_AT[s], D_ROWS[s])
        dcopies.append(
            pltpu.make_async_remote_copy(
                src_ref=dsend.at[rows],
                dst_ref=drecv.at[rows],
                send_sem=dsend_sem.at[s],
                recv_sem=drecv_sem.at[s],
                device_id=neighbour(dims, -1),
                device_id_type=MESH,
            )
        )
        dcopies[-1].start()

    wait_one()
    one_own[1] = sum_of(one_parts.at[0])
    wait_one = reduce_one(1, y, y_peers)
    wait_two()
    wait_two = reduce_two(2, z_at, z_peers)
    wait_one()
    one_own[2] = sum_of(one_parts.at[1])
    wait_one = reduce_one(2, z_at, z_peers)

    for copy in dcopies:
        copy.wait_recv()
    higher = halo_masks(flags(3))
    halo = jnp.concatenate([unpack(t, drecv, D_AT, higher) for t in range(4)], axis=0)
    halo = jnp.concatenate(split(halo, 2), axis=0)
    moved = [jnp.zeros((64, 256), BF16)] * 8
    for s, dims in enumerate(SUBSETS):
        moved[sum(4 >> d for d in dims)] = dot(halo, up(s, 256, 384, 256)).astype(BF16)
    value = given[:, 0:256] + through_filter(moved)
    for q in range(8):
        for t in range(2):
            back[t, pl.ds(q, 16, stride=8), :] = value[16 * q : 16 * q + 16, 128 * t : 128 * t + 128]
    hid_ref[...] = jnp.concatenate([back[0], back[1]], axis=1)[:, 0:CELLS]

    wait_two()
    wait_two = reduce_two(3, xc_at, xc_peers)
    wait_one()
    value = sum_of(one_parts.at[2])
    for c in range(4):
        one_ref[:, c, :] = value[:, 32 * c : 32 * c + 27]
    wait_two()
    for n in range(4):
        count = 16 * min(7, 27 - 7 * n)
        two_ref[112 * n : 112 * n + count, :] = two_parts[3, 0:count, 32 * n : 32 * n + 32]
    for copy in copies + dcopies + sent:
        copy.wait_send()


def finish_kernel(*refs):
    copies = [pltpu.make_async_copy(refs[n], refs[4 + n], refs[8].at[n]) for n in range(4)]
    for copy in copies:
        copy.start()
    for copy in copies:
        copy.wait()


def body(volume_in, filter_one, filter_two, out_grad):
    hbm = pl.BlockSpec(memory_space=pltpu.HBM)
    vmem = pl.BlockSpec(memory_space=pltpu.VMEM)
    dma = pltpu.SemaphoreType.DMA
    shapes = [
        jax.ShapeDtypeStruct((32, CELLS), F32),
        jax.ShapeDtypeStruct((128, CELLS), F32),
        jax.ShapeDtypeStruct((16, 4, 27), F32),
        jax.ShapeDtypeStruct((432, 32), F32),
    ]
    operands = (
        volume_in.reshape(256, CELLS),
        jnp.transpose(filter_one, (1, 2, 0)).reshape(64, 27),
        jnp.transpose(filter_two, (0, 2, 1)).reshape(432, 32),
        out_grad.reshape(32, CELLS),
        jnp.asarray(constant_rows(), BF16),
        jnp.asarray(spread_matrix(), BF16),
        jnp.asarray(collect_matrix(), BF16),
    )
    results = pl.pallas_call(
        level_kernel,
        out_shape=[pltpu.VMEM(shape.shape, F32) for shape in shapes],
        in_specs=[hbm] * 7,
        out_specs=[vmem] * 4,
        scratch_shapes=[
            pltpu.VMEM((256, CELLS), F32),
            pltpu.VMEM((64, 27), F32),
            pltpu.VMEM((432, 32), F32),
            pltpu.VMEM((32, CELLS), F32),
            pltpu.VMEM((5632, 384), BF16),
            pltpu.VMEM((32, 432), BF16),
            pltpu.VMEM((432, 128), BF16),
            dma((8,)),
            pltpu.VMEM((3, 512, 128), F32),
            pltpu.VMEM((2000, 384), BF16),
            pltpu.VMEM((2000, 256), BF16),
            pltpu.VMEM((3, 432, 384), BF16),
            pltpu.VMEM((8, 16, 384), F32),
            pltpu.VMEM((2, 128, 128), F32),
            pltpu.VMEM((sum(IN_ROWS), 128), F32),
            pltpu.VMEM((sum(IN_ROWS), 128), F32),
            pltpu.VMEM((sum(D_ROWS), 128), F32),
            pltpu.VMEM((sum(D_ROWS), 128), F32),
            dma((7,)),
            dma((7,)),
            dma((7,)),
            dma((7,)),
            pltpu.VMEM((3, 16, 128), F32),
            pltpu.VMEM((3, 128, 128), F32),
            pltpu.VMEM((128, 128), F32),
            pltpu.VMEM((4, 128, 128), F32),
            pltpu.VMEM((3, 16, 128), F32),
            dma((7, 8)),
            dma((7, 8)),
        ],
        compiler_params=pltpu.CompilerParams(
            collective_id=0, has_side_effects=True, vmem_limit_bytes=40 * 2**20
        ),
    )(*(pltpu.with_memory_space_constraint(operand, pltpu.HBM) for operand in operands))
    level, hidden, grad_one, grad_two = pl.pallas_call(
        finish_kernel,
        out_shape=shapes,
        in_specs=[vmem] * 4,
        out_specs=[hbm] * 4,
        scratch_shapes=[dma((4,))],
        compiler_params=pltpu.CompilerParams(vmem_limit_bytes=40 * 2**20),
    )(*results)
    return (
        level.reshape(1, 1, 32, CELLS),
        hidden.reshape(1, 1, 16, 8, CELLS),
        jnp.transpose(grad_one, (2, 0, 1)),
        jnp.transpose(grad_two.reshape(27, 16, 32), (0, 2, 1)),
    )


def solution(mesh):
    placed = (P("dp", "space", None, None, None), P(), P(), P("dp", "space", None, None))
    return jax.shard_map(
        body,
        mesh=mesh,
        in_specs=placed,
        out_specs=(P("dp", "space", None, None), P("dp", "space", None, None, None), P(), P()),
        check_vma=False,
    )
```
